512 devices in a mesh: pipe: 64 (over y, z_hi, x), expert: 8 (over z_lo, core).
Axes of the slice: x: 4, y: 4, z: 16 (z_hi: 4, z_lo: 4; z = z_hi * 4 + z_lo), core: 2. Of those that a mesh axis runs over, the one named last changes fastest.
Arguments:
- stash_a: bfloat16 [64, 2, 64, 3584], P('pipe', None, 'expert'), may hold values from -6 to 6
- stash_b: bfloat16 [64, 2, 64, 3584], P('pipe', None, 'expert'), may hold values from -6 to 6
- ids_a: int32 [64, 2, 64, 8], P('pipe', None, 'expert'), may hold values from 0 to 255, all different within a row
- ids_b: int32 [64, 2, 64, 8], P('pipe', None, 'expert'), may hold values from 0 to 255, all different within a row
- arriving_a: bfloat16 [64, 64, 3584], P('pipe', 'expert'), may hold values from -6 to 6
- arriving_b: bfloat16 [64, 64, 3584], P('pipe', 'expert'), may hold values from -6 to 6
- head_a: bfloat16 [1, 64, 3584], P(None, 'expert'), may hold values from -6 to 6
- head_b: bfloat16 [1, 64, 3584], P(None, 'expert'), may hold values from -6 to 6
- w_gate: bfloat16 [64, 3584, 1024], P('pipe', None, 'expert'), may hold values from -0.09375 to 0.09375
- w_up: bfloat16 [64, 3584, 1024], P('pipe', None, 'expert'), may hold values from -0.09375 to 0.09375
- w_down: bfloat16 [64, 1024, 3584], P('pipe', 'expert'), may hold values from -0.09375 to 0.09375
- router: bfloat16 [64, 256, 3584], P('pipe', 'expert'), may hold values from -2 to 2
Outputs:
- leaving_a: bfloat16 [64, 64, 3584], P('pipe', 'expert')
- leaving_b: bfloat16 [64, 64, 3584], P('pipe', 'expert')
- router_grad: float32 [64, 256, 3584], P('pipe', 'expert')
The draws below stay inside these ranges and needn't reach their ends.
Inputs may be any that keep to these rules, and one draw needn't show every extreme that they name: `ids_a`: each row names 8 different experts. `ids_b`: each row names 8 different experts.
All inputs are finite; a program needn't handle non-finite values.
Results may differ from the reference program's by a relative error of at most 0.019.
Values may be sent and summed in bfloat16 or wider, within the bound.
No kernel may reach another device: no remote copies, remote signals or barrier semaphores. Data moves between devices by JAX's collectives and lax.ppermute only.
A program may use at most 64 MiB of HBM per device.

```python
import math
import jax
import jax.numpy as jnp
from jax import lax

D = 3584
HID = 1024
EXPERTS = 256
TOPK = 8
TICKS = 2
TOK = 64
N_PIPE = 64
N_EXPERT = 8


def draw_stash_a(key, part):
    key = jax.random.fold_in(key, 21)
    values = jax.random.normal(key, (N_PIPE, TICKS, TOK, D), jnp.float32)
    return jnp.clip(values, -6.0, 6.0).astype(jnp.bfloat16)


def draw_stash_b(key, part):
    key = jax.random.fold_in(key, 22)
    values = jax.random.normal(key, (N_PIPE, TICKS, TOK, D), jnp.float32)
    return jnp.clip(values, -6.0, 6.0).astype(jnp.bfloat16)


def draw_router(key, part):
    key = jax.random.fold_in(key, 11)
    values = jax.random.normal(key, (N_PIPE, EXPERTS, D), jnp.float32) * (3.0 / math.sqrt(D))
    return values.astype(jnp.bfloat16)


def level_of(stream_key, extent, split, least, top_value):
    loudness = 1.0
    for axis_at, blocks in split:
        steps = jax.random.uniform(jax.random.fold_in(jax.random.fold_in(stream_key, 6), axis_at), (blocks,), jnp.float32, least / len(split), top_value / len(split))
        loudness = loudness * jnp.repeat(jnp.exp(steps), extent[axis_at] // blocks).reshape((-1,) + (1,) * (len(extent) - 1 - axis_at))
    return loudness


def picks_of(own_key, rows, amount, top, lift):
    order = jax.random.permutation(jax.random.fold_in(own_key, 1), amount)
    pull = order
    for power in range(3):
        pull = pull * pull // amount
    pull = pull * lift // amount
    tickets = jax.random.randint(jax.random.fold_in(own_key, 2), (rows, amount), 0, 4096) + pull
    holders = jax.random.permutation(jax.random.fold_in(own_key, 3), rows)[jnp.arange(amount) % rows]
    tickets = jnp.where(jnp.arange(rows)[:, None] == holders[None, :], 1 << 14, tickets)
    merit = tickets * amount + jnp.arange(amount)
    return lax.top_k(merit.astype(jnp.int32), top)[1].astype(jnp.int32)


def normal_values(key, shape, width, bound, shards=(), held_as=jnp.bfloat16):
    factor_of = level_of(key, shape, shards, -0.22, 0.18) if shards else 1.0
    drawn = jax.random.normal(key, shape, jnp.float32) * width * factor_of
    return jnp.minimum(jnp.maximum(drawn, -bound), bound).astype(held_as)


def setup_inputs(seed: int = 0) -> dict:
    key_of = jax.random.split(jax.random.key(seed), 13)
    stash_a = draw_stash_a(jax.random.fold_in(key_of[12], 71), 0)
    stash_b = draw_stash_b(jax.random.fold_in(key_of[12], 71), 0)
    ids_a = picks_of(key_of[2], N_PIPE * TICKS * TOK, EXPERTS, TOPK, 512).reshape((N_PIPE, TICKS, TOK, TOPK))
    ids_b = picks_of(key_of[3], N_PIPE * TICKS * TOK, EXPERTS, TOPK, 512).reshape((N_PIPE, TICKS, TOK, TOPK))
    arriving_a = normal_values(key_of[4], (N_PIPE, TOK, D), 1.0, 6.0, ((0, 64), (1, 8)))
    arriving_b = normal_values(key_of[5], (N_PIPE, TOK, D), 1.0, 6.0, ((0, 64), (1, 8)))
    head_a = normal_values(key_of[6], (TICKS - 1, TOK, D), 1.0, 6.0, ((1, 8),))
    head_b = normal_values(key_of[7], (TICKS - 1, TOK, D), 1.0, 6.0, ((1, 8),))
    w_gate = normal_values(key_of[8], (N_PIPE, D, HID), D ** -0.5, 0.09375, ((0, 64), (2, 8)))
    w_up = normal_values(key_of[9], (N_PIPE, D, HID), D ** -0.5, 0.09375, ((0, 64), (2, 8)))
    w_down = normal_values(key_of[10], (N_PIPE, HID, D), D ** -0.5, 0.09375, ((0, 64), (1, 8)))
    router = draw_router(jax.random.fold_in(key_of[12], 71), 0)
    return dict(stash_a=stash_a, stash_b=stash_b, ids_a=ids_a, ids_b=ids_b, arriving_a=arriving_a, arriving_b=arriving_b, head_a=head_a, head_b=head_b, w_gate=w_gate, w_up=w_up, w_down=w_down, router=router)


z_weight = 0.01
balance_weight = 1.0


def expert_backward(inputs, grads, w_gate, w_up, w_down):
    gate_pre = jnp.dot(inputs, w_gate, preferred_element_type=jnp.float32)
    up_pre = jnp.dot(inputs, w_up, preferred_element_type=jnp.float32)
    hidden_grad = jnp.dot(grads, w_down.T, preferred_element_type=jnp.float32)
    gate_sig = jax.nn.sigmoid(gate_pre)
    d_gate = (hidden_grad * up_pre * gate_sig * (1.0 + gate_pre * (1.0 - gate_sig))).astype(jnp.bfloat16)
    d_up = (hidden_grad * gate_pre * gate_sig).astype(jnp.bfloat16)
    span_cols = HID // N_EXPERT
    running = grads.astype(jnp.float32)
    for group_index in range(N_EXPERT):
        low_col = group_index * span_cols
        term_part = jnp.dot(d_gate[:, low_col:low_col + span_cols], w_gate[:, low_col:low_col + span_cols].T, preferred_element_type=jnp.float32)
        term_part = term_part + jnp.dot(d_up[:, low_col:low_col + span_cols], w_up[:, low_col:low_col + span_cols].T, preferred_element_type=jnp.float32)
        rounded = lax.optimization_barrier(term_part.astype(jnp.bfloat16))
        running = running + rounded.astype(jnp.float32)
    return running.astype(jnp.bfloat16)


def router_backward(inputs, chosen, weights):
    logits = jnp.dot(inputs, weights.T, preferred_element_type=jnp.float32)
    peak_val = jnp.max(logits, axis=-1, keepdims=True)
    expo_terms = jnp.exp(logits - peak_val)
    denom_sum = jnp.sum(expo_terms, axis=-1, keepdims=True)
    log_total = peak_val[:, 0] + jnp.log(denom_sum[:, 0])
    probs = expo_terms / denom_sum
    matches = (chosen.reshape(-1, 1) == jnp.arange(EXPERTS, dtype=jnp.int32)[None, :]).astype(jnp.float32)
    share_vec = jnp.sum(matches, axis=0) * (EXPERTS / (TOK * TOPK))
    mean_share = jnp.sum(probs * share_vec[None, :], axis=-1)
    slopes = (((2.0 * z_weight) * log_total - balance_weight * mean_share)[:, None] + balance_weight * share_vec[None, :]) * probs
    return jnp.dot(slopes.astype(jnp.bfloat16).T, inputs, preferred_element_type=jnp.float32)


def run_stream(stash, arriving, head, w_gate, w_up, w_down):
    incoming = arriving
    emitted = arriving
    for moment in range(TICKS):
        def section_step(section_idx):
            return expert_backward(stash[section_idx, moment], incoming[section_idx], w_gate[section_idx], w_up[section_idx], w_down[section_idx])
        emitted = lax.map(section_step, jnp.arange(N_PIPE, dtype=jnp.int32))
        if moment + 1 < TICKS:
            incoming = jnp.concatenate([emitted[1:], head[moment][None]], axis=0)
    return emitted


def reference(stash_a, stash_b, ids_a, ids_b, arriving_a, arriving_b, head_a, head_b, w_gate, w_up, w_down, router):
    stash_rev = stash_b[::-1]
    ids_rev = ids_b[::-1]
    arriving_rev = arriving_b[::-1]
    leaving_a = run_stream(stash_a, arriving_a, head_a, w_gate, w_up, w_down)
    leaving_b = run_stream(stash_rev, arriving_rev, head_b, w_gate, w_up, w_down)[::-1]

    def section_router(section_idx):
        summed = jnp.zeros((EXPERTS, D), jnp.float32)
        for moment in range(TICKS):
            summed = summed + router_backward(stash_a[section_idx, moment], ids_a[section_idx, moment], router[section_idx])
            summed = summed + router_backward(stash_rev[section_idx, moment], ids_rev[section_idx, moment], router[section_idx])
        return summed

    router_grad = lax.map(section_router, jnp.arange(N_PIPE, dtype=jnp.int32))
    return leaving_a, leaving_b, router_grad
```

```python
import functools

import jax
import jax.numpy as jnp
from jax import lax
from jax.experimental import pallas as pl
from jax.experimental.pallas import tpu as pltpu
from jax.sharding import PartitionSpec as P

D = 3584
HID = 128
EXPERTS = 256
OWN = 32
TOKENS = 64
TOPK = 8
ROWS = 8
CHIPS = 4
IDCOLS = 128
z_weight = 0.01
balance_weight = 1.0
F32 = jnp.float32
BF16 = jnp.bfloat16
VMEM_LIMIT = 48 * 1024 * 1024


def dot(lhs, rhs, lhs_dim, rhs_dim):
    return lax.dot_general(
        lhs, rhs, (((lhs_dim,), (rhs_dim,)), ((), ())), preferred_element_type=F32
    )


def call(body, out_shape, scratch, args, flops):
    spec = pl.BlockSpec(memory_space=pltpu.VMEM)
    total = sum(a.size * a.dtype.itemsize for a in args)
    return pl.pallas_call(
        body,
        out_shape=out_shape,
        in_specs=[spec] * len(args),
        out_specs=[spec] * len(out_shape),
        scratch_shapes=scratch,
        compiler_params=pltpu.CompilerParams(vmem_limit_bytes=VMEM_LIMIT),
        cost_estimate=pl.CostEstimate(flops=flops, bytes_accessed=total, transcendentals=0),
    )(*args)


def backward_terms(hidden, gate, up, gates, ups, outs):
    d_gate, d_up = [], []
    for h, g, u in zip(hidden, gate, up):
        q = jax.nn.sigmoid(g)
        d_gate.append((h * u * q * (1.0 + g * (1.0 - q))).astype(BF16))
        d_up.append((h * g * q).astype(BF16))
    width = 512
    for low in range(0, D, width):
        cols = pl.ds(low, width)
        total = dot(d_gate[0], gates[0][cols, :], 1, 1)
        total += dot(d_gate[1], gates[1][cols, :], 1, 1)
        total += dot(d_up[0], ups[0][cols, :], 1, 1)
        total += dot(d_up[1], ups[1][cols, :], 1, 1)
        for k in range(CHIPS):
            part = total[16 * k : 16 * k + 16]
            outs[k][:, cols] = part.astype(outs[k].dtype)


def pick(value, offset):
    return jnp.concatenate(
        [value[16 * b + offset : 16 * b + offset + 8] for b in range(2 * CHIPS)], axis=0
    )


def first_tick_kernel(*refs):
    blocks, weights, outs, held = refs[:8], refs[8:14], refs[14:18], refs[18]
    gates, ups, downs = weights[0:2], weights[2:4], weights[4:6]
    for b in range(8):
        held[pl.ds(16 * b, 16), :] = blocks[b][...]
    rows = held[...]
    gate = [pick(dot(rows, w[...], 1, 0), 0) for w in gates]
    up = [pick(dot(rows, w[...], 1, 0), 0) for w in ups]
    hidden = [pick(dot(rows, w[...], 1, 1), 8) for w in downs]
    backward_terms(hidden, gate, up, gates, ups, outs)


def second_tick_kernel(*refs):
    blocks, pre, weights, outs, held = refs[:4], refs[4:8], refs[8:14], refs[14:18], refs[18]
    gates, ups, downs = weights[0:2], weights[2:4], weights[4:6]
    for b in range(4):
        held[pl.ds(16 * b, 16), :] = blocks[b][...]
    rows = held[...]
    hidden = [dot(rows, w[...], 1, 1) for w in downs]
    gate = [pre[0][...], pre[1][...]]
    up = [pre[2][...], pre[3][...]]
    backward_terms(hidden, gate, up, gates, ups, outs)


def forward_kernel(*refs):
    first, second = refs[0:8], refs[8:12]
    gates, ups, routers = refs[12:14], refs[14:16], refs[16:18]
    base, pre = refs[18], refs[19:23]
    expo_ref, share_ref, stats_ref = refs[23:26]
    held0, held1, ids_ref = refs[26:29]
    for b in range(8):
        held0[pl.ds(16 * b, 16), :] = first[b][...]
    ids_ref[...] = jnp.full((128, IDCOLS), -1.0, F32)
    for b in range(4):
        held1[pl.ds(16 * b, 16), :] = second[b][:, 0:D]
        ids_ref[pl.ds(16 * b, 16), :] = second[b][:, D : D + IDCOLS].astype(F32)
    rows0, rows1 = held0[...], held1[...]
    for w, out in zip((*gates, *ups), pre):
        out[...] = dot(rows1, w[...], 1, 0)
    logits = jnp.concatenate(
        [
            jnp.concatenate([dot(r[...], rows, 1, 1) for r in routers], axis=0)
            for rows in (rows0, jnp.concatenate([rows1, rows1], axis=0))
        ],
        axis=1,
    )
    ids = ids_ref[...].T
    experts = base[:, 0:1]
    stream_b = (lax.broadcasted_iota(jnp.int32, (2 * OWN, 128), 1) % 16) >= 8
    scale = EXPERTS / (TOKENS * TOPK)
    shares = []
    for tick in range(2):
        hits = jnp.zeros((2 * OWN, 128), F32)
        for core in range(2):
            for j in range(TOPK):
                slot = 16 * core + 8 * tick + j
                hits += (experts == ids[slot : slot + 1, :]).astype(F32)
        count_a = jnp.sum(jnp.where(stream_b, 0.0, hits), axis=1, keepdims=True)
        count_b = jnp.sum(jnp.where(stream_b, hits, 0.0), axis=1, keepdims=True)
        shares.append((count_a * scale, count_b * scale))
    column = lax.broadcasted_iota(jnp.int32, (2 * OWN, 128), 1)
    share0 = jnp.where((column % 32) >= 16, shares[0][1], shares[0][0])
    share1 = jnp.where(stream_b, shares[1][1], shares[1][0])
    share = jnp.concatenate([share0, share1], axis=1)
    peak = jnp.max(logits, axis=0, keepdims=True)
    expo = jnp.exp(logits - peak)
    total = jnp.sum(expo, axis=0, keepdims=True)
    weighted = jnp.sum(expo * share, axis=0, keepdims=True)
    expo_ref[...] = expo
    share_ref[...] = share
    stats_ref[...] = jnp.concatenate(
        [peak, total, weighted, jnp.zeros((5, 256), F32)], axis=0
    )


def router_kernel(*refs):
    first, second = refs[0:8], refs[8:12]
    expo_ref, share_ref = refs[12:14]
    stats = refs[14:18]
    own_out, other_out = refs[18:20]
    held0, held1 = refs[20:22]
    for b in range(8):
        held0[pl.ds(16 * b, 16), :] = first[b][...]
    for b in range(4):
        held1[pl.ds(16 * b, 16), :] = second[b][:, 0:D]
    stats = [
        jnp.concatenate(
            [pltpu.roll(s[:, 0:128], 32 * k, 1), pltpu.roll(s[:, 128:256], 16 * k, 1)], axis=1
        )
        if k
        else s[...]
        for k, s in enumerate(stats)
    ]
    peaks = [s[0:1, :] for s in stats]
    peak = functools.reduce(jnp.maximum, peaks)
    factors = [jnp.exp(p - peak) for p in peaks]
    total = sum(s[1:2, :] * f for s, f in zip(stats, factors))
    weighted = sum(s[2:3, :] * f for s, f in zip(stats, factors))
    log_total = peak + jnp.log(total)
    mean_share = weighted / total
    probs = expo_ref[...] * (factors[0] / total)
    slopes = (
        2.0 * z_weight * log_total - balance_weight * mean_share + balance_weight * share_ref[...]
    ) * probs
    column = lax.broadcasted_iota(jnp.int32, (2 * OWN, 128), 1)
    slopes0 = jnp.where((column % 16) < 8, slopes[:, 0:128], 0.0).astype(BF16)
    slopes1 = slopes[:, 128:192].astype(BF16)
    width = 512
    for low in range(0, D, width):
        cols = pl.ds(low, width)
        part = dot(slopes0, held0[:, cols], 1, 0) + dot(slopes1, held1[:, cols], 1, 0)
        own_out[:, cols] = part[0:OWN]
        other_out[:, cols] = part[OWN:]


def swapped(value):
    return lax.ppermute(value, "expert", [(e, e ^ 1) for e in range(8)])


def mirrored(value):
    count = lax.axis_size("pipe")
    return lax.ppermute(value, "pipe", [(i, count - 1 - i) for i in range(count)])


def from_chip(value, k):
    return lax.ppermute(value, "expert", [((e + 2 * k) % 8, e) for e in range(8)])


def spread(value):
    return [value] + [from_chip(value, k) for k in range(1, CHIPS)]


def returned(parts):
    return [parts[0]] + [from_chip(parts[k], CHIPS - k) for k in range(1, CHIPS)]


def shards(
    stash_a, stash_b, ids_a, ids_b, arriving_a, arriving_b, head_a, head_b,
    w_gate, w_up, w_down, router,
):
    stash_a, stash_b, ids_a, ids_b = stash_a[0], stash_b[0], ids_a[0], ids_b[0]
    arriving_a, arriving_b = arriving_a[0], arriving_b[0]
    w_gate, w_up, w_down, router = w_gate[0], w_up[0], w_down[0], router[0]
    section = lax.axis_index("pipe")
    top = lax.axis_size("pipe") - 1
    member = lax.axis_index("expert")

    block_b = mirrored(jnp.concatenate([stash_b[0], arriving_b], axis=0))
    block_a = jnp.concatenate([stash_a[0], arriving_a], axis=0)
    blocks_a = spread(block_a)
    other_gate, other_up, other_down, other_router = (
        swapped(w_gate), swapped(w_up), swapped(w_down), swapped(router)
    )
    gates, ups = [w_gate, other_gate], [w_up, other_up]
    downs, routers = [w_down, other_down], [router, other_router]

    def id_rows(ids):
        return jnp.concatenate([ids[0], ids[1]], axis=1)

    ids = jnp.concatenate([id_rows(ids_a), id_rows(ids_b)], axis=0).astype(BF16)
    ids = jnp.pad(ids, ((0, 0), (0, 112)), constant_values=-1)
    ids_other = swapped(ids)
    ids = jnp.concatenate([ids[:, :16], ids_other[:, :16], ids[:, 32:]], axis=1)
    later_b = mirrored(jnp.concatenate([stash_b[1], ids[8:]], axis=1))
    later_a = jnp.concatenate([stash_a[1], ids[:8]], axis=1)
    blocks_b = spread(block_b)
    later = spread(jnp.concatenate([later_a, later_b], axis=0))
    first = [block for pair in zip(blocks_a, blocks_b) for block in pair]

    sums = [
        jax.ShapeDtypeStruct((16, D), F32 if k == 0 else BF16) for k in range(CHIPS)
    ]
    terms = call(
        first_tick_kernel, sums, [pltpu.VMEM((128, D), BF16)],
        first + gates + ups + downs, 2 * 128 * D * 128 * 10,
    )
    base = jnp.concatenate(
        [OWN * member + jnp.arange(OWN), OWN * (member ^ 1) + jnp.arange(OWN)]
    ).astype(F32)
    base = jnp.broadcast_to(base[:, None], (2 * OWN, 128))
    pre = [jax.ShapeDtypeStruct((64, HID), F32)] * 4
    *pre, expo, share, stats = call(
        forward_kernel,
        pre
        + [
            jax.ShapeDtypeStruct((2 * OWN, 256), F32),
            jax.ShapeDtypeStruct((2 * OWN, 256), F32),
            jax.ShapeDtypeStruct((8, 256), F32),
        ],
        [pltpu.VMEM((128, D), BF16), pltpu.VMEM((64, D), BF16), pltpu.VMEM((128, IDCOLS), F32)],
        first + later + gates + ups + routers + [base], 2 * 128 * D * 128 * 4,
    )

    def emitted(grads, parts):
        total = grads.astype(F32) + parts[0]
        for part in parts[1:]:
            total = total + part.astype(F32)
        return total.astype(BF16)

    grads = jnp.concatenate([block_a[8:], block_b[8:]], axis=0)
    out = emitted(grads, returned(terms))
    moved = lax.ppermute(out, "pipe", [(i, i - 1) for i in range(1, top + 1)])
    head = jnp.concatenate([head_a[0], head_b[0]], axis=0)
    grads = jnp.where(section == top, head, moved)
    terms = call(
        second_tick_kernel, sums, [pltpu.VMEM((64, D), BF16)],
        spread(grads) + pre + gates + ups + downs, 2 * 64 * D * 128 * 6,
    )
    own, other = call(
        router_kernel, [jax.ShapeDtypeStruct((OWN, D), F32)] * 2,
        [pltpu.VMEM((128, D), BF16), pltpu.VMEM((64, D), BF16)],
        first + later + [expo, share] + spread(stats), 2 * 192 * D * 64,
    )
    router_grad = own + swapped(other)
    out = emitted(grads, returned(terms))
    return out[None, :8], mirrored(out[8:])[None], router_grad[None]


def solution(mesh):
    placed = (
        P("pipe", None, "expert", None),
        P("pipe", None, "expert", None),
        P("pipe", None, "expert", None),
        P("pipe", None, "expert", None),
        P("pipe", "expert", None),
        P("pipe", "expert", None),
        P(None, "expert", None),
        P(None, "expert", None),
        P("pipe", None, "expert"),
        P("pipe", None, "expert"),
        P("pipe", "expert", None),
        P("pipe", "expert", None),
    )
    return jax.shard_map(
        shards,
        mesh=mesh,
        in_specs=placed,
        out_specs=(P("pipe", "expert", None), P("pipe", "expert", None), P("pipe", "expert", None)),
        check_vma=False,
    )
```

```python
import functools

import jax
import jax.numpy as jnp
from jax import lax
from jax.experimental import pallas as pl
from jax.experimental.pallas import tpu as pltpu
from jax.sharding import PartitionSpec as P

D = 3584
HID = 128
EXPERTS = 256
OWN = 32
TOKENS = 64
TOPK = 8
ROWS = 8
CHIPS = 4
IDCOLS = 128
z_weight = 0.01
balance_weight = 1.0
F32 = jnp.float32
BF16 = jnp.bfloat16
VMEM_LIMIT = 48 * 1024 * 1024


def dot(lhs, rhs, lhs_dim, rhs_dim):
    return lax.dot_general(
        lhs, rhs, (((lhs_dim,), (rhs_dim,)), ((), ())), preferred_element_type=F32
    )


def call(body, out_shape, scratch, args, flops):
    spec = pl.BlockSpec(memory_space=pltpu.VMEM)
    total = sum(a.size * a.dtype.itemsize for a in args)
    return pl.pallas_call(
        body,
        out_shape=out_shape,
        in_specs=[spec] * len(args),
        out_specs=[spec] * len(out_shape),
        scratch_shapes=scratch,
        compiler_params=pltpu.CompilerParams(vmem_limit_bytes=VMEM_LIMIT),
        cost_estimate=pl.CostEstimate(flops=flops, bytes_accessed=total, transcendentals=0),
    )(*args)


def backward_terms(hidden, gate, up, gates, ups, out):
    d_gate, d_up = [], []
    for h, g, u in zip(hidden, gate, up):
        q = jax.nn.sigmoid(g)
        d_gate.append((h * u * q * (1.0 + g * (1.0 - q))).astype(BF16))
        d_up.append((h * g * q).astype(BF16))
    width = 512
    for low in range(0, D, width):
        cols = pl.ds(low, width)
        total = dot(d_gate[0], gates[0][cols, :], 1, 1)
        total += dot(d_gate[1], gates[1][cols, :], 1, 1)
        total += dot(d_up[0], ups[0][cols, :], 1, 1)
        total += dot(d_up[1], ups[1][cols, :], 1, 1)
        out[:, cols] = total.astype(BF16)


def first_tick_kernel(*refs):
    streams, weights, out, held = refs[:2], refs[2:8], refs[8], refs[9]
    gates, ups, downs = weights[0:2], weights[2:4], weights[4:6]
    for s in range(2):
        held[pl.ds(64 * s, 64), :] = streams[s][...]
    rows = held[...]

    def pick(value, offset):
        return jnp.concatenate(
            [
                value[64 * s + 16 * k + offset : 64 * s + 16 * k + offset + 8]
                for k in range(CHIPS)
                for s in range(2)
            ],
            axis=0,
        )

    gate = [pick(dot(rows, w[...], 1, 0), 0) for w in gates]
    up = [pick(dot(rows, w[...], 1, 0), 0) for w in ups]
    hidden = [pick(dot(rows, w[...], 1, 1), 8) for w in downs]
    backward_terms(hidden, gate, up, gates, ups, out)


def second_tick_kernel(*refs):
    grads, pre, weights, out = refs[0], refs[1:5], refs[5:11], refs[11]
    gates, ups, downs = weights[0:2], weights[2:4], weights[4:6]
    rows = grads[...]
    hidden = [dot(rows, w[...], 1, 1) for w in downs]
    gate = [pre[0][...], pre[1][...]]
    up = [pre[2][...], pre[3][...]]
    backward_terms(hidden, gate, up, gates, ups, out)


def forward_kernel(*refs):
    first_a, first_b, second = refs[0:3]
    gates, ups, routers = refs[3:5], refs[5:7], refs[7:9]
    base, pre = refs[9], refs[10:14]
    expo_ref, share_ref, stats_ref = refs[14:17]
    held0, ids_ref = refs[17:19]
    held0[0:64, :] = first_a[...]
    held0[64:128, :] = first_b[...]
    ids_ref[0:64, :] = second[:, D : D + IDCOLS].astype(F32)
    ids_ref[64:128, :] = jnp.full((64, IDCOLS), -1.0, F32)
    rows0, rows1 = held0[...], second[:, 0:D]
    for w, out in zip((*gates, *ups), pre):
        out[...] = dot(rows1, w[...], 1, 0)
    logits = jnp.concatenate(
        [
            jnp.concatenate([dot(r[...], rows, 1, 1) for r in routers], axis=0)
            for rows in (rows0, jnp.concatenate([rows1, rows1], axis=0))
        ],
        axis=1,
    )
    ids = ids_ref[...].T
    experts = base[:, 0:1]
    stream_b = (lax.broadcasted_iota(jnp.int32, (2 * OWN, 128), 1) % 16) >= 8
    scale = EXPERTS / (TOKENS * TOPK)
    shares = []
    for tick in range(2):
        hits = jnp.zeros((2 * OWN, 128), F32)
        for core in range(2):
            for j in range(TOPK):
                slot = 16 * core + 8 * tick + j
                hits += (experts == ids[slot : slot + 1, :]).astype(F32)
        count_a = jnp.sum(jnp.where(stream_b, 0.0, hits), axis=1, keepdims=True)
        count_b = jnp.sum(jnp.where(stream_b, hits, 0.0), axis=1, keepdims=True)
        shares.append((count_a * scale, count_b * scale))
    column = lax.broadcasted_iota(jnp.int32, (2 * OWN, 128), 1)
    share0 = jnp.where(column >= 64, shares[0][1], shares[0][0])
    share1 = jnp.where(stream_b, shares[1][1], shares[1][0])
    share = jnp.concatenate([share0, share1], axis=1)
    peak = jnp.max(logits, axis=0, keepdims=True)
    expo = jnp.exp(logits - peak)
    total = jnp.sum(expo, axis=0, keepdims=True)
    weighted = jnp.sum(expo * share, axis=0, keepdims=True)
    expo_ref[...] = expo
    share_ref[...] = share
    stats_ref[...] = jnp.concatenate(
        [peak, total, weighted, jnp.zeros((5, 256), F32)], axis=0
    )


def router_kernel(*refs):
    first_a, first_b, second, expo_ref, share_ref, all_stats, chip, own_out, other_out = refs
    mine = chip[...]
    stats = [all_stats[pl.ds(8 * k, 8), :] for k in range(CHIPS)]
    peaks = [s[0:1, :] for s in stats]
    peak = functools.reduce(jnp.maximum, peaks)
    factors = [jnp.exp(p - peak) for p in peaks]
    total = sum(s[1:2, :] * f for s, f in zip(stats, factors))
    weighted = sum(s[2:3, :] * f for s, f in zip(stats, factors))
    log_total = peak + jnp.log(total)
    mean_share = weighted / total
    own_factor = sum(jnp.where(mine == k, f, 0.0) for k, f in enumerate(factors))
    probs = expo_ref[...] * (own_factor / total)
    slopes = (
        2.0 * z_weight * log_total - balance_weight * mean_share + balance_weight * share_ref[...]
    ) * probs
    column = lax.broadcasted_iota(jnp.int32, (2 * OWN, 128), 1)
    slopes0 = jnp.where((column % 16) < 8, slopes[:, 0:128], 0.0).astype(BF16)
    slopes1 = slopes[:, 128:192].astype(BF16)
    width = 512
    for low in range(0, D, width):
        cols = pl.ds(low, width)
        part = dot(slopes0[:, 0:64], first_a[:, cols], 1, 0)
        part += dot(slopes0[:, 64:128], first_b[:, cols], 1, 0)
        part += dot(slopes1, second[:, cols], 1, 0)
        own_out[:, cols] = part[0:OWN]
        other_out[:, cols] = part[OWN:]


def swapped(value):
    return lax.ppermute(value, "expert", [(e, e ^ 1) for e in range(8)])


def mirrored(value):
    count = lax.axis_size("pipe")
    return lax.ppermute(value, "pipe", [(i, count - 1 - i) for i in range(count)])


def exchanged(blocks):
    return lax.all_to_all(
        blocks, "expert", split_axis=0, concat_axis=0, tiled=True,
        axis_index_groups=[[0, 2, 4, 6], [1, 3, 5, 7]],
    )


def spread(value):
    return exchanged(jnp.concatenate([value] * CHIPS, axis=0))


def shards(
    stash_a, stash_b, ids_a, ids_b, arriving_a, arriving_b, head_a, head_b,
    w_gate, w_up, w_down, router,
):
    stash_a, stash_b, ids_a, ids_b = stash_a[0], stash_b[0], ids_a[0], ids_b[0]
    arriving_a, arriving_b = arriving_a[0], arriving_b[0]
    w_gate, w_up, w_down, router = w_gate[0], w_up[0], w_down[0], router[0]
    section = lax.axis_index("pipe")
    top = lax.axis_size("pipe") - 1
    member = lax.axis_index("expert")

    block_b = mirrored(jnp.concatenate([stash_b[0], arriving_b], axis=0))
    block_a = jnp.concatenate([stash_a[0], arriving_a], axis=0)
    first_a = spread(block_a)
    other_gate, other_up, other_down, other_router = (
        swapped(w_gate), swapped(w_up), swapped(w_down), swapped(router)
    )
    gates, ups = [w_gate, other_gate], [w_up, other_up]
    downs, routers = [w_down, other_down], [router, other_router]

    def id_rows(ids):
        return jnp.concatenate([ids[0], ids[1]], axis=1)

    ids = jnp.concatenate([id_rows(ids_a), id_rows(ids_b)], axis=0).astype(BF16)
    ids = jnp.pad(ids, ((0, 0), (0, 112)), constant_values=-1)
    ids_other = swapped(ids)
    ids = jnp.concatenate([ids[:, :16], ids_other[:, :16], ids[:, 32:]], axis=1)
    later_b = mirrored(jnp.concatenate([stash_b[1], ids[8:]], axis=1))
    later_a = jnp.concatenate([stash_a[1], ids[:8]], axis=1)
    first_b = spread(block_b)
    later = jnp.concatenate([later_a, later_b], axis=0)
    sums = [jax.ShapeDtypeStruct((64, D), BF16)]
    (terms,) = call(
        first_tick_kernel, sums, [pltpu.VMEM((128, D), BF16)],
        [first_a, first_b] + gates + ups + downs, 2 * 128 * D * 128 * 10,
    )
    base = jnp.concatenate(
        [OWN * member + jnp.arange(OWN), OWN * (member ^ 1) + jnp.arange(OWN)]
    ).astype(F32)
    base = jnp.broadcast_to(base[:, None], (2 * OWN, 128))

    def emitted(grads, parts):
        total = grads.astype(F32)
        for k in range(CHIPS):
            total = total + parts[16 * k : 16 * k + 16].astype(F32)
        return total.astype(BF16)

    grads = jnp.concatenate([block_a[8:], block_b[8:]], axis=0)
    out = emitted(grads, exchanged(terms))
    out, later = lax.optimization_barrier((out, later))
    moved = lax.ppermute(out, "pipe", [(i, i - 1) for i in range(1, top + 1)])
    second = spread(later)
    head = jnp.concatenate([head_a[0], head_b[0]], axis=0)
    grads = jnp.where(section == top, head, moved)
    all_grads = spread(grads)
    pre = [jax.ShapeDtypeStruct((64, HID), F32)] * 4
    *pre, expo, share, stats = call(
        forward_kernel,
        pre
        + [
            jax.ShapeDtypeStruct((2 * OWN, 256), F32),
            jax.ShapeDtypeStruct((2 * OWN, 256), F32),
            jax.ShapeDtypeStruct((8, 256), F32),
        ],
        [pltpu.VMEM((128, D), BF16), pltpu.VMEM((128, IDCOLS), F32)],
        [first_a, first_b, second] + gates + ups + routers + [base], 2 * 128 * D * 128 * 4,
    )
    (terms,) = call(
        second_tick_kernel, sums, [],
        [all_grads] + pre + gates + ups + downs, 2 * 64 * D * 128 * 6,
    )
    terms, stats = lax.optimization_barrier((terms, stats))
    parts = exchanged(terms)
    chip = jnp.full((1, 256), member // 2, jnp.int32)
    own, other = call(
        router_kernel, [jax.ShapeDtypeStruct((OWN, D), F32)] * 2, [],
        [first_a, first_b, second, expo, share, spread(stats), chip], 2 * 192 * D * 64,
    )
    router_grad = own + swapped(other)
    out = emitted(grads, parts)
    return out[None, :8], mirrored(out[8:])[None], router_grad[None]


def solution(mesh):
    placed = (
        P("pipe", None, "expert", None),
        P("pipe", None, "expert", None),
        P("pipe", None, "expert", None),
        P("pipe", None, "expert", None),
        P("pipe", "expert", None),
        P("pipe", "expert", None),
        P(None, "expert", None),
        P(None, "expert", None),
        P("pipe", None, "expert"),
        P("pipe", None, "expert"),
        P("pipe", "expert", None),
        P("pipe", "expert", None),
    )
    return jax.shard_map(
        shards,
        mesh=mesh,
        in_specs=placed,
        out_specs=(P("pipe", "expert", None), P("pipe", "expert", None), P("pipe", "expert", None)),
        check_vma=False,
    )
```

```python
import functools

import jax
import jax.numpy as jnp
from jax import lax
from jax.experimental import pallas as pl
from jax.experimental.pallas import tpu as pltpu
from jax.sharding import PartitionSpec as P

D = 3584
HID = 128
EXPERTS = 256
OWN = 32
TOKENS = 64
TOPK = 8
ROWS = 8
CHIPS = 4
IDCOLS = 128
z_weight = 0.01
balance_weight = 1.0
F32 = jnp.float32
BF16 = jnp.bfloat16
VMEM_LIMIT = 16 * 1024 * 1024


def dot(lhs, rhs, lhs_dim, rhs_dim):
    return lax.dot_general(
        lhs, rhs, (((lhs_dim,), (rhs_dim,)), ((), ())), preferred_element_type=F32
    )


def call(body, out_shape, scratch, args, flops):
    spec = pl.BlockSpec(memory_space=pltpu.VMEM)
    total = sum(a.size * a.dtype.itemsize for a in args)
    return pl.pallas_call(
        body,
        out_shape=out_shape,
        in_specs=[spec] * len(args),
        out_specs=[spec] * len(out_shape),
        scratch_shapes=scratch,
        compiler_params=pltpu.CompilerParams(vmem_limit_bytes=VMEM_LIMIT),
        cost_estimate=pl.CostEstimate(flops=flops, bytes_accessed=total, transcendentals=0),
    )(*args)


def packed(parts):
    return jnp.concatenate([p.astype(F32) for p in parts], axis=0).astype(BF16)


def spread_first_kernel(inputs, grads, out):
    block = packed([inputs[...], grads[...]])
    for k in range(CHIPS):
        out[16 * k : 16 * k + 16, :] = block


def spread_kernel(block, out):
    for k in range(CHIPS):
        out[16 * k : 16 * k + 16, :] = block[...]


def join_kernel(a, b, ids, out):
    out[:, 0:D] = packed([a[...], b[...]])
    out[:, D:] = ids[...]


def backward_terms(hidden, gate, up, gates, ups, out):
    d_gate, d_up = [], []
    for h, g, u in zip(hidden, gate, up):
        q = jax.nn.sigmoid(g)
        d_gate.append((h * u * q * (1.0 + g * (1.0 - q))).astype(BF16))
        d_up.append((h * g * q).astype(BF16))
    width = 512
    for low in range(0, D, width):
        cols = pl.ds(low, width)
        total = dot(d_gate[0], gates[0][cols, :], 1, 1)
        total += dot(d_gate[1], gates[1][cols, :], 1, 1)
        total += dot(d_up[0], ups[0][cols, :], 1, 1)
        total += dot(d_up[1], ups[1][cols, :], 1, 1)
        out[:, cols] = total.astype(BF16)


def first_tick_kernel(*refs):
    streams, weights, out, held = refs[:2], refs[2:8], refs[8], refs[9]
    gates, ups, downs = weights[0:2], weights[2:4], weights[4:6]
    for s in range(2):
        held[pl.ds(64 * s, 64), :] = streams[s][...]
    rows = held[...]

    def pick(value, offset):
        return jnp.concatenate(
            [
                value[64 * s + 16 * k + offset : 64 * s + 16 * k + offset + 8]
                for k in range(CHIPS)
                for s in range(2)
            ],
            axis=0,
        )

    gate = [pick(dot(rows, w[...], 1, 0), 0) for w in gates]
    up = [pick(dot(rows, w[...], 1, 0), 0) for w in ups]
    hidden = [pick(dot(rows, w[...], 1, 1), 8) for w in downs]
    backward_terms(hidden, gate, up, gates, ups, out)


def second_tick_kernel(*refs):
    grads, pre, weights, out = refs[0], refs[1:5], refs[5:11], refs[11]
    gates, ups, downs = weights[0:2], weights[2:4], weights[4:6]
    rows = grads[...]
    hidden = [dot(rows, w[...], 1, 1) for w in downs]
    gate = [pre[0][...], pre[1][...]]
    up = [pre[2][...], pre[3][...]]
    backward_terms(hidden, gate, up, gates, ups, out)


def forward_kernel(*refs):
    first_a, first_b, second = refs[0], refs[1], refs[2:6]
    gates, ups, routers = refs[6:8], refs[8:10], refs[10:12]
    base, pre = refs[12], refs[13:17]
    expo_ref, share_ref, stats_ref, held1 = refs[17:21]
    held0, ids_ref = refs[21:23]
    chip = lax.axis_index("expert") // 2
    held0[0:64, :] = first_a[...]
    held0[64:128, :] = first_b[...]
    for k in range(CHIPS):
        rows = pl.ds(pl.multiple_of(lax.rem(chip + k, CHIPS) * 16, 16), 16)
        held1[rows, :] = second[k][:, 0:D]
        ids_ref[rows, :] = second[k][:, D : D + IDCOLS].astype(F32)
    ids_ref[64:128, :] = jnp.full((64, IDCOLS), -1.0, F32)
    rows0, rows1 = held0[...], held1[...]
    for w, out in zip((*gates, *ups), pre):
        out[...] = dot(rows1, w[...], 1, 0)
    logits = jnp.concatenate(
        [
            jnp.concatenate([dot(r[...], rows, 1, 1) for r in routers], axis=0)
            for rows in (rows0, jnp.concatenate([rows1, rows1], axis=0))
        ],
        axis=1,
    )
    ids = ids_ref[...].T
    experts = base[:, 0:1]
    stream_b = (lax.broadcasted_iota(jnp.int32, (2 * OWN, 128), 1) % 16) >= 8
    scale = EXPERTS / (TOKENS * TOPK)
    shares = []
    for tick in range(2):
        hits = jnp.zeros((2 * OWN, 128), F32)
        for core in range(2):
            for j in range(TOPK):
                slot = 16 * core + 8 * tick + j
                hits += (experts == ids[slot : slot + 1, :]).astype(F32)
        count_a = jnp.sum(jnp.where(stream_b, 0.0, hits), axis=1, keepdims=True)
        count_b = jnp.sum(jnp.where(stream_b, hits, 0.0), axis=1, keepdims=True)
        shares.append((count_a * scale, count_b * scale))
    column = lax.broadcasted_iota(jnp.int32, (2 * OWN, 128), 1)
    share0 = jnp.where(column >= 64, shares[0][1], shares[0][0])
    share1 = jnp.where(stream_b, shares[1][1], shares[1][0])
    share = jnp.concatenate([share0, share1], axis=1)
    peak = jnp.max(logits, axis=0, keepdims=True)
    expo = jnp.exp(logits - peak)
    total = jnp.sum(expo, axis=0, keepdims=True)
    weighted = jnp.sum(expo * share, axis=0, keepdims=True)
    expo_ref[...] = expo
    share_ref[...] = share
    stats_ref[...] = jnp.concatenate(
        [peak, total, weighted, jnp.zeros((5, 256), F32)], axis=0
    )


def router_kernel(*refs):
    first_a, first_b, second, expo_ref, share_ref = refs[0:5]
    stats, own_out, other_out = refs[5:9], refs[9], refs[10]
    peaks = [s[0:1, :] for s in stats]
    peak = functools.reduce(jnp.maximum, peaks)
    factors = [jnp.exp(p - peak) for p in peaks]
    total = sum(s[1:2, :] * f for s, f in zip(stats, factors))
    weighted = sum(s[2:3, :] * f for s, f in zip(stats, factors))
    log_total = peak + jnp.log(total)
    mean_share = weighted / total
    probs = expo_ref[...] * (factors[0] / total)
    slopes = (
        2.0 * z_weight * log_total - balance_weight * mean_share + balance_weight * share_ref[...]
    ) * probs
    column = lax.broadcasted_iota(jnp.int32, (2 * OWN, 128), 1)
    slopes0 = jnp.where((column % 16) < 8, slopes[:, 0:128], 0.0).astype(BF16)
    slopes1 = slopes[:, 128:192].astype(BF16)
    width = 512
    for low in range(0, D, width):
        cols = pl.ds(low, width)
        part = dot(slopes0[:, 0:64], first_a[:, cols], 1, 0)
        part += dot(slopes0[:, 64:128], first_b[:, cols], 1, 0)
        part += dot(slopes1, second[:, cols], 1, 0)
        own_out[:, cols] = part[0:OWN]
        other_out[:, cols] = part[OWN:]


def swapped(value):
    return lax.ppermute(value, "expert", [(e, e ^ 1) for e in range(8)])


def mirrored(value):
    count = lax.axis_size("pipe")
    return lax.ppermute(value, "pipe", [(i, count - 1 - i) for i in range(count)])


def exchanged(blocks):
    return lax.all_to_all(
        blocks, "expert", split_axis=0, concat_axis=0, tiled=True,
        axis_index_groups=[[0, 2, 4, 6], [1, 3, 5, 7]],
    )


def spread(value):
    wide = jax.ShapeDtypeStruct((CHIPS * value.shape[0], value.shape[1]), value.dtype)
    return exchanged(call(spread_kernel, [wide], [], [value], 0)[0])


def spread_first(inputs, grads):
    wide = jax.ShapeDtypeStruct((64, D), BF16)
    return exchanged(call(spread_first_kernel, [wide], [], [inputs, grads], 0)[0])


def from_chip(value, k):
    return lax.ppermute(value, "expert", [((e + 2 * k) % 8, e) for e in range(8)])


def ring(value):
    return [value] + [from_chip(value, k) for k in range(1, CHIPS)]


def after(value, *earlier):
    return lax.optimization_barrier((value, *earlier))[0]


def shards(
    stash_a, stash_b, ids_a, ids_b, arriving_a, arriving_b, head_a, head_b,
    w_gate, w_up, w_down, router,
):
    stash_a, stash_b, ids_a, ids_b = stash_a[0], stash_b[0], ids_a[0], ids_b[0]
    arriving_a, arriving_b = arriving_a[0], arriving_b[0]
    w_gate, w_up, w_down, router = w_gate[0], w_up[0], w_down[0], router[0]
    section = lax.axis_index("pipe")
    top = lax.axis_size("pipe") - 1
    member = lax.axis_index("expert")

    arrived_b = mirrored(arriving_b)
    inputs_b = mirrored(stash_b[0])
    first_a = spread_first(stash_a[0], arriving_a)
    first_b = spread_first(inputs_b, arrived_b)

    def id_rows(ids):
        return jnp.concatenate([ids[0], ids[1]], axis=1)

    ids = jnp.concatenate([id_rows(ids_a), id_rows(ids_b)], axis=0).astype(BF16)
    ids = jnp.pad(ids, ((0, 0), (0, 112)), constant_values=-1)
    other_ids = swapped(after(ids, first_a))
    other_gate, other_up, other_down, other_router = (
        swapped(after(weight, first_a)) for weight in (w_gate, w_up, w_down, router)
    )
    gates, ups = [w_gate, other_gate], [w_up, other_up]
    downs, routers = [w_down, other_down], [router, other_router]
    ids = jnp.concatenate([ids[:, :16], other_ids[:, :16], ids[:, 32:]], axis=1)
    later_b = mirrored(jnp.concatenate([stash_b[1], ids[8:]], axis=1))
    sums = [jax.ShapeDtypeStruct((64, D), BF16)]
    (terms,) = call(
        first_tick_kernel, sums, [pltpu.VMEM((128, D), BF16)],
        [first_a, first_b] + gates + ups + downs, 2 * 128 * D * 128 * 10,
    )
    base = jnp.concatenate(
        [OWN * member + jnp.arange(OWN), OWN * (member ^ 1) + jnp.arange(OWN)]
    ).astype(F32)
    base = jnp.broadcast_to(base[:, None], (2 * OWN, 128))

    def emitted(grads, parts):
        total = grads.astype(F32)
        for k in range(CHIPS):
            total = total + parts[16 * k : 16 * k + 16].astype(F32)
        return total.astype(BF16)

    grads = jnp.concatenate([arriving_a, arrived_b], axis=0)
    out = emitted(grads, exchanged(terms))
    moved = lax.ppermute(out, "pipe", [(i, i - 1) for i in range(1, top + 1)])
    (later,) = call(
        join_kernel, [jax.ShapeDtypeStruct((16, D + IDCOLS), BF16)], [],
        [stash_a[1], later_b[:, :D], jnp.concatenate([ids[:8], later_b[:, D:]], axis=0)], 0,
    )
    second = ring(after(later, out))
    head = jnp.concatenate([head_a[0], head_b[0]], axis=0)
    grads = jnp.where(section == top, head, moved)
    all_grads = spread(grads)
    pre = [jax.ShapeDtypeStruct((64, HID), F32)] * 4
    *pre, expo, share, stats, rows1 = call(
        forward_kernel,
        pre
        + [
            jax.ShapeDtypeStruct((2 * OWN, 256), F32),
            jax.ShapeDtypeStruct((2 * OWN, 256), F32),
            jax.ShapeDtypeStruct((8, 256), F32),
            jax.ShapeDtypeStruct((64, D), BF16),
        ],
        [pltpu.VMEM((128, D), BF16), pltpu.VMEM((128, IDCOLS), F32)],
        [first_a, first_b, *second] + gates + ups + routers + [base], 2 * 128 * D * 128 * 4,
    )
    (terms,) = call(
        second_tick_kernel, sums, [],
        [all_grads] + pre + gates + ups + downs, 2 * 64 * D * 128 * 6,
    )
    parts = exchanged(terms)
    stats = ring(stats)
    own, other = call(
        router_kernel, [jax.ShapeDtypeStruct((OWN, D), F32)] * 2, [],
        [first_a, first_b, rows1, after(expo, terms), share, *stats], 2 * 192 * D * 64,
    )
    router_grad = own + swapped(other)
    out = emitted(grads, parts)
    return out[None, :8], mirrored(out[8:])[None], router_grad[None]


def solution(mesh):
    placed = (
        P("pipe", None, "expert", None),
        P("pipe", None, "expert", None),
        P("pipe", None, "expert", None),
        P("pipe", None, "expert", None),
        P("pipe", "expert", None),
        P("pipe", "expert", None),
        P(None, "expert", None),
        P(None, "expert", None),
        P("pipe", None, "expert"),
        P("pipe", None, "expert"),
        P("pipe", "expert", None),
        P("pipe", "expert", None),
    )
    return jax.shard_map(
        shards,
        mesh=mesh,
        in_specs=placed,
        out_specs=(P("pipe", "expert", None), P("pipe", "expert", None), P("pipe", "expert", None)),
        check_vma=False,
    )
```

```python
import functools

import jax
import jax.numpy as jnp
from jax import lax
from jax.experimental import pallas as pl
from jax.experimental.pallas import tpu as pltpu
from jax.sharding import PartitionSpec as P

D = 3584
HID = 128
EXPERTS = 256
OWN = 32
TOKENS = 64
TOPK = 8
ROWS = 8
CHIPS = 4
IDCOLS = 128
WIDE = D + IDCOLS
WIDTH = 512
z_weight = 0.01
balance_weight = 1.0
F32 = jnp.float32
BF16 = jnp.bfloat16
VMEM_LIMIT = 16 * 1024 * 1024


def dot(lhs, rhs, lhs_dim, rhs_dim):
    return lax.dot_general(
        lhs, rhs, (((lhs_dim,), (rhs_dim,)), ((), ())), preferred_element_type=F32
    )


HBM = object()


def call(body, outs, scratch, args, flops):
    vmem = pl.BlockSpec(memory_space=pltpu.VMEM)
    hbm = pl.BlockSpec(memory_space=pltpu.HBM)
    total = sum(a.size * a.dtype.itemsize for a in args)
    return pl.pallas_call(
        body,
        out_shape=[jax.ShapeDtypeStruct(o[0], o[1]) for o in outs],
        in_specs=[vmem] * len(args),
        out_specs=[hbm if o[-1] is HBM else vmem for o in outs],
        scratch_shapes=scratch,
        compiler_params=pltpu.CompilerParams(vmem_limit_bytes=VMEM_LIMIT),
        cost_estimate=pl.CostEstimate(flops=flops, bytes_accessed=total, transcendentals=0),
    )(*args)


def packed(parts):
    return jnp.concatenate([p.astype(F32) for p in parts], axis=0).astype(BF16)


def write_all(block, out, sems):
    rows = block.shape[0]
    copies = [
        pltpu.make_async_copy(block, out.at[pl.ds(rows * k, rows), :], sems.at[k])
        for k in range(CHIPS)
    ]
    for copy in copies:
        copy.start()
    for copy in copies:
        copy.wait()


def id_columns(ids):
    empty = jnp.full((ROWS, IDCOLS - 2 * TOPK), -1.0, F32)
    used = jnp.concatenate([ids[0].astype(F32), ids[1].astype(F32), empty], axis=1)
    return jnp.concatenate([used, jnp.full((ROWS, IDCOLS), -1.0, F32)], axis=0).astype(BF16)


def mirror_pack_kernel(stash, grads, ids, out):
    out[:, 0:D] = packed([stash[0], grads[...]])
    out[:, D:WIDE] = id_columns(ids)


def first_spread_kernel(stash, grads, ids, other, out, block, sems):
    block[0:16, 0:D] = packed([stash[0], grads[...]])
    block[0:16, D:WIDE] = id_columns(ids)
    block[16:32, :] = other[...]
    write_all(block, out, sems)


def second_spread_kernel(stash, other, out, block, sems):
    block[...] = packed([stash[1], other[...]])
    write_all(block, out, sems)


def grads_spread_kernel(moved, head_a, head_b, out, block, sems):
    top = lax.axis_index("pipe") == lax.axis_size("pipe") - 1
    block[...] = moved[...]

    @pl.when(top)
    def _():
        block[...] = packed([head_a[0], head_b[0]])

    write_all(block, out, sems)


def summed(parts, cols):
    total = parts[0:16, cols].astype(F32)
    for k in range(1, CHIPS):
        total += parts[16 * k : 16 * k + 16, cols].astype(F32)
    return total


def first_emit_kernel(parts, grads_a, block_b, out):
    for low in range(0, D, WIDTH):
        cols = pl.ds(low, WIDTH)
        both = jnp.concatenate(
            [grads_a[:, cols].astype(F32), block_b[:, cols].astype(F32)[8:16]], axis=0
        )
        out[:, cols] = (both + summed(parts, cols)).astype(BF16)


def second_emit_kernel(parts, grads, out_a, out_b):
    for low in range(0, D, WIDTH):
        cols = pl.ds(low, WIDTH)
        both = grads[:, cols].astype(F32) + summed(parts, cols)
        out_a[:, cols] = both[0:8].astype(BF16)
        out_b[:, cols] = both[8:16].astype(BF16)


def backward_terms(hidden, gate, up, gates, ups, out, held, sems):
    d_gate, d_up = [], []
    for h, g, u in zip(hidden, gate, up):
        q = jax.nn.sigmoid(g)
        d_gate.append((h * u * q * (1.0 + g * (1.0 - q))).astype(BF16))
        d_up.append((h * g * q).astype(BF16))
    copies = []
    for low in range(0, D, WIDTH):
        cols = pl.ds(low, WIDTH)
        total = dot(d_gate[0], gates[0][cols, :], 1, 1)
        total += dot(d_gate[1], gates[1][cols, :], 1, 1)
        total += dot(d_up[0], ups[0][cols, :], 1, 1)
        total += dot(d_up[1], ups[1][cols, :], 1, 1)
        held[:, cols] = total.astype(BF16)
        copies.append(
            pltpu.make_async_copy(held.at[:, cols], out.at[:, cols], sems.at[low // WIDTH])
        )
        copies[-1].start()
    for copy in copies:
        copy.wait()


def first_tick_kernel(*refs):
    first, weights, out, held, sems = refs[0], refs[1:7], refs[7], refs[8], refs[9]
    gates, ups, downs = weights[0:2], weights[2:4], weights[4:6]
    rows = first[:, 0:D]

    def pick(value, offset):
        return jnp.concatenate(
            [value[16 * b + offset : 16 * b + offset + 8] for b in range(2 * CHIPS)], axis=0
        )

    gate = [pick(dot(rows, w[...], 1, 0), 0) for w in gates]
    up = [pick(dot(rows, w[...], 1, 0), 0) for w in ups]
    hidden = [pick(dot(rows, w[...], 1, 1), 8) for w in downs]
    backward_terms(hidden, gate, up, gates, ups, out, held, sems)


def second_tick_kernel(*refs):
    grads, pre, weights, out, held, sems = refs[0], refs[1:5], refs[5:11], *refs[11:14]
    gates, ups, downs = weights[0:2], weights[2:4], weights[4:6]
    rows = grads[...]
    hidden = [dot(rows, w[...], 1, 1) for w in downs]
    gate = [pre[0][...], pre[1][...]]
    up = [pre[2][...], pre[3][...]]
    backward_terms(hidden, gate, up, gates, ups, out, held, sems)


def forward_kernel(*refs):
    first, second, other_ids = refs[0:3]
    gates, ups, routers = refs[3:5], refs[5:7], refs[7:9]
    pre, expo_ref, share_ref, stats_ref = refs[9:13], *refs[13:16]
    member = lax.axis_index("expert")
    rows0, rows1 = first[:, 0:D], second[...]
    for w, out in zip((*gates, *ups), pre):
        out[...] = dot(rows1, w[...], 1, 0)
    logits = jnp.concatenate(
        [
            jnp.concatenate([dot(r[...], rows, 1, 1) for r in routers], axis=0)
            for rows in (rows0, jnp.concatenate([rows1, rows1], axis=0))
        ],
        axis=1,
    )
    ids = [first[:, D:WIDE].astype(F32).T, other_ids[...].astype(F32).T]
    row = lax.broadcasted_iota(jnp.int32, (2 * OWN, 128), 0)
    column = lax.broadcasted_iota(jnp.int32, (2 * OWN, 128), 1)
    own = row + OWN * member
    other = row - OWN + OWN * (member + 1 - 2 * lax.rem(member, 2))
    experts = jnp.where(row < OWN, own, other).astype(F32)
    stream_b = (column % 32) >= 16
    scale = EXPERTS / (TOKENS * TOPK)
    shares = []
    for tick in range(2):
        hits = jnp.zeros((2 * OWN, 128), F32)
        for core in range(2):
            for j in range(TOPK):
                slot = TOPK * tick + j
                hits += (experts == ids[core][slot : slot + 1, :]).astype(F32)
        count_a = jnp.sum(jnp.where(stream_b, 0.0, hits), axis=1, keepdims=True)
        count_b = jnp.sum(jnp.where(stream_b, hits, 0.0), axis=1, keepdims=True)
        shares.append((count_a * scale, count_b * scale))
    share0 = jnp.where(stream_b, shares[0][1], shares[0][0])
    share1 = jnp.where((column % 16) >= 8, shares[1][1], shares[1][0])
    share = jnp.concatenate([share0, share1], axis=1)
    peak = jnp.max(logits, axis=0, keepdims=True)
    expo = jnp.exp(logits - peak)
    total = jnp.sum(expo, axis=0, keepdims=True)
    weighted = jnp.sum(expo * share, axis=0, keepdims=True)
    expo_ref[...] = expo
    share_ref[...] = share
    stats_ref[...] = jnp.concatenate(
        [peak, total, weighted, jnp.zeros((5, 256), F32)], axis=0
    )


def router_kernel(*refs):
    first, second, expo_ref, share_ref = refs[0:4]
    stats, own_out, other_out = refs[4:8], refs[8], refs[9]
    peaks = [s[0:1, :] for s in stats]
    peak = functools.reduce(jnp.maximum, peaks)
    factors = [jnp.exp(p - peak) for p in peaks]
    total = sum(s[1:2, :] * f for s, f in zip(stats, factors))
    weighted = sum(s[2:3, :] * f for s, f in zip(stats, factors))
    log_total = peak + jnp.log(total)
    mean_share = weighted / total
    probs = expo_ref[...] * (factors[0] / total)
    slopes = (
        2.0 * z_weight * log_total - balance_weight * mean_share + balance_weight * share_ref[...]
    ) * probs
    column = lax.broadcasted_iota(jnp.int32, (2 * OWN, 128), 1)
    slopes0 = jnp.where((column % 16) < 8, slopes[:, 0:128], 0.0).astype(BF16)
    slopes1 = slopes[:, 128:192].astype(BF16)
    for low in range(0, D, WIDTH):
        cols = pl.ds(low, WIDTH)
        part = dot(slopes0, first[:, cols], 1, 0) + dot(slopes1, second[:, cols], 1, 0)
        own_out[:, cols] = part[0:OWN]
        other_out[:, cols] = part[OWN:]


def swapped(value):
    return lax.ppermute(value, "expert", [(e, e ^ 1) for e in range(8)])


def mirrored(value):
    count = lax.axis_size("pipe")
    return lax.ppermute(value, "pipe", [(i, count - 1 - i) for i in range(count)])


def exchanged(blocks):
    return lax.all_to_all(
        blocks, "expert", split_axis=0, concat_axis=0, tiled=True,
        axis_index_groups=[[0, 2, 4, 6], [1, 3, 5, 7]],
    )


def from_chip(value, k):
    return lax.ppermute(value, "expert", [((e + 2 * k) % 8, e) for e in range(8)])


def ring(value):
    return [value] + [from_chip(value, k) for k in range(1, CHIPS)]


def after(value, *earlier):
    return lax.optimization_barrier((value, *earlier))[0]


def shards(
    stash_a, stash_b, ids_a, ids_b, arriving_a, arriving_b, head_a, head_b,
    w_gate, w_up, w_down, router,
):
    stash_a, stash_b, ids_a, ids_b = stash_a[0], stash_b[0], ids_a[0], ids_b[0]
    arriving_a, arriving_b = arriving_a[0], arriving_b[0]
    w_gate, w_up, w_down, router = w_gate[0], w_up[0], w_down[0], router[0]
    top = lax.axis_size("pipe") - 1
    weights = (w_gate, w_up, w_down)
    spread_sems = pltpu.SemaphoreType.DMA((CHIPS,))
    terms_scratch = [pltpu.VMEM((64, D), BF16), pltpu.SemaphoreType.DMA((D // WIDTH,))]

    (packed_b,) = call(mirror_pack_kernel, [((16, WIDE), BF16)], [], [stash_b, arriving_b, ids_b], 0)
    block_b = mirrored(packed_b)
    (blocks,) = call(
        first_spread_kernel, [((128, WIDE), BF16, HBM)],
        [pltpu.VMEM((32, WIDE), BF16), spread_sems], [stash_a, arriving_a, ids_a, block_b], 0,
    )
    first = exchanged(blocks)
    later_b = mirrored(after(stash_b[1], block_b))
    others = [swapped(after(weight, block_b)) for weight in weights]
    pairs = [w for pair in zip(weights, others) for w in pair]

    (terms,) = call(
        first_tick_kernel, [((64, D), BF16, HBM)], terms_scratch,
        [first] + pairs, 2 * 128 * D * 128 * 10,
    )
    parts = exchanged(after(terms, later_b))
    other_router = swapped(after(router, terms))
    other_ids = swapped(after(first[:, D:], terms))
    (out,) = call(first_emit_kernel, [((16, D), BF16)], [], [parts, arriving_a, block_b], 0)
    out = after(out, other_router, other_ids)
    moved = lax.ppermute(out, "pipe", [(i, i - 1) for i in range(1, top + 1)])

    (blocks,) = call(
        second_spread_kernel, [((64, D), BF16, HBM)],
        [pltpu.VMEM((16, D), BF16), spread_sems], [stash_a, later_b], 0,
    )
    second = exchanged(after(blocks, out))
    blocks, grads = call(
        grads_spread_kernel, [((64, D), BF16, HBM), ((16, D), BF16)], [spread_sems],
        [moved, head_a, head_b], 0,
    )
    all_grads = exchanged(after(blocks, second))
    *pre, expo, share, stats = call(
        forward_kernel,
        [((64, HID), F32)] * 4 + [((2 * OWN, 256), F32)] * 2 + [((8, 256), F32)], [],
        [first, second, other_ids] + pairs[:4] + [router, other_router], 2 * 128 * D * 128 * 4,
    )
    stats = ring(stats)
    (terms,) = call(
        second_tick_kernel, [((64, D), BF16, HBM)], terms_scratch,
        [after(all_grads, *stats)] + pre + pairs, 2 * 64 * D * 128 * 6,
    )
    parts = exchanged(terms)
    own, other = call(
        router_kernel, [((OWN, D), F32)] * 2, [],
        [first, second, after(expo, terms), share, *stats], 2 * 192 * D * 64,
    )
    router_grad = own + swapped(other)
    out_a, out_b = call(second_emit_kernel, [((ROWS, D), BF16)] * 2, [], [parts, grads], 0)
    return out_a[None], mirrored(out_b)[None], router_grad[None]


def solution(mesh):
    placed = (
        P("pipe", None, "expert", None),
        P("pipe", None, "expert", None),
        P("pipe", None, "expert", None),
        P("pipe", None, "expert", None),
        P("pipe", "expert", None),
        P("pipe", "expert", None),
        P(None, "expert", None),
        P(None, "expert", None),
        P("pipe", None, "expert"),
        P("pipe", None, "expert"),
        P("pipe", "expert", None),
        P("pipe", "expert", None),
    )
    return jax.shard_map(
        shards,
        mesh=mesh,
        in_specs=placed,
        out_specs=(P("pipe", "expert", None), P("pipe", "expert", None), P("pipe", "expert", None)),
        check_vma=False,
    )
```

```python
import functools

import jax
import jax.numpy as jnp
from jax import lax
from jax.experimental import pallas as pl
from jax.experimental.pallas import tpu as pltpu
from jax.sharding import PartitionSpec as P

D = 3584
HID = 128
EXPERTS = 256
OWN = 32
TOKENS = 64
TOPK = 8
ROWS = 8
CHIPS = 4
IDCOLS = 128
WIDE = D + IDCOLS
WIDTH = 512
z_weight = 0.01
balance_weight = 1.0
F32 = jnp.float32
BF16 = jnp.bfloat16


def dot(lhs, rhs, lhs_dim, rhs_dim):
    return lax.dot_general(
        lhs, rhs, (((lhs_dim,), (rhs_dim,)), ((), ())), preferred_element_type=F32
    )


class Fetched:
    def __init__(self, copies, held):
        self.copies, self.held = copies, held

    def ref(self):
        for copy in self.copies:
            copy.wait()
        self.copies = []
        return self.held


def call(body, outs, args, scratch=(), flops=0):
    n, m = len(args), len(outs)

    def kernel(*refs):
        ins, results, held, made = refs[:n], refs[n : n + m], refs[n + m : 2 * n + m], refs[2 * n + m :]
        made, in_sems, out_sems, rest = made[:m], made[m], made[m + 1], made[m + 2 :]
        fetched = []
        for i, (src, dst) in enumerate(zip(ins, held)):
            copy = pltpu.make_async_copy(src, dst, in_sems.at[i])
            copy.start()
            fetched.append(Fetched([copy], dst))
        pending = body(fetched, made, results, out_sems, *rest) or []
        done = set()
        for index, copies in pending:
            done.add(index)
        for j in range(m):
            if j not in done:
                copy = pltpu.make_async_copy(made[j], results[j], out_sems.at[j, 0])
                copy.start()
                pending.append((j, [copy]))
        for _, copies in pending:
            for copy in copies:
                copy.wait()
        for operand in fetched:
            operand.ref()

    hbm = pl.BlockSpec(memory_space=pltpu.HBM)
    total = sum(a.size * a.dtype.itemsize for a in args)
    return pl.pallas_call(
        kernel,
        out_shape=[jax.ShapeDtypeStruct(o[0], o[1]) for o in outs],
        in_specs=[hbm] * n,
        out_specs=[hbm] * m,
        scratch_shapes=[pltpu.VMEM(a.shape, a.dtype) for a in args]
        + [pltpu.VMEM(o[-1] if len(o) > 2 else o[0], o[1]) for o in outs]
        + [pltpu.SemaphoreType.DMA((n,)), pltpu.SemaphoreType.DMA((m, D // WIDTH + 1))]
        + list(scratch),
        cost_estimate=pl.CostEstimate(flops=flops, bytes_accessed=total, transcendentals=0),
    )(*args)


def packed(parts):
    return jnp.concatenate([p.astype(F32) for p in parts], axis=0).astype(BF16)


def write_all(block, out, sems, j):
    rows = block.shape[0]
    copies = [
        pltpu.make_async_copy(block, out.at[pl.ds(rows * k, rows), :], sems.at[j, k])
        for k in range(CHIPS)
    ]
    for copy in copies:
        copy.start()
    return (j, copies)


def id_columns(ids):
    empty = jnp.full((ROWS, IDCOLS - 2 * TOPK), -1.0, F32)
    used = jnp.concatenate([ids[0].astype(F32), ids[1].astype(F32), empty], axis=1)
    return jnp.concatenate([used, jnp.full((ROWS, IDCOLS), -1.0, F32)], axis=0).astype(BF16)


def mirror_pack_kernel(args, made, results, sems):
    stash, grads, ids = [a.ref() for a in args]
    made[0][:, 0:D] = packed([stash[0], grads[...]])
    made[0][:, D:WIDE] = id_columns(ids)


def first_spread_kernel(args, made, results, sems):
    stash, grads, ids, other = [a.ref() for a in args]
    block = made[0]
    block[0:16, 0:D] = packed([stash[0], grads[...]])
    block[0:16, D:WIDE] = id_columns(ids)
    block[16:32, :] = other[...]
    return [write_all(block, results[0], sems, 0)]


def later_join_kernel(args, made, results, sems):
    stash, other = [a.ref() for a in args]
    made[0][...] = packed([stash[1], other[...]])


def grads_spread_kernel(args, made, results, sems):
    moved, head_a, head_b = [a.ref() for a in args]
    top = lax.axis_index("pipe") == lax.axis_size("pipe") - 1
    heads = packed([head_a[0], head_b[0]]).astype(F32)
    made[1][...] = jnp.where(top, heads, moved[...].astype(F32)).astype(BF16)
    made[0][...] = made[1][...]
    return [write_all(made[0], results[0], sems, 0)]


def summed(parts, cols):
    total = parts[0:16, cols].astype(F32)
    for k in range(1, CHIPS):
        total += parts[16 * k : 16 * k + 16, cols].astype(F32)
    return total


def first_emit_kernel(args, made, results, sems):
    parts, grads_a, block_b = [a.ref() for a in args]
    for low in range(0, D, WIDTH):
        cols = pl.ds(low, WIDTH)
        both = jnp.concatenate(
            [grads_a[:, cols].astype(F32), block_b[:, cols].astype(F32)[8:16]], axis=0
        )
        made[0][:, cols] = (both + summed(parts, cols)).astype(BF16)


def second_emit_kernel(args, made, results, sems):
    parts, grads = [a.ref() for a in args]
    for low in range(0, D, WIDTH):
        cols = pl.ds(low, WIDTH)
        both = grads[:, cols].astype(F32) + summed(parts, cols)
        made[0][:, cols] = both[0:8].astype(BF16)
        made[1][:, cols] = both[8:16].astype(BF16)


def backward_terms(hidden, gate, up, gates, ups, made, results, sems):
    d_gate, d_up = [], []
    for h, g, u in zip(hidden, gate, up):
        q = jax.nn.sigmoid(g)
        d_gate.append((h * u * q * (1.0 + g * (1.0 - q))).astype(BF16))
        d_up.append((h * g * q).astype(BF16))
    copies = []
    for low in range(0, D, WIDTH):
        cols = pl.ds(low, WIDTH)
        total = dot(d_gate[0], gates[0][cols, :], 1, 1)
        total += dot(d_gate[1], gates[1][cols, :], 1, 1)
        total += dot(d_up[0], ups[0][cols, :], 1, 1)
        total += dot(d_up[1], ups[1][cols, :], 1, 1)
        made[0][:, cols] = total.astype(BF16)
        copies.append(
            pltpu.make_async_copy(
                made[0].at[:, cols], results[0].at[:, cols], sems.at[0, low // WIDTH]
            )
        )
        copies[-1].start()
    return copies


def first_tick_kernel(args, made, results, sems):
    first = args[0].ref()
    rows = first[:, 0:D]
    made[1][...] = first[:, D:WIDE]

    def pick(value, offset):
        return jnp.concatenate(
            [value[16 * b + offset : 16 * b + offset + 8] for b in range(2 * CHIPS)], axis=0
        )

    gate = [pick(dot(rows, w.ref()[...], 1, 0), 0) for w in args[1:3]]
    up = [pick(dot(rows, w.ref()[...], 1, 0), 0) for w in args[3:5]]
    hidden = [pick(dot(rows, w.ref()[...], 1, 1), 8) for w in args[5:7]]
    gates, ups = [w.ref() for w in args[1:3]], [w.ref() for w in args[3:5]]
    return [(0, backward_terms(hidden, gate, up, gates, ups, made, results, sems))]


def second_tick_kernel(args, made, results, sems):
    rows = args[0].ref()[...]
    hidden = [dot(rows, w.ref()[...], 1, 1) for w in args[1:3]]
    pre = args[3].ref()
    gate = [pre[:, 0:HID], pre[:, HID : 2 * HID]]
    up = [pre[:, 2 * HID : 3 * HID], pre[:, 3 * HID : 4 * HID]]
    gates, ups = [w.ref() for w in args[4:6]], [w.ref() for w in args[6:8]]
    copies = backward_terms(hidden, gate, up, gates, ups, made, results, sems)
    stats = args[8].ref()
    for k in range(CHIPS):
        made[0][16 * k : 16 * k + 16, D:WIDE] = stats[...]
    last = pltpu.make_async_copy(
        made[0].at[:, pl.ds(D, IDCOLS)], results[0].at[:, pl.ds(D, IDCOLS)], sems.at[0, D // WIDTH]
    )
    last.start()
    return [(0, copies + [last])]


def later_rows(blocks, held1):
    chip = lax.axis_index("expert") // 2
    for k, block in enumerate(blocks):
        rows = pl.ds(pl.multiple_of(lax.rem(chip + k, CHIPS) * 16, 16), 16)
        held1[rows, :] = block.ref()[...]


def forward_kernel(args, made, results, sems, held1):
    pre, expo_ref, share_ref, stats_ref = made
    member = lax.axis_index("expert")
    later_rows(args[2:6], held1)
    rows1 = held1[...]
    for i, w in enumerate(args[6:10]):
        pre[:, HID * i : HID * i + HID] = dot(rows1, w.ref()[...], 1, 0)
    first, other_ids, routers = args[0].ref(), args[1].ref(), [r.ref() for r in args[10:12]]
    rows0 = first[:, 0:D]
    logits = jnp.concatenate(
        [
            jnp.concatenate([dot(r[...], rows, 1, 1) for r in routers], axis=0)
            for rows in (rows0, jnp.concatenate([rows1, rows1], axis=0))
        ],
        axis=1,
    )
    ids = [first[:, D:WIDE].astype(F32).T, other_ids[...].astype(F32).T]
    row = lax.broadcasted_iota(jnp.int32, (2 * OWN, 128), 0)
    column = lax.broadcasted_iota(jnp.int32, (2 * OWN, 128), 1)
    own = row + OWN * member
    other = row - OWN + OWN * (member + 1 - 2 * lax.rem(member, 2))
    experts = jnp.where(row < OWN, own, other).astype(F32)
    stream_b = (column % 32) >= 16
    scale = EXPERTS / (TOKENS * TOPK)
    shares = []
    for tick in range(2):
        hits = jnp.zeros((2 * OWN, 128), F32)
        for core in range(2):
            for j in range(TOPK):
                slot = TOPK * tick + j
                hits += (experts == ids[core][slot : slot + 1, :]).astype(F32)
        count_a = jnp.sum(jnp.where(stream_b, 0.0, hits), axis=1, keepdims=True)
        count_b = jnp.sum(jnp.where(stream_b, hits, 0.0), axis=1, keepdims=True)
        shares.append((count_a * scale, count_b * scale))
    share0 = jnp.where(stream_b, shares[0][1], shares[0][0])
    share1 = jnp.where((column % 16) >= 8, shares[1][1], shares[1][0])
    share = jnp.concatenate([share0, share1], axis=1)
    peak = jnp.max(logits, axis=0, keepdims=True)
    expo = jnp.exp(logits - peak)
    total = jnp.sum(expo, axis=0, keepdims=True)
    weighted = jnp.sum(expo * share, axis=0, keepdims=True)
    expo_ref[...] = expo
    share_ref[...] = share
    figures = []
    for value, count in ((peak, 3), (total, 2), (weighted, 2)):
        for _ in range(count):
            figures.append(value.astype(BF16).astype(F32))
            value = value - figures[-1]
    rows = [f[:, low : low + 128] for low in (0, 128) for f in figures]
    stats_ref[...] = jnp.concatenate(rows + [jnp.zeros((2, 128), F32)], axis=0).astype(BF16)


def router_kernel(args, made, results, sems, held1):
    first, expo_ref, share_ref, parts, own = [a.ref() for a in args[0:5]]
    later_rows(args[5:9], held1)
    stats = []
    for value in [own[...]] + [parts[16 * k : 16 * k + 16, D:WIDE] for k in range(CHIPS)]:
        value = value.astype(F32)
        wide = [jnp.concatenate([value[i : i + 1], value[i + 7 : i + 8]], axis=1) for i in range(7)]
        stats.append((wide[0] + wide[1] + wide[2], wide[3] + wide[4], wide[5] + wide[6]))
    mine, stats = stats[0], stats[1:]
    peaks = [s[0] for s in stats]
    peak = functools.reduce(jnp.maximum, peaks)
    factors = [jnp.exp(p - peak) for p in peaks]
    total = sum(s[1] * f for s, f in zip(stats, factors))
    weighted = sum(s[2] * f for s, f in zip(stats, factors))
    log_total = peak + jnp.log(total)
    mean_share = weighted / total
    probs = expo_ref[...] * (jnp.exp(mine[0] - peak) / total)
    slopes = (
        2.0 * z_weight * log_total - balance_weight * mean_share + balance_weight * share_ref[...]
    ) * probs
    column = lax.broadcasted_iota(jnp.int32, (2 * OWN, 128), 1)
    slopes0 = jnp.where((column % 16) < 8, slopes[:, 0:128], 0.0).astype(BF16)
    slopes1 = slopes[:, 128:192].astype(BF16)
    for low in range(0, D, WIDTH):
        cols = pl.ds(low, WIDTH)
        part = dot(slopes0, first[:, cols], 1, 0) + dot(slopes1, held1[:, cols], 1, 0)
        made[0][:, cols] = part[0:OWN]
        made[1][:, cols] = part[OWN:]


def swapped(value):
    return lax.ppermute(value, "expert", [(e, e ^ 1) for e in range(8)])


def mirrored(value):
    count = lax.axis_size("pipe")
    return lax.ppermute(value, "pipe", [(i, count - 1 - i) for i in range(count)])


def exchanged(blocks):
    return lax.all_to_all(
        blocks, "expert", split_axis=0, concat_axis=0, tiled=True,
        axis_index_groups=[[0, 2, 4, 6], [1, 3, 5, 7]],
    )


def from_chip(value, k):
    return lax.ppermute(value, "expert", [((e + 2 * k) % 8, e) for e in range(8)])


def ring(value):
    return [value] + [from_chip(value, k) for k in range(1, CHIPS)]


def after(value, *earlier):
    return lax.optimization_barrier((value, *earlier))[0]


def shards(
    stash_a, stash_b, ids_a, ids_b, arriving_a, arriving_b, head_a, head_b,
    w_gate, w_up, w_down, router,
):
    stash_a, stash_b, ids_a, ids_b = stash_a[0], stash_b[0], ids_a[0], ids_b[0]
    arriving_a, arriving_b = arriving_a[0], arriving_b[0]
    w_gate, w_up, w_down, router = w_gate[0], w_up[0], w_down[0], router[0]
    top = lax.axis_size("pipe") - 1
    rows_scratch = [pltpu.VMEM((64, D), BF16)]

    (packed_b,) = call(mirror_pack_kernel, [((16, WIDE), BF16)], [stash_b, arriving_b, ids_b])
    block_b = mirrored(packed_b)
    (blocks,) = call(
        first_spread_kernel, [((128, WIDE), BF16, (32, WIDE))],
        [stash_a, arriving_a, ids_a, block_b],
    )
    first = exchanged(blocks)
    gates, ups, downs = (
        [weight, swapped(after(weight, block_b))] for weight in (w_gate, w_up, w_down)
    )
    later_b = mirrored(after(stash_b[1], first))

    terms, ids = call(
        first_tick_kernel, [((64, D), BF16), ((128, IDCOLS), BF16)],
        [first] + gates + ups + downs, (), 2 * 128 * D * 128 * 10,
    )
    parts = exchanged(after(terms, later_b))
    other_router = swapped(after(router, terms))
    other_ids = swapped(ids)
    (later,) = call(later_join_kernel, [((16, D), BF16)], [stash_a, later_b])
    (out,) = call(first_emit_kernel, [((16, D), BF16)], [parts, arriving_a, block_b])
    out = after(out, other_router, other_ids, later)
    moved = lax.ppermute(out, "pipe", [(i, i - 1) for i in range(1, top + 1)])

    second = ring(after(later, out))
    blocks, grads = call(
        grads_spread_kernel, [((64, D), BF16, (16, D)), ((16, D), BF16)], [moved, head_a, head_b]
    )
    all_grads = exchanged(after(blocks, *second))
    pre, expo, share, stats = call(
        forward_kernel,
        [((64, 4 * HID), F32), ((2 * OWN, 256), F32), ((2 * OWN, 256), F32), ((16, IDCOLS), BF16)],
        [first, other_ids] + second + gates + ups + [router, other_router], rows_scratch,
        2 * 128 * D * 128 * 4,
    )
    (terms,) = call(
        second_tick_kernel, [((64, WIDE), BF16)],
        [all_grads] + downs + [pre] + gates + ups + [stats], (), 2 * 64 * D * 128 * 6,
    )
    parts = exchanged(terms)
    out_a, out_b = call(second_emit_kernel, [((ROWS, D), BF16)] * 2, [parts, grads])
    out_b = mirrored(out_b)
    own, other = call(
        router_kernel, [((OWN, D), F32)] * 2, [first, expo, share, parts, stats] + second,
        rows_scratch, 2 * 192 * D * 64,
    )
    return out_a[None], out_b[None], (own + swapped(other))[None]


def solution(mesh):
    placed = (
        P("pipe", None, "expert", None),
        P("pipe", None, "expert", None),
        P("pipe", None, "expert", None),
        P("pipe", None, "expert", None),
        P("pipe", "expert", None),
        P("pipe", "expert", None),
        P(None, "expert", None),
        P(None, "expert", None),
        P("pipe", None, "expert"),
        P("pipe", None, "expert"),
        P("pipe", "expert", None),
        P("pipe", "expert", None),
    )
    return jax.shard_map(
        shards,
        mesh=mesh,
        in_specs=placed,
        out_specs=(P("pipe", "expert", None), P("pipe", "expert", None), P("pipe", "expert", None)),
        check_vma=False,
    )
```

```python
import functools

import jax
import jax.numpy as jnp
from jax import lax
from jax.experimental import pallas as pl
from jax.experimental.pallas import tpu as pltpu
from jax.sharding import PartitionSpec as P

D = 3584
HID = 128
EXPERTS = 256
OWN = 32
TOKENS = 64
TOPK = 8
ROWS = 8
CHIPS = 4
IDCOLS = 128
WIDE = D + IDCOLS
WIDTH = 512
VMEM_LIMIT = 16 * 1024 * 1024
z_weight = 0.01
balance_weight = 1.0
F32 = jnp.float32
BF16 = jnp.bfloat16


def dot(lhs, rhs, lhs_dim, rhs_dim):
    return lax.dot_general(
        lhs, rhs, (((lhs_dim,), (rhs_dim,)), ((), ())), preferred_element_type=F32
    )


def call(body, outs, args, scratch=(), flops=0):
    spec = pl.BlockSpec(memory_space=pltpu.VMEM)
    total = sum(a.size * a.dtype.itemsize for a in args)
    return pl.pallas_call(
        body,
        out_shape=[jax.ShapeDtypeStruct(shape, dtype) for shape, dtype in outs],
        in_specs=[spec] * len(args),
        out_specs=[spec] * len(outs),
        scratch_shapes=list(scratch),
        compiler_params=pltpu.CompilerParams(vmem_limit_bytes=VMEM_LIMIT),
        cost_estimate=pl.CostEstimate(flops=flops, bytes_accessed=total, transcendentals=0),
    )(*args)


def packed(parts):
    return jnp.concatenate([p.astype(F32) for p in parts], axis=0).astype(BF16)


def id_columns(ids):
    empty = jnp.full((ROWS, IDCOLS - 2 * TOPK), -1.0, F32)
    used = jnp.concatenate([ids[0].astype(F32), ids[1].astype(F32), empty], axis=1)
    return jnp.concatenate([used, jnp.full((ROWS, IDCOLS), -1.0, F32)], axis=0).astype(BF16)


def pack_kernel(stash, grads, ids, out):
    out[:, 0:D] = packed([stash[0], grads[...]])
    out[:, D:WIDE] = id_columns(ids)


def join_kernel(stash, other, out):
    out[...] = packed([stash[1], other[...]])


def backward_terms(hidden, gate, up, gates, ups, outs):
    d_gate, d_up = [], []
    for h, g, u in zip(hidden, gate, up):
        q = jax.nn.sigmoid(g)
        d_gate.append((h * u * q * (1.0 + g * (1.0 - q))).astype(BF16))
        d_up.append((h * g * q).astype(BF16))
    for low in range(0, D, WIDTH):
        cols = pl.ds(low, WIDTH)
        total = dot(d_gate[0], gates[0][cols, :], 1, 1)
        total += dot(d_gate[1], gates[1][cols, :], 1, 1)
        total += dot(d_up[0], ups[0][cols, :], 1, 1)
        total += dot(d_up[1], ups[1][cols, :], 1, 1)
        for k in range(CHIPS):
            outs[k][:, cols] = total[16 * k : 16 * k + 16].astype(outs[k].dtype)


def first_rows(blocks, held):
    for b, block in enumerate(blocks):
        held[16 * b : 16 * b + 16, :] = block[:, 0:D]


def first_tick_kernel(*refs):
    blocks, weights, outs, ids, held = refs[:8], refs[8:14], refs[14:18], refs[18], refs[19]
    gates, ups, downs = weights[0:2], weights[2:4], weights[4:6]
    first_rows(blocks, held)
    for b, block in enumerate(blocks):
        ids[16 * b : 16 * b + 16, :] = block[:, D:WIDE]
    rows = held[...]

    def pick(value, offset):
        return jnp.concatenate(
            [value[16 * b + offset : 16 * b + offset + 8] for b in range(2 * CHIPS)], axis=0
        )

    gate = [pick(dot(rows, w[...], 1, 0), 0) for w in gates]
    up = [pick(dot(rows, w[...], 1, 0), 0) for w in ups]
    hidden = [pick(dot(rows, w[...], 1, 1), 8) for w in downs]
    backward_terms(hidden, gate, up, gates, ups, outs)


def second_tick_kernel(*refs):
    blocks, pre, stats, weights = refs[:4], refs[4], refs[5], refs[6:12]
    outs, held = refs[12:16], refs[16]
    gates, ups, downs = weights[0:2], weights[2:4], weights[4:6]
    for k in range(CHIPS):
        held[16 * k : 16 * k + 16, :] = blocks[k][...]
    rows = held[...]
    hidden = [dot(rows, w[...], 1, 1) for w in downs]
    gate = [pre[:, 0:HID], pre[:, HID : 2 * HID]]
    up = [pre[:, 2 * HID : 3 * HID], pre[:, 3 * HID : 4 * HID]]
    backward_terms(hidden, gate, up, gates, ups, outs)
    for k in range(1, CHIPS):
        outs[k][:, D:WIDE] = stats[...]


def forward_kernel(*refs):
    blocks, second, other_ids = refs[0:8], refs[8:12], refs[12]
    weights, routers = refs[13:17], refs[17:19]
    pre, expo_ref, share_ref, stats_ref = refs[19:23]
    held0, held1, ids_ref = refs[23:26]
    member = lax.axis_index("expert")
    first_rows(blocks, held0)
    for b, block in enumerate(blocks):
        ids_ref[16 * b : 16 * b + 16, :] = block[:, D:WIDE].astype(F32)
    for k in range(CHIPS):
        held1[16 * k : 16 * k + 16, :] = second[k][...]
    rows0, rows1 = held0[...], held1[...]
    for i, w in enumerate(weights):
        pre[:, HID * i : HID * i + HID] = dot(rows1, w[...], 1, 0)
    logits = jnp.concatenate(
        [
            jnp.concatenate([dot(r[...], rows, 1, 1) for r in routers], axis=0)
            for rows in (rows0, jnp.concatenate([rows1, rows1], axis=0))
        ],
        axis=1,
    )
    ids = [ids_ref[...].T, other_ids[...].astype(F32).T]
    row = lax.broadcasted_iota(jnp.int32, (2 * OWN, 128), 0)
    column = lax.broadcasted_iota(jnp.int32, (2 * OWN, 128), 1)
    own = row + OWN * member
    other = row - OWN + OWN * (member + 1 - 2 * lax.rem(member, 2))
    experts = jnp.where(row < OWN, own, other).astype(F32)
    stream_b = (column % 32) >= 16
    scale = EXPERTS / (TOKENS * TOPK)
    shares = []
    for tick in range(2):
        hits = jnp.zeros((2 * OWN, 128), F32)
        for core in range(2):
            for j in range(TOPK):
                slot = TOPK * tick + j
                hits += (experts == ids[core][slot : slot + 1, :]).astype(F32)
        count_a = jnp.sum(jnp.where(stream_b, 0.0, hits), axis=1, keepdims=True)
        count_b = jnp.sum(jnp.where(stream_b, hits, 0.0), axis=1, keepdims=True)
        shares.append((count_a * scale, count_b * scale))
    share0 = jnp.where(stream_b, shares[0][1], shares[0][0])
    share1 = jnp.where((column % 16) >= 8, shares[1][1], shares[1][0])
    share = jnp.concatenate([share0, share1], axis=1)
    peak = jnp.max(logits, axis=0, keepdims=True)
    expo = jnp.exp(logits - peak)
    total = jnp.sum(expo, axis=0, keepdims=True)
    weighted = jnp.sum(expo * share, axis=0, keepdims=True)
    expo_ref[...] = expo
    share_ref[...] = share
    figures = []
    for value, count in ((peak, 3), (total, 2), (weighted, 2)):
        for _ in range(count):
            figures.append(value.astype(BF16).astype(F32))
            value = value - figures[-1]
    rows = [f[:, low : low + 128] for low in (0, 128) for f in figures]
    stats_ref[...] = jnp.concatenate(rows + [jnp.zeros((2, 128), F32)], axis=0).astype(BF16)


def router_kernel(*refs):
    blocks, second, expo_ref, share_ref, parts = refs[0:8], refs[8:12], refs[12], refs[13], refs[14:18]
    own_out, other_out, held0, held1 = refs[18:22]
    first_rows(blocks, held0)
    for k in range(CHIPS):
        held1[16 * k : 16 * k + 16, :] = second[k][...]
    stats = []
    for k, part in enumerate(parts):
        value = (part[...] if k == 0 else part[:, D:WIDE]).astype(F32)
        wide = [
            jnp.concatenate(
                [pltpu.roll(value, 32 * k, 1)[i : i + 1], pltpu.roll(value, 16 * k, 1)[i + 7 : i + 8]],
                axis=1,
            )
            if k
            else jnp.concatenate([value[i : i + 1], value[i + 7 : i + 8]], axis=1)
            for i in range(7)
        ]
        stats.append((wide[0] + wide[1] + wide[2], wide[3] + wide[4], wide[5] + wide[6]))
    mine = stats[0]
    peaks = [s[0] for s in stats]
    peak = functools.reduce(jnp.maximum, peaks)
    factors = [jnp.exp(p - peak) for p in peaks]
    total = sum(s[1] * f for s, f in zip(stats, factors))
    weighted = sum(s[2] * f for s, f in zip(stats, factors))
    log_total = peak + jnp.log(total)
    mean_share = weighted / total
    probs = expo_ref[...] * (jnp.exp(mine[0] - peak) / total)
    slopes = (
        2.0 * z_weight * log_total - balance_weight * mean_share + balance_weight * share_ref[...]
    ) * probs
    column = lax.broadcasted_iota(jnp.int32, (2 * OWN, 128), 1)
    slopes0 = jnp.where((column % 16) < 8, slopes[:, 0:128], 0.0).astype(BF16)
    slopes1 = slopes[:, 128:192].astype(BF16)
    for low in range(0, D, WIDTH):
        cols = pl.ds(low, WIDTH)
        part = dot(slopes0, held0[:, cols], 1, 0) + dot(slopes1, held1[:, cols], 1, 0)
        own_out[:, cols] = part[0:OWN]
        other_out[:, cols] = part[OWN:]


def swapped(value):
    return lax.ppermute(value, "expert", [(e, e ^ 1) for e in range(8)])


def mirrored(value):
    count = lax.axis_size("pipe")
    return lax.ppermute(value, "pipe", [(i, count - 1 - i) for i in range(count)])


def from_chip(value, k):
    return lax.ppermute(value, "expert", [((e + 2 * k) % 8, e) for e in range(8)])


def ring(value):
    return [value] + [from_chip(value, k) for k in range(1, CHIPS)]


def returned(parts):
    return [parts[0]] + [from_chip(parts[CHIPS - k], k) for k in range(1, CHIPS)]


def emitted(grads, parts):
    total = grads.astype(F32)
    for part in parts:
        total = total + part[:, :D].astype(F32)
    return total.astype(BF16)


def after(value, *earlier):
    return lax.optimization_barrier((value, *earlier))[0]


def shards(
    stash_a, stash_b, ids_a, ids_b, arriving_a, arriving_b, head_a, head_b,
    w_gate, w_up, w_down, router,
):
    stash_a, stash_b, ids_a, ids_b = stash_a[0], stash_b[0], ids_a[0], ids_b[0]
    arriving_a, arriving_b = arriving_a[0], arriving_b[0]
    w_gate, w_up, w_down, router = w_gate[0], w_up[0], w_down[0], router[0]
    section = lax.axis_index("pipe")
    top = lax.axis_size("pipe") - 1
    rows0, rows1 = pltpu.VMEM((128, D), BF16), pltpu.VMEM((64, D), BF16)

    (packed_b,) = call(pack_kernel, [((16, WIDE), BF16)], [stash_b, arriving_b, ids_b])
    block_b = mirrored(packed_b)
    (block_a,) = call(pack_kernel, [((16, WIDE), BF16)], [stash_a, arriving_a, ids_a])
    blocks_a = ring(block_a)
    blocks_b = ring(block_b)
    first = [block for pair in zip(blocks_a, blocks_b) for block in pair]
    other_gate, other_up, other_down, other_router = lax.optimization_barrier(
        tuple(swapped(weight) for weight in (w_gate, w_up, w_down, router))
    )
    gates, ups, downs = [w_gate, other_gate], [w_up, other_up], [w_down, other_down]
    later_b = mirrored(after(stash_b[1], block_b))
    (later,) = call(join_kernel, [((16, D), BF16)], [stash_a, later_b])
    second = ring(later)

    own_terms = ((16, D), F32)
    *terms, ids = call(
        first_tick_kernel, [own_terms] + [((16, D), BF16)] * 3 + [((128, IDCOLS), BF16)],
        first + gates + ups + downs, [rows0], 2 * 128 * D * 128 * 10,
    )
    terms = lax.optimization_barrier((*terms, *second))[:CHIPS]
    grads = jnp.concatenate([arriving_a, block_b[8:, :D]], axis=0)
    out = emitted(grads, returned(terms))
    moved = lax.ppermute(out, "pipe", [(i, i - 1) for i in range(1, top + 1)])
    head = jnp.concatenate([head_a[0], head_b[0]], axis=0)
    grads = jnp.where(section == top, head, moved)
    all_grads = ring(grads)
    other_ids = swapped(after(ids, out))
    pre, expo, share, stats = call(
        forward_kernel,
        [((64, 4 * HID), F32), ((2 * OWN, 256), F32), ((2 * OWN, 256), F32), ((16, IDCOLS), BF16)],
        first + second + [other_ids] + gates + ups + [router, other_router],
        [rows0, rows1, pltpu.VMEM((128, IDCOLS), F32)], 2 * 128 * D * 128 * 4,
    )
    terms = call(
        second_tick_kernel, [own_terms] + [((16, WIDE), BF16)] * 3,
        all_grads + [pre, stats] + gates + ups + downs, [rows1], 2 * 64 * D * 128 * 6,
    )
    parts = returned(terms)
    out = emitted(grads, parts)
    own, other = call(
        router_kernel, [((OWN, D), F32)] * 2,
        first + second + [after(expo, out), share, stats] + parts[1:], [rows0, rows1],
        2 * 192 * D * 64,
    )
    return out[None, :8], mirrored(out[8:])[None], (own + swapped(other))[None]


def solution(mesh):
    placed = (
        P("pipe", None, "expert", None),
        P("pipe", None, "expert", None),
        P("pipe", None, "expert", None),
        P("pipe", None, "expert", None),
        P("pipe", "expert", None),
        P("pipe", "expert", None),
        P(None, "expert", None),
        P(None, "expert", None),
        P("pipe", None, "expert"),
        P("pipe", None, "expert"),
        P("pipe", "expert", None),
        P("pipe", "expert", None),
    )
    return jax.shard_map(
        shards,
        mesh=mesh,
        in_specs=placed,
        out_specs=(P("pipe", "expert", None), P("pipe", "expert", None), P("pipe", "expert", None)),
        check_vma=False,
    )
```

```python
import functools

import jax
import jax.numpy as jnp
from jax import lax
from jax.experimental import pallas as pl
from jax.experimental.pallas import tpu as pltpu
from jax.sharding import PartitionSpec as P

D = 3584
HID = 128
EXPERTS = 256
OWN = 32
TOKENS = 64
TOPK = 8
ROWS = 8
CHIPS = 4
IDCOLS = 128
WIDE = D + IDCOLS
WIDTH = 512
VMEM_LIMIT = 48 * 1024 * 1024
z_weight = 0.01
balance_weight = 1.0
F32 = jnp.float32
BF16 = jnp.bfloat16


def dot(lhs, rhs, lhs_dim, rhs_dim):
    return lax.dot_general(
        lhs, rhs, (((lhs_dim,), (rhs_dim,)), ((), ())), preferred_element_type=F32
    )


def call(body, outs, args, scratch=(), flops=0):
    spec = pl.BlockSpec(memory_space=pltpu.VMEM)
    total = sum(a.size * a.dtype.itemsize for a in args)
    return pl.pallas_call(
        body,
        out_shape=[jax.ShapeDtypeStruct(shape, dtype) for shape, dtype in outs],
        in_specs=[spec] * len(args),
        out_specs=[spec] * len(outs),
        scratch_shapes=list(scratch),
        compiler_params=pltpu.CompilerParams(vmem_limit_bytes=VMEM_LIMIT),
        cost_estimate=pl.CostEstimate(flops=flops, bytes_accessed=total, transcendentals=0),
    )(*args)


def packed(parts):
    return jnp.concatenate([p.astype(F32) for p in parts], axis=0).astype(BF16)


def pack_kernel(stash, grads, ids, out, held_stash, held_grads, held_ids, sems):
    copies = [
        pltpu.make_async_copy(src, dst, sems.at[i])
        for i, (src, dst) in enumerate(
            ((ids, held_ids), (stash, held_stash), (grads, held_grads))
        )
    ]
    for copy in copies:
        copy.start()
    for copy in copies:
        copy.wait()
    empty = jnp.full((ROWS, IDCOLS - 2 * TOPK), -1.0, F32)
    used = [held_ids[0].astype(F32), held_ids[1].astype(F32), empty]
    for i, rows in enumerate((held_stash[0], held_grads[...], held_stash[1])):
        out[i, :, 0:D] = rows
        out[i, :, D:WIDE] = jnp.full((ROWS, IDCOLS), -1.0, F32).astype(BF16)
    out[0, :, D:WIDE] = jnp.concatenate(used, axis=1).astype(BF16)


def payload(stash, grads, ids):
    hbm = pl.BlockSpec(memory_space=pltpu.HBM)
    return pl.pallas_call(
        pack_kernel,
        out_shape=jax.ShapeDtypeStruct((3, ROWS, WIDE), BF16),
        in_specs=[hbm] * 3,
        out_specs=pl.BlockSpec(memory_space=pltpu.VMEM),
        scratch_shapes=[pltpu.VMEM(a.shape, a.dtype) for a in (stash, grads, ids)]
        + [pltpu.SemaphoreType.DMA((3,))],
    )(stash, grads, ids)


def backward_terms(hidden, gate, up, gates, ups, outs):
    d_gate, d_up = [], []
    for h, g, u in zip(hidden, gate, up):
        q = jax.nn.sigmoid(g)
        d_gate.append((h * u * q * (1.0 + g * (1.0 - q))).astype(BF16))
        d_up.append((h * g * q).astype(BF16))
    for low in range(0, D, WIDTH):
        cols = pl.ds(low, WIDTH)
        total = dot(d_gate[0], gates[0][cols, :], 1, 1)
        total += dot(d_gate[1], gates[1][cols, :], 1, 1)
        total += dot(d_up[0], ups[0][cols, :], 1, 1)
        total += dot(d_up[1], ups[1][cols, :], 1, 1)
        for k in range(CHIPS):
            outs[k][:, cols] = total[16 * k : 16 * k + 16].astype(outs[k].dtype)


def first_rows(blocks, held):
    for b, block in enumerate(blocks):
        held[16 * b : 16 * b + 16, :] = packed([block[0, :, 0:D], block[1, :, 0:D]])


def later_rows(blocks, held):
    for k in range(CHIPS):
        pair = [blocks[2 * k][2, :, 0:D], blocks[2 * k + 1][2, :, 0:D]]
        held[16 * k : 16 * k + 16, :] = packed(pair)


def first_tick_kernel(*refs):
    blocks, weights, outs, ids, held = refs[:8], refs[8:14], refs[14:18], refs[18], refs[19]
    gates, ups, downs = weights[0:2], weights[2:4], weights[4:6]
    first_rows(blocks, held)
    for b, block in enumerate(blocks):
        ids[16 * b : 16 * b + 16, :] = packed([block[0, :, D:WIDE], block[1, :, D:WIDE]])
    rows = held[...]

    def pick(value, offset):
        return jnp.concatenate(
            [value[16 * b + offset : 16 * b + offset + 8] for b in range(2 * CHIPS)], axis=0
        )

    gate = [pick(dot(rows, w[...], 1, 0), 0) for w in gates]
    up = [pick(dot(rows, w[...], 1, 0), 0) for w in ups]
    hidden = [pick(dot(rows, w[...], 1, 1), 8) for w in downs]
    backward_terms(hidden, gate, up, gates, ups, outs)


def second_tick_kernel(*refs):
    blocks, pre, weights = refs[:4], refs[4], refs[5:11]
    outs, held = refs[11:15], refs[15]
    gates, ups, downs = weights[0:2], weights[2:4], weights[4:6]
    for k in range(CHIPS):
        held[16 * k : 16 * k + 16, :] = blocks[k][:, 0:D]
    rows = held[...]
    hidden = [dot(rows, w[...], 1, 1) for w in downs]
    gate = [pre[:, 0:HID], pre[:, HID : 2 * HID]]
    up = [pre[:, 2 * HID : 3 * HID], pre[:, 3 * HID : 4 * HID]]
    backward_terms(hidden, gate, up, gates, ups, outs)


def forward_kernel(*refs):
    blocks, own_ids, other_ids = refs[0:8], refs[8], refs[9]
    weights, routers = refs[10:14], refs[14:16]
    pre, expo_ref, share_ref, stats_ref = refs[16:20]
    held0, held1 = refs[20:22]
    member = lax.axis_index("expert")
    first_rows(blocks, held0)
    later_rows(blocks, held1)
    rows0, rows1 = held0[...], held1[...]
    for i, w in enumerate(weights):
        pre[:, HID * i : HID * i + HID] = dot(rows1, w[...], 1, 0)
    logits = jnp.concatenate(
        [
            jnp.concatenate([dot(r[...], rows, 1, 1) for r in routers], axis=0)
            for rows in (rows0, jnp.concatenate([rows1, rows1], axis=0))
        ],
        axis=1,
    )
    ids = [own_ids[...].astype(F32).T, other_ids[...].astype(F32).T]
    row = lax.broadcasted_iota(jnp.int32, (2 * OWN, 128), 0)
    column = lax.broadcasted_iota(jnp.int32, (2 * OWN, 128), 1)
    own = row + OWN * member
    other = row - OWN + OWN * (member + 1 - 2 * lax.rem(member, 2))
    experts = jnp.where(row < OWN, own, other).astype(F32)
    stream_b = (column % 32) >= 16
    scale = EXPERTS / (TOKENS * TOPK)
    shares = []
    for tick in range(2):
        hits = jnp.zeros((2 * OWN, 128), F32)
        for core in range(2):
            for j in range(TOPK):
                slot = TOPK * tick + j
                hits += (experts == ids[core][slot : slot + 1, :]).astype(F32)
        count_a = jnp.sum(jnp.where(stream_b, 0.0, hits), axis=1, keepdims=True)
        count_b = jnp.sum(jnp.where(stream_b, hits, 0.0), axis=1, keepdims=True)
        shares.append((count_a * scale, count_b * scale))
    share0 = jnp.where(stream_b, shares[0][1], shares[0][0])
    share1 = jnp.where((column % 16) >= 8, shares[1][1], shares[1][0])
    share = jnp.concatenate([share0, share1], axis=1)
    peak = jnp.max(logits, axis=0, keepdims=True)
    expo = jnp.exp(logits - peak)
    total = jnp.sum(expo, axis=0, keepdims=True)
    weighted = jnp.sum(expo * share, axis=0, keepdims=True)
    expo_ref[...] = expo
    share_ref[...] = share
    figures = []
    for value, count in ((peak, 3), (total, 2), (weighted, 2)):
        for _ in range(count):
            figures.append(value.astype(BF16).astype(F32))
            value = value - figures[-1]
    rows = [f[:, low : low + 128] for low in (0, 128) for f in figures]
    stats_ref[...] = jnp.concatenate(rows + [jnp.zeros((2, 128), F32)], axis=0).astype(BF16)


def router_kernel(*refs):
    blocks, expo_ref, share_ref, parts = refs[0:8], refs[8], refs[9], refs[10:14]
    own_out, other_out, held0, held1 = refs[14:18]
    first_rows(blocks, held0)
    later_rows(blocks, held1)
    stats = []
    for k, part in enumerate(parts):
        value = part[:, D:WIDE].astype(F32)
        wide = [
            jnp.concatenate(
                [pltpu.roll(value, 32 * k, 1)[i : i + 1], pltpu.roll(value, 16 * k, 1)[i + 7 : i + 8]],
                axis=1,
            )
            if k
            else jnp.concatenate([value[i : i + 1], value[i + 7 : i + 8]], axis=1)
            for i in range(7)
        ]
        stats.append((wide[0] + wide[1] + wide[2], wide[3] + wide[4], wide[5] + wide[6]))
    mine = stats[0]
    peaks = [s[0] for s in stats]
    peak = functools.reduce(jnp.maximum, peaks)
    factors = [jnp.exp(p - peak) for p in peaks]
    total = sum(s[1] * f for s, f in zip(stats, factors))
    weighted = sum(s[2] * f for s, f in zip(stats, factors))
    log_total = peak + jnp.log(total)
    mean_share = weighted / total
    probs = expo_ref[...] * (jnp.exp(mine[0] - peak) / total)
    slopes = (
        2.0 * z_weight * log_total - balance_weight * mean_share + balance_weight * share_ref[...]
    ) * probs
    column = lax.broadcasted_iota(jnp.int32, (2 * OWN, 128), 1)
    slopes0 = jnp.where((column % 16) < 8, slopes[:, 0:128], 0.0).astype(BF16)
    slopes1 = slopes[:, 128:192].astype(BF16)
    for low in range(0, D, WIDTH):
        cols = pl.ds(low, WIDTH)
        part = dot(slopes0, held0[:, cols], 1, 0) + dot(slopes1, held1[:, cols], 1, 0)
        own_out[:, cols] = part[0:OWN]
        other_out[:, cols] = part[OWN:]


def touch_kernel(value, out):
    pass


def passed(value, flops):
    spec = pl.BlockSpec(memory_space=pl.ANY)
    return pl.pallas_call(
        touch_kernel, out_shape=jax.ShapeDtypeStruct(value.shape, value.dtype),
        in_specs=[spec], out_specs=spec, input_output_aliases={0: 0},
        cost_estimate=pl.CostEstimate(flops=flops, bytes_accessed=0, transcendentals=0),
    )(value)


def swapped(value):
    return lax.ppermute(value, "expert", [(e, e ^ 1) for e in range(8)])


def mirrored(value):
    count = lax.axis_size("pipe")
    return lax.ppermute(value, "pipe", [(i, count - 1 - i) for i in range(count)])


def from_chip(value, k):
    return lax.ppermute(value, "expert", [((e + 2 * k) % 8, e) for e in range(8)])


def ring(value):
    return [value] + [from_chip(value, k) for k in range(1, CHIPS)]


def returned(parts):
    return [parts[0]] + [from_chip(parts[CHIPS - k], k) for k in range(1, CHIPS)]


def emitted(grads, parts):
    total = grads.astype(F32)
    for part in parts:
        total = total + part.astype(F32)
    return total.astype(BF16)


def after(value, *earlier):
    return lax.optimization_barrier((value, *earlier))[0]


def shards(
    stash_a, stash_b, ids_a, ids_b, arriving_a, arriving_b, head_a, head_b,
    w_gate, w_up, w_down, router,
):
    stash_a, stash_b, ids_a, ids_b = stash_a[0], stash_b[0], ids_a[0], ids_b[0]
    arriving_a, arriving_b = arriving_a[0], arriving_b[0]
    w_gate, w_up, w_down, router = w_gate[0], w_up[0], w_down[0], router[0]
    section = lax.axis_index("pipe")
    top = lax.axis_size("pipe") - 1
    rows0, rows1 = pltpu.VMEM((128, D), BF16), pltpu.VMEM((64, D), BF16)

    block_b = mirrored(payload(stash_b, arriving_b, ids_b))
    block_a = payload(stash_a, arriving_a, ids_a)
    blocks_a = ring(block_a)
    other_gate, other_up, other_down, other_router = (
        swapped(weight) for weight in (w_gate, w_up, w_down, router)
    )
    blocks_b = ring(passed(after(block_b, other_gate, other_up, other_down), int(3e9)))
    first = [block for pair in zip(blocks_a, blocks_b) for block in pair]
    gates, ups, downs = [w_gate, other_gate], [w_up, other_up], [w_down, other_down]

    sends = [((16, D), F32)] + [((16, D), BF16)] * 3
    *terms, ids = call(
        first_tick_kernel, sends + [((128, IDCOLS), BF16)],
        first + gates + ups + downs, [rows0], 2 * 128 * D * 128 * 10,
    )
    other_ids = swapped(ids)
    grads = jnp.concatenate([arriving_a, block_b[1, :, :D]], axis=0)
    out = emitted(grads, returned(terms))
    moved = lax.ppermute(out, "pipe", [(i, i - 1) for i in range(1, top + 1)])
    pre, expo, share, stats = call(
        forward_kernel,
        [((64, 4 * HID), F32), ((2 * OWN, 256), F32), ((2 * OWN, 256), F32), ((16, IDCOLS), BF16)],
        first + [ids, other_ids] + gates + ups + [router, other_router],
        [rows0, rows1], 2 * 128 * D * 128 * 4,
    )
    head = jnp.concatenate([head_a[0], head_b[0]], axis=0)
    grads = jnp.where(section == top, head, moved)
    gathered = ring(jnp.concatenate([grads, stats], axis=1))
    terms = call(
        second_tick_kernel, sends, gathered + [pre] + gates + ups + downs, [rows1],
        2 * 64 * D * 128 * 6,
    )
    own, other = call(
        router_kernel, [((OWN, D), F32)] * 2,
        first + [after(expo, *terms), share] + gathered, [rows0, rows1], 2 * 192 * D * 64,
    )
    router_grad = own + swapped(other)
    parts = returned(terms)
    out_a = emitted(grads[:ROWS], [part[:ROWS] for part in parts])
    out_b = emitted(grads[ROWS:], [part[ROWS:] for part in parts])
    return out_a[None], mirrored(out_b)[None], router_grad[None]


def solution(mesh):
    placed = (
        P("pipe", None, "expert", None),
        P("pipe", None, "expert", None),
        P("pipe", None, "expert", None),
        P("pipe", None, "expert", None),
        P("pipe", "expert", None),
        P("pipe", "expert", None),
        P(None, "expert", None),
        P(None, "expert", None),
        P("pipe", None, "expert"),
        P("pipe", None, "expert"),
        P("pipe", "expert", None),
        P("pipe", "expert", None),
    )
    return jax.shard_map(
        shards,
        mesh=mesh,
        in_specs=placed,
        out_specs=(P("pipe", "expert", None), P("pipe", "expert", None), P("pipe", "expert", None)),
        check_vma=False,
    )
```

```python
import functools

import jax
import jax.numpy as jnp
from jax import lax
from jax.experimental import pallas as pl
from jax.experimental.pallas import tpu as pltpu
from jax.sharding import PartitionSpec as P

D = 3584
HID = 128
EXPERTS = 256
OWN = 32
TOKENS = 64
TOPK = 8
ROWS = 8
CHIPS = 4
IDCOLS = 128
WIDE = D + IDCOLS
WIDTH = 512
VMEM_LIMIT = 48 * 1024 * 1024
z_weight = 0.01
balance_weight = 1.0
F32 = jnp.float32
BF16 = jnp.bfloat16


def dot(lhs, rhs, lhs_dim, rhs_dim):
    return lax.dot_general(
        lhs, rhs, (((lhs_dim,), (rhs_dim,)), ((), ())), preferred_element_type=F32
    )


def call(body, outs, args, scratch=(), flops=0):
    spec = pl.BlockSpec(memory_space=pltpu.VMEM)
    total = sum(a.size * a.dtype.itemsize for a in args)
    return pl.pallas_call(
        body,
        out_shape=[jax.ShapeDtypeStruct(shape, dtype) for shape, dtype in outs],
        in_specs=[spec] * len(args),
        out_specs=[spec] * len(outs),
        scratch_shapes=list(scratch),
        compiler_params=pltpu.CompilerParams(vmem_limit_bytes=VMEM_LIMIT),
        cost_estimate=pl.CostEstimate(flops=flops, bytes_accessed=total, transcendentals=0),
    )(*args)


def packed(parts):
    return jnp.concatenate([p.astype(F32) for p in parts], axis=0).astype(BF16)


def pack_kernel(stash, grads, ids, out, held_stash, held_grads, held_ids, sems):
    copies = [
        pltpu.make_async_copy(src, dst, sems.at[i])
        for i, (src, dst) in enumerate(
            ((ids, held_ids), (stash, held_stash), (grads, held_grads))
        )
    ]
    for copy in copies:
        copy.start()
    for copy in copies:
        copy.wait()
    empty = jnp.full((ROWS, IDCOLS - 2 * TOPK), -1.0, F32)
    used = [held_ids[0].astype(F32), held_ids[1].astype(F32), empty]
    for i, rows in enumerate((held_stash[0], held_grads[...], held_stash[1])):
        out[i, :, 0:D] = rows
        out[i, :, D:WIDE] = jnp.full((ROWS, IDCOLS), -1.0, F32).astype(BF16)
    out[0, :, D:WIDE] = jnp.concatenate(used, axis=1).astype(BF16)


def payload(stash, grads, ids):
    hbm = pl.BlockSpec(memory_space=pltpu.HBM)
    return pl.pallas_call(
        pack_kernel,
        out_shape=jax.ShapeDtypeStruct((3, ROWS, WIDE), BF16),
        in_specs=[hbm] * 3,
        out_specs=pl.BlockSpec(memory_space=pltpu.VMEM),
        scratch_shapes=[pltpu.VMEM(a.shape, a.dtype) for a in (stash, grads, ids)]
        + [pltpu.SemaphoreType.DMA((3,))],
    )(stash, grads, ids)


def backward_terms(hidden, gate, up, gates, ups, outs):
    d_gate, d_up = [], []
    for h, g, u in zip(hidden, gate, up):
        q = jax.nn.sigmoid(g)
        d_gate.append((h * u * q * (1.0 + g * (1.0 - q))).astype(BF16))
        d_up.append((h * g * q).astype(BF16))
    for low in range(0, D, WIDTH):
        cols = pl.ds(low, WIDTH)
        total = dot(d_gate[0], gates[0][cols, :], 1, 1)
        total += dot(d_gate[1], gates[1][cols, :], 1, 1)
        total += dot(d_up[0], ups[0][cols, :], 1, 1)
        total += dot(d_up[1], ups[1][cols, :], 1, 1)
        for k in range(CHIPS):
            outs[k][:, cols] = total[16 * k : 16 * k + 16].astype(outs[k].dtype)


def first_rows(blocks, held):
    for b, block in enumerate(blocks):
        held[16 * b : 16 * b + 16, :] = packed([block[0, :, 0:D], block[1, :, 0:D]])


def later_rows(blocks, held):
    for k in range(CHIPS):
        pair = [blocks[2 * k][2, :, 0:D], blocks[2 * k + 1][2, :, 0:D]]
        held[16 * k : 16 * k + 16, :] = packed(pair)


def first_tick_kernel(*refs):
    blocks, weights, outs, ids, held = refs[:8], refs[8:14], refs[14:18], refs[18], refs[19]
    gates, ups, downs = weights[0:2], weights[2:4], weights[4:6]
    first_rows(blocks, held)
    for b, block in enumerate(blocks):
        ids[16 * b : 16 * b + 16, :] = packed([block[0, :, D:WIDE], block[1, :, D:WIDE]])
    rows = held[...]

    def pick(value, offset):
        return jnp.concatenate(
            [value[16 * b + offset : 16 * b + offset + 8] for b in range(2 * CHIPS)], axis=0
        )

    gate = [pick(dot(rows, w[...], 1, 0), 0) for w in gates]
    up = [pick(dot(rows, w[...], 1, 0), 0) for w in ups]
    hidden = [pick(dot(rows, w[...], 1, 1), 8) for w in downs]
    backward_terms(hidden, gate, up, gates, ups, outs)


def second_tick_kernel(*refs):
    blocks, pre, weights = refs[:4], refs[4], refs[5:11]
    outs, held = refs[11:15], refs[15]
    gates, ups, downs = weights[0:2], weights[2:4], weights[4:6]
    for k in range(CHIPS):
        held[16 * k : 16 * k + 16, :] = blocks[k][:, 0:D]
    rows = held[...]
    hidden = [dot(rows, w[...], 1, 1) for w in downs]
    gate = [pre[:, 0:HID], pre[:, HID : 2 * HID]]
    up = [pre[:, 2 * HID : 3 * HID], pre[:, 3 * HID : 4 * HID]]
    backward_terms(hidden, gate, up, gates, ups, outs)


def forward_kernel(*refs):
    blocks, own_ids, other_ids = refs[0:8], refs[8], refs[9]
    weights, routers = refs[10:14], refs[14:16]
    pre, expo_ref, share_ref, stats_ref = refs[16:20]
    held0, held1 = refs[20:22]
    member = lax.axis_index("expert")
    first_rows(blocks, held0)
    later_rows(blocks, held1)
    rows0, rows1 = held0[...], held1[...]
    for i, w in enumerate(weights):
        pre[:, HID * i : HID * i + HID] = dot(rows1, w[...], 1, 0)
    logits = jnp.concatenate(
        [
            jnp.concatenate([dot(r[...], rows, 1, 1) for r in routers], axis=0)
            for rows in (rows0, jnp.concatenate([rows1, rows1], axis=0))
        ],
        axis=1,
    )
    ids = [own_ids[...].astype(F32).T, other_ids[...].astype(F32).T]
    row = lax.broadcasted_iota(jnp.int32, (2 * OWN, 128), 0)
    column = lax.broadcasted_iota(jnp.int32, (2 * OWN, 128), 1)
    own = row + OWN * member
    other = row - OWN + OWN * (member + 1 - 2 * lax.rem(member, 2))
    experts = jnp.where(row < OWN, own, other).astype(F32)
    stream_b = (column % 32) >= 16
    scale = EXPERTS / (TOKENS * TOPK)
    shares = []
    for tick in range(2):
        hits = jnp.zeros((2 * OWN, 128), F32)
        for core in range(2):
            for j in range(TOPK):
                slot = TOPK * tick + j
                hits += (experts == ids[core][slot : slot + 1, :]).astype(F32)
        count_a = jnp.sum(jnp.where(stream_b, 0.0, hits), axis=1, keepdims=True)
        count_b = jnp.sum(jnp.where(stream_b, hits, 0.0), axis=1, keepdims=True)
        shares.append((count_a * scale, count_b * scale))
    share0 = jnp.where(stream_b, shares[0][1], shares[0][0])
    share1 = jnp.where((column % 16) >= 8, shares[1][1], shares[1][0])
    share = jnp.concatenate([share0, share1], axis=1)
    peak = jnp.max(logits, axis=0, keepdims=True)
    expo = jnp.exp(logits - peak)
    total = jnp.sum(expo, axis=0, keepdims=True)
    weighted = jnp.sum(expo * share, axis=0, keepdims=True)
    expo_ref[...] = expo
    share_ref[...] = share
    figures = []
    for value, count in ((peak, 3), (total, 2), (weighted, 2)):
        for _ in range(count):
            figures.append(value.astype(BF16).astype(F32))
            value = value - figures[-1]
    rows = [f[:, low : low + 128] for low in (0, 128) for f in figures]
    stats_ref[...] = jnp.concatenate(rows + [jnp.zeros((2, 128), F32)], axis=0).astype(BF16)


def router_kernel(*refs):
    blocks, expo_ref, share_ref, parts = refs[0:8], refs[8], refs[9], refs[10:14]
    own_out, other_out, held0, held1 = refs[14:18]
    first_rows(blocks, held0)
    later_rows(blocks, held1)
    stats = []
    for k, part in enumerate(parts):
        value = part[:, D:WIDE].astype(F32)
        wide = [
            jnp.concatenate(
                [pltpu.roll(value, 32 * k, 1)[i : i + 1], pltpu.roll(value, 16 * k, 1)[i + 7 : i + 8]],
                axis=1,
            )
            if k
            else jnp.concatenate([value[i : i + 1], value[i + 7 : i + 8]], axis=1)
            for i in range(7)
        ]
        stats.append((wide[0] + wide[1] + wide[2], wide[3] + wide[4], wide[5] + wide[6]))
    mine = stats[0]
    peaks = [s[0] for s in stats]
    peak = functools.reduce(jnp.maximum, peaks)
    factors = [jnp.exp(p - peak) for p in peaks]
    total = sum(s[1] * f for s, f in zip(stats, factors))
    weighted = sum(s[2] * f for s, f in zip(stats, factors))
    log_total = peak + jnp.log(total)
    mean_share = weighted / total
    probs = expo_ref[...] * (jnp.exp(mine[0] - peak) / total)
    slopes = (
        2.0 * z_weight * log_total - balance_weight * mean_share + balance_weight * share_ref[...]
    ) * probs
    column = lax.broadcasted_iota(jnp.int32, (2 * OWN, 128), 1)
    slopes0 = jnp.where((column % 16) < 8, slopes[:, 0:128], 0.0).astype(BF16)
    slopes1 = slopes[:, 128:192].astype(BF16)
    for low in range(0, D, WIDTH):
        cols = pl.ds(low, WIDTH)
        part = dot(slopes0, held0[:, cols], 1, 0) + dot(slopes1, held1[:, cols], 1, 0)
        own_out[:, cols] = part[0:OWN]
        other_out[:, cols] = part[OWN:]


def touch_kernel(value, out):
    pass


def passed(value, flops):
    spec = pl.BlockSpec(memory_space=pl.ANY)
    return pl.pallas_call(
        touch_kernel, out_shape=jax.ShapeDtypeStruct(value.shape, value.dtype),
        in_specs=[spec], out_specs=spec, input_output_aliases={0: 0},
        cost_estimate=pl.CostEstimate(flops=flops, bytes_accessed=0, transcendentals=0),
    )(value)


def swapped(value):
    return lax.ppermute(value, "expert", [(e, e ^ 1) for e in range(8)])


def mirrored(value):
    count = lax.axis_size("pipe")
    return lax.ppermute(value, "pipe", [(i, count - 1 - i) for i in range(count)])


def from_chip(value, k):
    return lax.ppermute(value, "expert", [((e + 2 * k) % 8, e) for e in range(8)])


def ring(value):
    return [value] + [from_chip(value, k) for k in range(1, CHIPS)]


def forwarded_ring(value):
    up, down = from_chip(value, 1), from_chip(value, CHIPS - 1)
    chip = lax.axis_index("expert") // 2
    passed_on = jnp.where(chip == 1, up, jnp.where(chip == 2, down, value))
    route = [(1, 0), (2, 3), (3, 1), (0, 2)]
    far = lax.ppermute(
        passed_on, "expert", [(2 * a + core, 2 * b + core) for a, b in route for core in range(2)]
    )
    return [value, up, far, down]


def returned(parts):
    return [parts[0]] + [from_chip(parts[CHIPS - k], k) for k in range(1, CHIPS)]


def emitted(grads, parts):
    total = grads.astype(F32)
    for part in parts:
        total = total + part.astype(F32)
    return total.astype(BF16)


def after(value, *earlier):
    return lax.optimization_barrier((value, *earlier))[0]


def shards(
    stash_a, stash_b, ids_a, ids_b, arriving_a, arriving_b, head_a, head_b,
    w_gate, w_up, w_down, router,
):
    stash_a, stash_b, ids_a, ids_b = stash_a[0], stash_b[0], ids_a[0], ids_b[0]
    arriving_a, arriving_b = arriving_a[0], arriving_b[0]
    w_gate, w_up, w_down, router = w_gate[0], w_up[0], w_down[0], router[0]
    section = lax.axis_index("pipe")
    top = lax.axis_size("pipe") - 1
    rows0, rows1 = pltpu.VMEM((128, D), BF16), pltpu.VMEM((64, D), BF16)

    block_b = mirrored(payload(stash_b, arriving_b, ids_b))
    block_a = payload(stash_a, arriving_a, ids_a)
    blocks_a = forwarded_ring(block_a)
    other_gate, other_up, other_down = (swapped(weight) for weight in (w_gate, w_up, w_down))
    blocks_b = forwarded_ring(passed(after(block_b, other_gate, other_up, other_down), int(3e9)))
    first = [block for pair in zip(blocks_a, blocks_b) for block in pair]
    other_router = swapped(after(router, blocks_b[1]))
    gates, ups, downs = [w_gate, other_gate], [w_up, other_up], [w_down, other_down]

    sends = [((16, D), F32)] + [((16, D), BF16)] * 3
    *terms, ids = call(
        first_tick_kernel, sends + [((128, IDCOLS), BF16)],
        [after(first[0], other_router)] + first[1:] + gates + ups + downs, [rows0],
        2 * 128 * D * 128 * 10,
    )
    other_ids = swapped(ids)
    grads = jnp.concatenate([arriving_a, block_b[1, :, :D]], axis=0)
    out = after(emitted(grads, returned(terms)), other_ids)
    moved = lax.ppermute(out, "pipe", [(i, i - 1) for i in range(1, top + 1)])
    pre, expo, share, stats = call(
        forward_kernel,
        [((64, 4 * HID), F32), ((2 * OWN, 256), F32), ((2 * OWN, 256), F32), ((16, IDCOLS), BF16)],
        first + [ids, other_ids] + gates + ups + [router, other_router],
        [rows0, rows1], 2 * 128 * D * 128 * 4,
    )
    head = jnp.concatenate([head_a[0], head_b[0]], axis=0)
    grads = jnp.where(section == top, head, moved)
    gathered = ring(jnp.concatenate([grads, stats], axis=1))
    terms = call(
        second_tick_kernel, sends, gathered + [pre] + gates + ups + downs, [rows1],
        2 * 64 * D * 128 * 6,
    )
    own, other = call(
        router_kernel, [((OWN, D), F32)] * 2,
        first + [after(expo, *terms), share] + gathered, [rows0, rows1], 2 * 192 * D * 64,
    )
    router_grad = own + swapped(other)
    parts = returned(terms)
    out_a = emitted(grads[:ROWS], [part[:ROWS] for part in parts])
    out_b = emitted(grads[ROWS:], [part[ROWS:] for part in parts])
    return out_a[None], mirrored(out_b)[None], router_grad[None]


def solution(mesh):
    placed = (
        P("pipe", None, "expert", None),
        P("pipe", None, "expert", None),
        P("pipe", None, "expert", None),
        P("pipe", None, "expert", None),
        P("pipe", "expert", None),
        P("pipe", "expert", None),
        P(None, "expert", None),
        P(None, "expert", None),
        P("pipe", None, "expert"),
        P("pipe", None, "expert"),
        P("pipe", "expert", None),
        P("pipe", "expert", None),
    )
    return jax.shard_map(
        shards,
        mesh=mesh,
        in_specs=placed,
        out_specs=(P("pipe", "expert", None), P("pipe", "expert", None), P("pipe", "expert", None)),
        check_vma=False,
    )
```

```python
import functools

import jax
import jax.numpy as jnp
from jax import lax
from jax.experimental import pallas as pl
from jax.experimental.pallas import tpu as pltpu
from jax.sharding import PartitionSpec as P

D = 3584
HID = 128
EXPERTS = 256
OWN = 32
TOKENS = 64
TOPK = 8
ROWS = 8
CHIPS = 4
IDCOLS = 128
WIDE = D + IDCOLS
WIDTH = 512
VMEM_LIMIT = 48 * 1024 * 1024
z_weight = 0.01
balance_weight = 1.0
F32 = jnp.float32
BF16 = jnp.bfloat16


def dot(lhs, rhs, lhs_dim, rhs_dim):
    return lax.dot_general(
        lhs, rhs, (((lhs_dim,), (rhs_dim,)), ((), ())), preferred_element_type=F32
    )


def call(body, outs, args, scratch=(), flops=0):
    spec = pl.BlockSpec(memory_space=pltpu.VMEM)
    total = sum(a.size * a.dtype.itemsize for a in args)
    return pl.pallas_call(
        body,
        out_shape=[jax.ShapeDtypeStruct(shape, dtype) for shape, dtype in outs],
        in_specs=[spec] * len(args),
        out_specs=[spec] * len(outs),
        scratch_shapes=list(scratch),
        compiler_params=pltpu.CompilerParams(vmem_limit_bytes=VMEM_LIMIT),
        cost_estimate=pl.CostEstimate(flops=flops, bytes_accessed=total, transcendentals=0),
    )(*args)


def packed(parts):
    return jnp.concatenate([p.astype(F32) for p in parts], axis=0).astype(BF16)


def pack_kernel(stash, grads, ids, out, held_stash, held_grads, held_ids, sems):
    copies = [
        pltpu.make_async_copy(src, dst, sems.at[i])
        for i, (src, dst) in enumerate(
            ((ids, held_ids), (stash, held_stash), (grads, held_grads))
        )
    ]
    for copy in copies:
        copy.start()
    for copy in copies:
        copy.wait()
    empty = jnp.full((ROWS, IDCOLS - 2 * TOPK), -1.0, F32)
    used = [held_ids[0].astype(F32), held_ids[1].astype(F32), empty]
    for i, rows in enumerate((held_stash[0], held_grads[...], held_stash[1])):
        out[i, :, 0:D] = rows
        out[i, :, D:WIDE] = jnp.full((ROWS, IDCOLS), -1.0, F32).astype(BF16)
    out[0, :, D:WIDE] = jnp.concatenate(used, axis=1).astype(BF16)


def payload(stash, grads, ids):
    hbm = pl.BlockSpec(memory_space=pltpu.HBM)
    return pl.pallas_call(
        pack_kernel,
        out_shape=jax.ShapeDtypeStruct((3, ROWS, WIDE), BF16),
        in_specs=[hbm] * 3,
        out_specs=pl.BlockSpec(memory_space=pltpu.VMEM),
        scratch_shapes=[pltpu.VMEM(a.shape, a.dtype) for a in (stash, grads, ids)]
        + [pltpu.SemaphoreType.DMA((3,))],
    )(stash, grads, ids)


def differentials(hidden, gate, up):
    d_gate, d_up = [], []
    for h, g, u in zip(hidden, gate, up):
        q = jax.nn.sigmoid(g)
        d_gate.append((h * u * q * (1.0 + g * (1.0 - q))).astype(BF16))
        d_up.append((h * g * q).astype(BF16))
    return d_gate, d_up


def terms_of(d_gate, d_up, gates, ups, cols):
    total = dot(d_gate[0], gates[0][cols, :], 1, 1)
    total += dot(d_gate[1], gates[1][cols, :], 1, 1)
    total += dot(d_up[0], ups[0][cols, :], 1, 1)
    total += dot(d_up[1], ups[1][cols, :], 1, 1)
    return total


def stream_rows(blocks, held):
    for k, block in enumerate(blocks):
        held[16 * k : 16 * k + 16, :] = packed([block[0, :, 0:D], block[1, :, 0:D]])
    for k in range(0, CHIPS, 2):
        pair = [blocks[k][2, :, 0:D], blocks[k + 1][2, :, 0:D]]
        held[64 + 8 * k : 80 + 8 * k, :] = packed(pair)


def first_tick(blocks, weights, pre, ids, held):
    gates, ups, downs = weights[0:2], weights[2:4], weights[4:6]
    stream_rows(blocks, held)
    for k, block in enumerate(blocks):
        ids[16 * k : 16 * k + 16, :] = packed([block[0, :, D:WIDE], block[1, :, D:WIDE]])
    rows = held[...]

    def pick(value, offset):
        return jnp.concatenate(
            [value[16 * k + offset : 16 * k + offset + 8] for k in range(CHIPS)], axis=0
        )

    values = [dot(rows, w[...], 1, 0) for w in (*gates, *ups)]
    for i, value in enumerate(values):
        pre[:, HID * i : HID * i + HID] = value[64:96]
    hidden = [pick(dot(rows[0:64], w[...], 1, 1), 8) for w in downs]
    picked = [pick(value, 0) for value in values]
    return (*differentials(hidden, picked[0:2], picked[2:4]), gates, ups)


def first_a_kernel(*refs):
    blocks, weights, (terms, pre, ids, held) = refs[:4], refs[4:10], refs[10:14]
    operands = first_tick(blocks, weights, pre, ids, held)
    for low in range(0, D, WIDTH):
        cols = pl.ds(low, WIDTH)
        terms[:, cols] = terms_of(*operands, cols)


def first_b_kernel(*refs):
    blocks, weights, terms_a, outs, (pre, ids, held) = (
        refs[:4], refs[4:10], refs[10], refs[11:15], refs[15:18]
    )
    operands = first_tick(blocks, weights, pre, ids, held)
    for low in range(0, D, WIDTH):
        cols = pl.ds(low, WIDTH)
        terms_b = terms_of(*operands, cols)
        for k in range(CHIPS):
            both = [terms_a[8 * k : 8 * k + 8, cols], terms_b[8 * k : 8 * k + 8]]
            outs[k][:, cols] = jnp.concatenate(both, axis=0).astype(outs[k].dtype)


def second_tick_kernel(*refs):
    blocks, pre_a, pre_b, weights = refs[:4], refs[4], refs[5], refs[6:12]
    outs, held = refs[12:16], refs[16]
    gates, ups, downs = weights[0:2], weights[2:4], weights[4:6]
    for k in range(CHIPS):
        held[16 * k : 16 * k + 16, :] = blocks[k][:, 0:D]
    rows = held[...]
    hidden = [dot(rows, w[...], 1, 1) for w in downs]
    pre = jnp.concatenate(
        [p[8 * k : 8 * k + 8, :] for k in range(CHIPS) for p in (pre_a, pre_b)], axis=0
    )
    parts = [pre[:, HID * i : HID * i + HID] for i in range(4)]
    operands = (*differentials(hidden, parts[0:2], parts[2:4]), gates, ups)
    for low in range(0, D, WIDTH):
        cols = pl.ds(low, WIDTH)
        total = terms_of(*operands, cols)
        for k in range(CHIPS):
            outs[k][:, cols] = total[16 * k : 16 * k + 16].astype(outs[k].dtype)


def forward_kernel(*refs):
    streams, own_ids, other_ids, routers = (refs[0:4], refs[4:8]), refs[8:10], refs[10], refs[11:13]
    expo_ref, share_ref, stats_ref, held = refs[13:17]
    member = lax.axis_index("expert")
    logits = []
    for blocks in streams:
        stream_rows(blocks, held)
        held[96:128, :] = held[64:96, :]
        rows = held[...]
        logits.append(jnp.concatenate([dot(r[...], rows, 1, 1) for r in routers], axis=0))
    logits = jnp.concatenate(logits, axis=1)
    ids = [
        jnp.concatenate([own_ids[0][...], own_ids[1][...]], axis=0).astype(F32).T,
        other_ids[...].astype(F32).T,
    ]
    row = lax.broadcasted_iota(jnp.int32, (2 * OWN, 128), 0)
    column = lax.broadcasted_iota(jnp.int32, (2 * OWN, 128), 1)
    own = row + OWN * member
    other = row - OWN + OWN * (member + 1 - 2 * lax.rem(member, 2))
    experts = jnp.where(row < OWN, own, other).astype(F32)
    scale = EXPERTS / (TOKENS * TOPK)
    shares = []
    for tick in range(2):
        hits = jnp.zeros((2 * OWN, 128), F32)
        for core in range(2):
            for j in range(TOPK):
                slot = TOPK * tick + j
                hits += (experts == ids[core][slot : slot + 1, :]).astype(F32)
        count_a = jnp.sum(jnp.where(column < 64, hits, 0.0), axis=1, keepdims=True)
        count_b = jnp.sum(jnp.where(column < 64, 0.0, hits), axis=1, keepdims=True)
        shares.append((count_a * scale, count_b * scale))
    share = jnp.concatenate(
        [jnp.where(column < 64, shares[0][i], shares[1][i]) for i in range(2)], axis=1
    )
    peak = jnp.max(logits, axis=0, keepdims=True)
    expo = jnp.exp(logits - peak)
    total = jnp.sum(expo, axis=0, keepdims=True)
    weighted = jnp.sum(expo * share, axis=0, keepdims=True)
    expo_ref[...] = expo
    share_ref[...] = share
    figures = []
    for value, count in ((peak, 3), (total, 2), (weighted, 2)):
        for _ in range(count):
            figures.append(value.astype(BF16).astype(F32))
            value = value - figures[-1]
    rows = [f[:, low : low + 128] for low in (0, 128) for f in figures]
    stats_ref[...] = jnp.concatenate(rows + [jnp.zeros((2, 128), F32)], axis=0).astype(BF16)


def turned(value, k):
    if k == 0:
        return value
    early, late = value[:, 0:64], value[:, 64:96]
    early = pltpu.roll(jnp.concatenate([early, early], axis=1), 16 * k, 1)
    late = pltpu.roll(jnp.concatenate([late] * 4, axis=1), 8 * k, 1)
    return jnp.concatenate([early[:, 0:64], late[:, 0:64]], axis=1)


def router_kernel(*refs):
    streams, expo_ref, share_ref, parts = (refs[0:4], refs[4:8]), refs[8], refs[9], refs[10:14]
    own_out, other_out, held = refs[14:17]
    stats = []
    for k, part in enumerate(parts):
        value = turned(part[:, D:WIDE].astype(F32), k)
        wide = [jnp.concatenate([value[i : i + 1], value[i + 7 : i + 8]], axis=1) for i in range(7)]
        stats.append((wide[0] + wide[1] + wide[2], wide[3] + wide[4], wide[5] + wide[6]))
    mine = stats[0]
    peaks = [s[0] for s in stats]
    peak = functools.reduce(jnp.maximum, peaks)
    factors = [jnp.exp(p - peak) for p in peaks]
    total = sum(s[1] * f for s, f in zip(stats, factors))
    weighted = sum(s[2] * f for s, f in zip(stats, factors))
    log_total = peak + jnp.log(total)
    mean_share = weighted / total
    probs = expo_ref[...] * (jnp.exp(mine[0] - peak) / total)
    slopes = (
        2.0 * z_weight * log_total - balance_weight * mean_share + balance_weight * share_ref[...]
    ) * probs
    column = lax.broadcasted_iota(jnp.int32, (2 * OWN, 128), 1)
    kept = ((column % 16) < 8) & (column < 64) | (column >= 64) & (column < 96)
    for i, blocks in enumerate(streams):
        stream_rows(blocks, held.at[pl.ds(96 * i, 96), :])
    chosen = [
        jnp.where(kept, slopes[:, 128 * i : 128 * i + 128], 0.0).astype(BF16)[:, 0:96] for i in range(2)
    ]
    for low in range(0, D, WIDTH):
        cols = pl.ds(low, WIDTH)
        part = dot(chosen[0], held[0:96, cols], 1, 0) + dot(chosen[1], held[96:192, cols], 1, 0)
        own_out[:, cols] = part[0:OWN]
        other_out[:, cols] = part[OWN:]


def touch_kernel(value, out):
    pass


def passed(value, flops):
    spec = pl.BlockSpec(memory_space=pl.ANY)
    return pl.pallas_call(
        touch_kernel, out_shape=jax.ShapeDtypeStruct(value.shape, value.dtype),
        in_specs=[spec], out_specs=spec, input_output_aliases={0: 0},
        cost_estimate=pl.CostEstimate(flops=flops, bytes_accessed=0, transcendentals=0),
    )(value)


def swapped(value):
    return lax.ppermute(value, "expert", [(e, e ^ 1) for e in range(8)])


def mirrored(value):
    count = lax.axis_size("pipe")
    return lax.ppermute(value, "pipe", [(i, count - 1 - i) for i in range(count)])


def from_chip(value, k):
    return lax.ppermute(value, "expert", [((e + 2 * k) % 8, e) for e in range(8)])


def ring(value):
    return [value] + [from_chip(value, k) for k in range(1, CHIPS)]


def returned(parts):
    return [parts[0]] + [from_chip(parts[CHIPS - k], k) for k in range(1, CHIPS)]


def emitted(grads, parts):
    total = grads.astype(F32)
    for part in parts:
        total = total + part.astype(F32)
    return total.astype(BF16)


def after(value, *earlier):
    return lax.optimization_barrier((value, *earlier))[0]


def shards(
    stash_a, stash_b, ids_a, ids_b, arriving_a, arriving_b, head_a, head_b,
    w_gate, w_up, w_down, router,
):
    stash_a, stash_b, ids_a, ids_b = stash_a[0], stash_b[0], ids_a[0], ids_b[0]
    arriving_a, arriving_b = arriving_a[0], arriving_b[0]
    w_gate, w_up, w_down, router = w_gate[0], w_up[0], w_down[0], router[0]
    section = lax.axis_index("pipe")
    top = lax.axis_size("pipe") - 1
    block_b = mirrored(payload(stash_b, arriving_b, ids_b))
    block_a = payload(stash_a, arriving_a, ids_a)
    blocks_a = ring(block_a)
    other_gate, other_up, other_down = (swapped(weight) for weight in (w_gate, w_up, w_down))
    blocks_b = ring(passed(after(block_b, other_gate, other_up, other_down), int(3e9)))
    weights = [w_gate, other_gate, w_up, other_up, w_down, other_down]
    rows = [pltpu.VMEM((96, D), BF16)]

    terms_a, pre_a, ids_a = call(
        first_a_kernel, [((32, D), F32), ((32, 4 * HID), F32), ((64, IDCOLS), BF16)],
        blocks_a + weights, rows, 2 * 96 * D * 128 * 8,
    )
    sends = [((16, D), F32)] + [((16, D), BF16)] * 3
    *terms, pre_b, ids_b = call(
        first_b_kernel, sends + [((32, 4 * HID), F32), ((64, IDCOLS), BF16)],
        blocks_b + weights + [terms_a], rows, 2 * 96 * D * 128 * 8,
    )
    other_router = swapped(after(router, terms[0]))
    other_ids = swapped(jnp.concatenate([ids_a, ids_b], axis=0))
    grads = jnp.concatenate([arriving_a, block_b[1, :, :D]], axis=0)
    out = after(emitted(grads, returned(terms)), other_ids)
    moved = lax.ppermute(out, "pipe", [(i, i - 1) for i in range(1, top + 1)])
    expo, share, stats = call(
        forward_kernel, [((2 * OWN, 256), F32), ((2 * OWN, 256), F32), ((16, IDCOLS), BF16)],
        blocks_a + blocks_b + [ids_a, ids_b, other_ids, router, other_router],
        [pltpu.VMEM((128, D), BF16)], 2 * 256 * D * 64,
    )
    head = jnp.concatenate([head_a[0], head_b[0]], axis=0)
    grads = jnp.where(section == top, head, moved)
    gathered = ring(jnp.concatenate([grads, stats], axis=1))
    terms = call(
        second_tick_kernel, sends, gathered + [pre_a, pre_b] + weights, [pltpu.VMEM((64, D), BF16)],
        2 * 64 * D * 128 * 6,
    )
    own, other = call(
        router_kernel, [((OWN, D), F32)] * 2,
        blocks_a + blocks_b + [after(expo, *terms), share] + gathered,
        [pltpu.VMEM((192, D), BF16)], 2 * 192 * D * 64,
    )
    router_grad = own + swapped(other)
    parts = returned(terms)
    out_a = emitted(grads[:ROWS], [part[:ROWS] for part in parts])
    out_b = emitted(grads[ROWS:], [part[ROWS:] for part in parts])
    return out_a[None], after(mirrored(out_b), router_grad)[None], router_grad[None]


def solution(mesh):
    placed = (
        P("pipe", None, "expert", None),
        P("pipe", None, "expert", None),
        P("pipe", None, "expert", None),
        P("pipe", None, "expert", None),
        P("pipe", "expert", None),
        P("pipe", "expert", None),
        P(None, "expert", None),
        P(None, "expert", None),
        P("pipe", None, "expert"),
        P("pipe", None, "expert"),
        P("pipe", "expert", None),
        P("pipe", "expert", None),
    )
    return jax.shard_map(
        shards,
        mesh=mesh,
        in_specs=placed,
        out_specs=(P("pipe", "expert", None), P("pipe", "expert", None), P("pipe", "expert", None)),
        check_vma=False,
    )
```

```python
import functools

import jax
import jax.numpy as jnp
from jax import lax
from jax.experimental import pallas as pl
from jax.experimental.pallas import tpu as pltpu
from jax.sharding import PartitionSpec as P

D = 3584
HID = 128
EXPERTS = 256
OWN = 32
TOKENS = 64
TOPK = 8
ROWS = 8
CHIPS = 4
IDCOLS = 128
WIDE = D + IDCOLS
WIDTH = 512
VMEM_LIMIT = 48 * 1024 * 1024
z_weight = 0.01
balance_weight = 1.0
F32 = jnp.float32
BF16 = jnp.bfloat16


def dot(lhs, rhs, lhs_dim, rhs_dim):
    return lax.dot_general(
        lhs, rhs, (((lhs_dim,), (rhs_dim,)), ((), ())), preferred_element_type=F32
    )


def call(body, outs, args, scratch=(), flops=0):
    spec = pl.BlockSpec(memory_space=pltpu.VMEM)
    total = sum(a.size * a.dtype.itemsize for a in args)
    return pl.pallas_call(
        body,
        out_shape=[jax.ShapeDtypeStruct(shape, dtype) for shape, dtype in outs],
        in_specs=[spec] * len(args),
        out_specs=[spec] * len(outs),
        scratch_shapes=list(scratch),
        compiler_params=pltpu.CompilerParams(vmem_limit_bytes=VMEM_LIMIT),
        cost_estimate=pl.CostEstimate(flops=flops, bytes_accessed=total, transcendentals=0),
    )(*args)


def packed(parts):
    return jnp.concatenate([p.astype(F32) for p in parts], axis=0).astype(BF16)


def pack_kernel(stash, grads, ids, out, held_stash, held_grads, held_ids, sems):
    copies = [
        pltpu.make_async_copy(src, dst, sems.at[i])
        for i, (src, dst) in enumerate(
            ((ids, held_ids), (stash, held_stash), (grads, held_grads))
        )
    ]
    for copy in copies:
        copy.start()
    for copy in copies:
        copy.wait()
    empty = jnp.full((ROWS, IDCOLS - 2 * TOPK), -1.0, F32)
    used = [held_ids[0].astype(F32), held_ids[1].astype(F32), empty]
    for i, rows in enumerate((held_stash[0], held_grads[...], held_stash[1])):
        out[i, :, 0:D] = rows
        out[i, :, D:WIDE] = jnp.full((ROWS, IDCOLS), -1.0, F32).astype(BF16)
    out[0, :, D:WIDE] = jnp.concatenate(used, axis=1).astype(BF16)


def payload(stash, grads, ids):
    hbm = pl.BlockSpec(memory_space=pltpu.HBM)
    return pl.pallas_call(
        pack_kernel,
        out_shape=jax.ShapeDtypeStruct((3, ROWS, WIDE), BF16),
        in_specs=[hbm] * 3,
        out_specs=pl.BlockSpec(memory_space=pltpu.VMEM),
        scratch_shapes=[pltpu.VMEM(a.shape, a.dtype) for a in (stash, grads, ids)]
        + [pltpu.SemaphoreType.DMA((3,))],
    )(stash, grads, ids)


def differentials(hidden, gate, up):
    d_gate, d_up = [], []
    for h, g, u in zip(hidden, gate, up):
        q = jax.nn.sigmoid(g)
        d_gate.append((h * u * q * (1.0 + g * (1.0 - q))).astype(BF16))
        d_up.append((h * g * q).astype(BF16))
    return d_gate, d_up


def terms_of(d_gate, d_up, gates, ups, cols):
    total = dot(d_gate[0], gates[0][cols, :], 1, 1)
    total += dot(d_gate[1], gates[1][cols, :], 1, 1)
    total += dot(d_up[0], ups[0][cols, :], 1, 1)
    total += dot(d_up[1], ups[1][cols, :], 1, 1)
    return total


def stream_rows(blocks, held):
    for k, block in enumerate(blocks):
        held[16 * k : 16 * k + 16, :] = packed([block[0, :, 0:D], block[1, :, 0:D]])
    for k in range(0, CHIPS, 2):
        pair = [blocks[k][2, :, 0:D], blocks[k + 1][2, :, 0:D]]
        held[64 + 8 * k : 80 + 8 * k, :] = packed(pair)


def first_tick(blocks, weights, pre, ids, held):
    gates, ups, downs = weights[0:2], weights[2:4], weights[4:6]
    stream_rows(blocks, held)
    for k, block in enumerate(blocks):
        ids[16 * k : 16 * k + 16, :] = packed([block[0, :, D:WIDE], block[1, :, D:WIDE]])
    rows = held[...]

    def pick(value, offset):
        return jnp.concatenate(
            [value[16 * k + offset : 16 * k + offset + 8] for k in range(CHIPS)], axis=0
        )

    values = [dot(rows, w[...], 1, 0) for w in (*gates, *ups)]
    for i, value in enumerate(values):
        pre[:, HID * i : HID * i + HID] = value[64:96]
    hidden = [pick(dot(rows[0:64], w[...], 1, 1), 8) for w in downs]
    picked = [pick(value, 0) for value in values]
    return (*differentials(hidden, picked[0:2], picked[2:4]), gates, ups)


def first_a_kernel(*refs):
    blocks, weights, (terms, pre, ids, held) = refs[:4], refs[4:10], refs[10:14]
    operands = first_tick(blocks, weights, pre, ids, held)
    for low in range(0, D, WIDTH):
        cols = pl.ds(low, WIDTH)
        terms[:, cols] = terms_of(*operands, cols)


def first_b_kernel(*refs):
    blocks, weights, terms_a, outs, (pre, ids, held) = (
        refs[:4], refs[4:10], refs[10], refs[11:15], refs[15:18]
    )
    operands = first_tick(blocks, weights, pre, ids, held)
    for low in range(0, D, WIDTH):
        cols = pl.ds(low, WIDTH)
        terms_b = terms_of(*operands, cols)
        for k in range(CHIPS):
            both = [terms_a[8 * k : 8 * k + 8, cols], terms_b[8 * k : 8 * k + 8]]
            outs[k][:, cols] = jnp.concatenate(both, axis=0).astype(outs[k].dtype)


def second_tick_kernel(*refs):
    blocks, pre_a, pre_b, weights = refs[:4], refs[4], refs[5], refs[6:12]
    outs, held = refs[12:16], refs[16]
    gates, ups, downs = weights[0:2], weights[2:4], weights[4:6]
    for k in range(CHIPS):
        held[16 * k : 16 * k + 16, :] = blocks[k][:, 0:D]
    rows = held[...]
    hidden = [dot(rows, w[...], 1, 1) for w in downs]
    pre = jnp.concatenate(
        [p[8 * k : 8 * k + 8, :] for k in range(CHIPS) for p in (pre_a, pre_b)], axis=0
    )
    parts = [pre[:, HID * i : HID * i + HID] for i in range(4)]
    operands = (*differentials(hidden, parts[0:2], parts[2:4]), gates, ups)
    for low in range(0, D, WIDTH):
        cols = pl.ds(low, WIDTH)
        total = terms_of(*operands, cols)
        for k in range(CHIPS):
            outs[k][:, cols] = total[16 * k : 16 * k + 16].astype(outs[k].dtype)


def forward_kernel(*refs):
    streams, own_ids, other_ids, routers = (refs[0:4], refs[4:8]), refs[8:10], refs[10], refs[11:13]
    expo_ref, share_ref, stats_ref, held = refs[13:17]
    member = lax.axis_index("expert")
    logits = []
    for blocks in streams:
        stream_rows(blocks, held)
        held[96:128, :] = held[64:96, :]
        rows = held[...]
        logits.append(jnp.concatenate([dot(r[...], rows, 1, 1) for r in routers], axis=0))
    logits = jnp.concatenate(logits, axis=1)
    ids = [
        jnp.concatenate([own_ids[0][...], own_ids[1][...]], axis=0).astype(F32).T,
        other_ids[...].astype(F32).T,
    ]
    row = lax.broadcasted_iota(jnp.int32, (2 * OWN, 128), 0)
    column = lax.broadcasted_iota(jnp.int32, (2 * OWN, 128), 1)
    own = row + OWN * member
    other = row - OWN + OWN * (member + 1 - 2 * lax.rem(member, 2))
    experts = jnp.where(row < OWN, own, other).astype(F32)
    scale = EXPERTS / (TOKENS * TOPK)
    shares = []
    for tick in range(2):
        hits = jnp.zeros((2 * OWN, 128), F32)
        for core in range(2):
            for j in range(TOPK):
                slot = TOPK * tick + j
                hits += (experts == ids[core][slot : slot + 1, :]).astype(F32)
        count_a = jnp.sum(jnp.where(column < 64, hits, 0.0), axis=1, keepdims=True)
        count_b = jnp.sum(jnp.where(column < 64, 0.0, hits), axis=1, keepdims=True)
        shares.append((count_a * scale, count_b * scale))
    share = jnp.concatenate(
        [jnp.where(column < 64, shares[0][i], shares[1][i]) for i in range(2)], axis=1
    )
    peak = jnp.max(logits, axis=0, keepdims=True)
    expo = jnp.exp(logits - peak)
    total = jnp.sum(expo, axis=0, keepdims=True)
    weighted = jnp.sum(expo * share, axis=0, keepdims=True)
    expo_ref[...] = expo
    share_ref[...] = share
    figures = []
    for value, count in ((peak, 3), (total, 2), (weighted, 2)):
        for _ in range(count):
            figures.append(value.astype(BF16).astype(F32))
            value = value - figures[-1]
    rows = [f[:, low : low + 128] for low in (0, 128) for f in figures]
    stats_ref[...] = jnp.concatenate(rows + [jnp.zeros((2, 128), F32)], axis=0).astype(BF16)


def turned(value, k):
    if k == 0:
        return value
    early, late = value[:, 0:64], value[:, 64:96]
    early = pltpu.roll(jnp.concatenate([early, early], axis=1), 16 * k, 1)
    late = pltpu.roll(jnp.concatenate([late] * 4, axis=1), 8 * k, 1)
    return jnp.concatenate([early[:, 0:64], late[:, 0:64]], axis=1)


def router_kernel(*refs):
    streams, expo_ref, share_ref, parts = (refs[0:4], refs[4:8]), refs[8], refs[9], refs[10:14]
    own_out, other_out, held = refs[14:17]
    stats = []
    for k, part in enumerate(parts):
        value = turned(part[:, D:WIDE].astype(F32), k)
        wide = [jnp.concatenate([value[i : i + 1], value[i + 7 : i + 8]], axis=1) for i in range(7)]
        stats.append((wide[0] + wide[1] + wide[2], wide[3] + wide[4], wide[5] + wide[6]))
    mine = stats[0]
    peaks = [s[0] for s in stats]
    peak = functools.reduce(jnp.maximum, peaks)
    factors = [jnp.exp(p - peak) for p in peaks]
    total = sum(s[1] * f for s, f in zip(stats, factors))
    weighted = sum(s[2] * f for s, f in zip(stats, factors))
    log_total = peak + jnp.log(total)
    mean_share = weighted / total
    probs = expo_ref[...] * (jnp.exp(mine[0] - peak) / total)
    slopes = (
        2.0 * z_weight * log_total - balance_weight * mean_share + balance_weight * share_ref[...]
    ) * probs
    column = lax.broadcasted_iota(jnp.int32, (2 * OWN, 128), 1)
    kept = ((column % 16) < 8) & (column < 64) | (column >= 64) & (column < 96)
    for i, blocks in enumerate(streams):
        stream_rows(blocks, held.at[pl.ds(96 * i, 96), :])
    chosen = [
        jnp.where(kept, slopes[:, 128 * i : 128 * i + 128], 0.0).astype(BF16)[:, 0:96] for i in range(2)
    ]
    for low in range(0, D, WIDTH):
        cols = pl.ds(low, WIDTH)
        part = dot(chosen[0], held[0:96, cols], 1, 0) + dot(chosen[1], held[96:192, cols], 1, 0)
        own_out[:, cols] = part[0:OWN]
        other_out[:, cols] = part[OWN:]


def touch_kernel(value, out):
    pass


def passed(value, flops):
    spec = pl.BlockSpec(memory_space=pl.ANY)
    return pl.pallas_call(
        touch_kernel, out_shape=jax.ShapeDtypeStruct(value.shape, value.dtype),
        in_specs=[spec], out_specs=spec, input_output_aliases={0: 0},
        cost_estimate=pl.CostEstimate(flops=flops, bytes_accessed=0, transcendentals=0),
    )(value)


def swapped(value):
    return lax.ppermute(value, "expert", [(e, e ^ 1) for e in range(8)])


def mirrored(value):
    count = lax.axis_size("pipe")
    return lax.ppermute(value, "pipe", [(i, count - 1 - i) for i in range(count)])


def from_chip(value, k):
    return lax.ppermute(value, "expert", [((e + 2 * k) % 8, e) for e in range(8)])


def ring(value):
    return [value] + [from_chip(value, k) for k in range(1, CHIPS)]


def returned(parts):
    return [parts[0]] + [from_chip(parts[CHIPS - k], k) for k in range(1, CHIPS)]


def emitted(grads, parts):
    total = grads.astype(F32)
    for part in parts:
        total = total + part.astype(F32)
    return total.astype(BF16)


def after(value, *earlier):
    return lax.optimization_barrier((value, *earlier))[0]


def shards(
    stash_a, stash_b, ids_a, ids_b, arriving_a, arriving_b, head_a, head_b,
    w_gate, w_up, w_down, router,
):
    stash_a, stash_b, ids_a, ids_b = stash_a[0], stash_b[0], ids_a[0], ids_b[0]
    arriving_a, arriving_b = arriving_a[0], arriving_b[0]
    w_gate, w_up, w_down, router = w_gate[0], w_up[0], w_down[0], router[0]
    section = lax.axis_index("pipe")
    top = lax.axis_size("pipe") - 1
    block_b = mirrored(payload(stash_b, arriving_b, ids_b))
    block_a = payload(stash_a, arriving_a, ids_a)
    blocks_a = ring(block_a)
    other_gate, other_up, other_down = (swapped(weight) for weight in (w_gate, w_up, w_down))
    blocks_b = ring(passed(after(block_b, other_gate, other_up, other_down), int(3e9)))
    weights = [w_gate, other_gate, w_up, other_up, w_down, other_down]
    rows = [pltpu.VMEM((96, D), BF16)]

    terms_a, pre_a, ids_a = call(
        first_a_kernel, [((32, D), F32), ((32, 4 * HID), F32), ((64, IDCOLS), BF16)],
        blocks_a + weights, rows, 2 * 96 * D * 128 * 8,
    )
    other_router = swapped(after(router, block_b))
    sends = [((16, D), F32)] + [((16, D), BF16)] * 3
    *terms, pre_b, ids_b = call(
        first_b_kernel, sends + [((32, 4 * HID), F32), ((64, IDCOLS), BF16)],
        blocks_b + weights + [after(terms_a, other_router)], rows, 2 * 96 * D * 128 * 8,
    )
    other_ids = swapped(jnp.concatenate([ids_a, ids_b], axis=0))
    grads = jnp.concatenate([arriving_a, block_b[1, :, :D]], axis=0)
    out = after(emitted(grads, returned(terms)), other_ids)
    moved = lax.ppermute(out, "pipe", [(i, i - 1) for i in range(1, top + 1)])
    expo, share, stats = call(
        forward_kernel, [((2 * OWN, 256), F32), ((2 * OWN, 256), F32), ((16, IDCOLS), BF16)],
        blocks_a + blocks_b + [ids_a, ids_b, other_ids, router, other_router],
        [pltpu.VMEM((128, D), BF16)], 2 * 256 * D * 64,
    )
    head = jnp.concatenate([head_a[0], head_b[0]], axis=0)
    grads = jnp.where(section == top, head, moved)
    gathered = ring(jnp.concatenate([grads, stats], axis=1))
    terms = call(
        second_tick_kernel, sends, gathered + [pre_a, pre_b] + weights, [pltpu.VMEM((64, D), BF16)],
        2 * 64 * D * 128 * 6,
    )
    parts = returned(terms)
    out_a = emitted(grads[:ROWS], [part[:ROWS] for part in parts])
    out_b = emitted(grads[ROWS:], [part[ROWS:] for part in parts])
    own, other = call(
        router_kernel, [((OWN, D), F32)] * 2,
        blocks_a + blocks_b + [after(expo, out_b), share] + gathered,
        [pltpu.VMEM((192, D), BF16)], 2 * 192 * D * 64,
    )
    router_grad = own + swapped(other)
    return out_a[None], passed(mirrored(out_b), int(3e11))[None], router_grad[None]


def solution(mesh):
    placed = (
        P("pipe", None, "expert", None),
        P("pipe", None, "expert", None),
        P("pipe", None, "expert", None),
        P("pipe", None, "expert", None),
        P("pipe", "expert", None),
        P("pipe", "expert", None),
        P(None, "expert", None),
        P(None, "expert", None),
        P("pipe", None, "expert"),
        P("pipe", None, "expert"),
        P("pipe", "expert", None),
        P("pipe", "expert", None),
    )
    return jax.shard_map(
        shards,
        mesh=mesh,
        in_specs=placed,
        out_specs=(P("pipe", "expert", None), P("pipe", "expert", None), P("pipe", "expert", None)),
        check_vma=False,
    )
```

```python
import functools

import jax
import jax.numpy as jnp
from jax import lax
from jax.experimental import pallas as pl
from jax.experimental.pallas import tpu as pltpu
from jax.sharding import PartitionSpec as P

D = 3584
HID = 128
EXPERTS = 256
OWN = 32
TOKENS = 64
TOPK = 8
ROWS = 8
CHIPS = 4
IDCOLS = 128
WIDE = D + IDCOLS
WIDTH = 512
VMEM_LIMIT = 40 * 1024 * 1024
z_weight = 0.01
balance_weight = 1.0
F32 = jnp.float32
BF16 = jnp.bfloat16


def dot(lhs, rhs, lhs_dim, rhs_dim):
    return lax.dot_general(
        lhs, rhs, (((lhs_dim,), (rhs_dim,)), ((), ())), preferred_element_type=F32
    )


def call(body, outs, args, scratch=(), flops=0):
    spec = pl.BlockSpec(memory_space=pltpu.VMEM)
    total = sum(a.size * a.dtype.itemsize for a in args)
    return pl.pallas_call(
        body,
        out_shape=[jax.ShapeDtypeStruct(shape, dtype) for shape, dtype in outs],
        in_specs=[spec] * len(args),
        out_specs=[spec] * len(outs),
        scratch_shapes=list(scratch),
        compiler_params=pltpu.CompilerParams(vmem_limit_bytes=VMEM_LIMIT),
        cost_estimate=pl.CostEstimate(flops=flops, bytes_accessed=total, transcendentals=0),
    )(*args)


def packed(parts):
    return jnp.concatenate([p.astype(F32) for p in parts], axis=0).astype(BF16)


def pack_kernel(stash, grads, ids, out, held_stash, held_grads, held_ids, sems):
    copies = [
        pltpu.make_async_copy(src, dst, sems.at[i])
        for i, (src, dst) in enumerate(
            ((ids, held_ids), (stash, held_stash), (grads, held_grads))
        )
    ]
    for copy in copies:
        copy.start()
    for copy in copies:
        copy.wait()
    empty = jnp.full((ROWS, IDCOLS - 2 * TOPK), -1.0, F32)
    used = [held_ids[0].astype(F32), held_ids[1].astype(F32), empty]
    for i, rows in enumerate((held_stash[0], held_grads[...], held_stash[1])):
        out[i, :, 0:D] = rows
        out[i, :, D:WIDE] = jnp.full((ROWS, IDCOLS), -1.0, F32).astype(BF16)
    out[0, :, D:WIDE] = jnp.concatenate(used, axis=1).astype(BF16)


def payload(stash, grads, ids):
    hbm = pl.BlockSpec(memory_space=pltpu.HBM)
    return pl.pallas_call(
        pack_kernel,
        out_shape=jax.ShapeDtypeStruct((3, ROWS, WIDE), BF16),
        in_specs=[hbm] * 3,
        out_specs=pl.BlockSpec(memory_space=pltpu.VMEM),
        scratch_shapes=[pltpu.VMEM(a.shape, a.dtype) for a in (stash, grads, ids)]
        + [pltpu.SemaphoreType.DMA((3,))],
    )(stash, grads, ids)


def differentials(hidden, gate, up):
    q = jax.nn.sigmoid(gate)
    d_gate = (hidden * up * q * (1.0 + gate * (1.0 - q))).astype(BF16)
    d_up = (hidden * gate * q).astype(BF16)
    return jnp.concatenate([d_gate, d_up], axis=1)


def stream_rows(blocks, held):
    for k, block in enumerate(blocks):
        held[16 * k : 16 * k + 16, :] = packed([block[0, :, 0:D], block[1, :, 0:D]])
    for k in range(0, CHIPS, 2):
        pair = [blocks[k][2, :, 0:D], blocks[k + 1][2, :, 0:D]]
        held[64 + 8 * k : 80 + 8 * k, :] = packed(pair)


def first_tick(blocks, wide, downs, pre, ids, held):
    stream_rows(blocks, held)
    for k, block in enumerate(blocks):
        ids[16 * k : 16 * k + 16, :] = packed([block[0, :, D:WIDE], block[1, :, D:WIDE]])
    rows = held[...]

    def pick(value, offset):
        return jnp.concatenate(
            [value[16 * k + offset : 16 * k + offset + 8] for k in range(CHIPS)], axis=0
        )

    values = dot(rows, wide[...], 1, 0)
    pre[...] = values[64:96]
    hidden = pick(dot(rows[0:64], downs[...], 1, 1), 8)
    values = pick(values, 0)
    return differentials(hidden, values[:, 0 : 2 * HID], values[:, 2 * HID :])


def first_a_kernel(*refs):
    blocks, weights, (terms, pre, ids, wide, downs, held) = refs[:4], refs[4:10], refs[10:16]
    for i, w in enumerate(weights[0:4]):
        wide[:, HID * i : HID * i + HID] = w[...]
    for i, w in enumerate(weights[4:6]):
        downs[HID * i : HID * i + HID, :] = w[...]
    operand = first_tick(blocks, wide, downs, pre, ids, held)
    for low in range(0, D, WIDTH):
        cols = pl.ds(low, WIDTH)
        terms[:, cols] = dot(operand, wide[cols, :], 1, 1)


def first_b_kernel(*refs):
    blocks, wide, downs, terms_a, outs = refs[:4], refs[4], refs[5], refs[6], refs[7:11]
    pre, ids, held = refs[11:14]
    operand = first_tick(blocks, wide, downs, pre, ids, held)
    for low in range(0, D, WIDTH):
        cols = pl.ds(low, WIDTH)
        terms_b = dot(operand, wide[cols, :], 1, 1)
        for k in range(CHIPS):
            both = [terms_a[8 * k : 8 * k + 8, cols], terms_b[8 * k : 8 * k + 8]]
            outs[k][:, cols] = jnp.concatenate(both, axis=0).astype(outs[k].dtype)


def second_tick_kernel(*refs):
    blocks, pre_a, pre_b, wide, downs = refs[:4], *refs[4:8]
    outs, held = refs[8:12], refs[12]
    for k in range(CHIPS):
        held[16 * k : 16 * k + 16, :] = blocks[k][:, 0:D]
    hidden = dot(held[...], downs[...], 1, 1)
    pre = jnp.concatenate(
        [p[8 * k : 8 * k + 8, :] for k in range(CHIPS) for p in (pre_a, pre_b)], axis=0
    )
    operand = differentials(hidden, pre[:, 0 : 2 * HID], pre[:, 2 * HID :])
    for low in range(0, D, WIDTH):
        cols = pl.ds(low, WIDTH)
        total = dot(operand, wide[cols, :], 1, 1)
        for k in range(CHIPS):
            outs[k][:, cols] = total[16 * k : 16 * k + 16].astype(outs[k].dtype)


def forward_kernel(*refs):
    streams, own_ids, other_ids, routers = (refs[0:4], refs[4:8]), refs[8:10], refs[10], refs[11:13]
    expo_ref, share_ref, stats_ref, held = refs[13:17]
    member = lax.axis_index("expert")
    logits = []
    for blocks in streams:
        stream_rows(blocks, held)
        held[96:128, :] = held[64:96, :]
        rows = held[...]
        logits.append(jnp.concatenate([dot(r[...], rows, 1, 1) for r in routers], axis=0))
    logits = jnp.concatenate(logits, axis=1)
    ids = [
        jnp.concatenate([own_ids[0][...], own_ids[1][...]], axis=0).astype(F32).T,
        other_ids[...].astype(F32).T,
    ]
    row = lax.broadcasted_iota(jnp.int32, (2 * OWN, 128), 0)
    column = lax.broadcasted_iota(jnp.int32, (2 * OWN, 128), 1)
    own = row + OWN * member
    other = row - OWN + OWN * (member + 1 - 2 * lax.rem(member, 2))
    experts = jnp.where(row < OWN, own, other).astype(F32)
    scale = EXPERTS / (TOKENS * TOPK)
    shares = []
    for tick in range(2):
        hits = jnp.zeros((2 * OWN, 128), F32)
        for core in range(2):
            for j in range(TOPK):
                slot = TOPK * tick + j
                hits += (experts == ids[core][slot : slot + 1, :]).astype(F32)
        count_a = jnp.sum(jnp.where(column < 64, hits, 0.0), axis=1, keepdims=True)
        count_b = jnp.sum(jnp.where(column < 64, 0.0, hits), axis=1, keepdims=True)
        shares.append((count_a * scale, count_b * scale))
    share = jnp.concatenate(
        [jnp.where(column < 64, shares[0][i], shares[1][i]) for i in range(2)], axis=1
    )
    peak = jnp.max(logits, axis=0, keepdims=True)
    expo = jnp.exp(logits - peak)
    total = jnp.sum(expo, axis=0, keepdims=True)
    weighted = jnp.sum(expo * share, axis=0, keepdims=True)
    expo_ref[...] = expo
    share_ref[...] = share
    figures = []
    for value, count in ((peak, 3), (total, 2), (weighted, 2)):
        for _ in range(count):
            figures.append(value.astype(BF16).astype(F32))
            value = value - figures[-1]
    rows = [f[:, low : low + 128] for low in (0, 128) for f in figures]
    stats_ref[...] = jnp.concatenate(rows + [jnp.zeros((2, 128), F32)], axis=0).astype(BF16)


def turned(value, k):
    if k == 0:
        return value
    early, late = value[:, 0:64], value[:, 64:96]
    early = pltpu.roll(jnp.concatenate([early, early], axis=1), 16 * k, 1)
    late = pltpu.roll(jnp.concatenate([late] * 4, axis=1), 8 * k, 1)
    return jnp.concatenate([early[:, 0:64], late[:, 0:64]], axis=1)


def router_kernel(*refs):
    streams, expo_ref, share_ref, parts = (refs[0:4], refs[4:8]), refs[8], refs[9], refs[10:14]
    own_out, other_out, held = refs[14:17]
    stats = []
    for k, part in enumerate(parts):
        value = turned(part[:, D:WIDE].astype(F32), k)
        wide = [jnp.concatenate([value[i : i + 1], value[i + 7 : i + 8]], axis=1) for i in range(7)]
        stats.append((wide[0] + wide[1] + wide[2], wide[3] + wide[4], wide[5] + wide[6]))
    mine = stats[0]
    peaks = [s[0] for s in stats]
    peak = functools.reduce(jnp.maximum, peaks)
    factors = [jnp.exp(p - peak) for p in peaks]
    total = sum(s[1] * f for s, f in zip(stats, factors))
    weighted = sum(s[2] * f for s, f in zip(stats, factors))
    log_total = peak + jnp.log(total)
    mean_share = weighted / total
    probs = expo_ref[...] * (jnp.exp(mine[0] - peak) / total)
    slopes = (
        2.0 * z_weight * log_total - balance_weight * mean_share + balance_weight * share_ref[...]
    ) * probs
    column = lax.broadcasted_iota(jnp.int32, (2 * OWN, 128), 1)
    kept = ((column % 16) < 8) & (column < 64) | (column >= 64) & (column < 96)
    for i, blocks in enumerate(streams):
        stream_rows(blocks, held.at[pl.ds(96 * i, 96), :])
    chosen = [
        jnp.where(kept, slopes[:, 128 * i : 128 * i + 128], 0.0).astype(BF16)[:, 0:96] for i in range(2)
    ]
    for low in range(0, D, WIDTH):
        cols = pl.ds(low, WIDTH)
        part = dot(chosen[0], held[0:96, cols], 1, 0) + dot(chosen[1], held[96:192, cols], 1, 0)
        own_out[:, cols] = part[0:OWN]
        other_out[:, cols] = part[OWN:]


def touch_kernel(value, out):
    pass


def passed(value, flops):
    spec = pl.BlockSpec(memory_space=pl.ANY)
    return pl.pallas_call(
        touch_kernel, out_shape=jax.ShapeDtypeStruct(value.shape, value.dtype),
        in_specs=[spec], out_specs=spec, input_output_aliases={0: 0},
        cost_estimate=pl.CostEstimate(flops=flops, bytes_accessed=0, transcendentals=0),
    )(value)


def swapped(value):
    return lax.ppermute(value, "expert", [(e, e ^ 1) for e in range(8)])


def mirrored(value):
    count = lax.axis_size("pipe")
    return lax.ppermute(value, "pipe", [(i, count - 1 - i) for i in range(count)])


def from_chip(value, k):
    return lax.ppermute(value, "expert", [((e + 2 * k) % 8, e) for e in range(8)])


def ring(value):
    return [value] + [from_chip(value, k) for k in range(1, CHIPS)]


def returned(parts):
    return [parts[0]] + [from_chip(parts[CHIPS - k], k) for k in range(1, CHIPS)]


def emitted(grads, parts):
    total = grads.astype(F32)
    for part in parts:
        total = total + part.astype(F32)
    return total.astype(BF16)


def after(value, *earlier):
    return lax.optimization_barrier((value, *earlier))[0]


def shards(
    stash_a, stash_b, ids_a, ids_b, arriving_a, arriving_b, head_a, head_b,
    w_gate, w_up, w_down, router,
):
    stash_a, stash_b, ids_a, ids_b = stash_a[0], stash_b[0], ids_a[0], ids_b[0]
    arriving_a, arriving_b = arriving_a[0], arriving_b[0]
    w_gate, w_up, w_down, router = w_gate[0], w_up[0], w_down[0], router[0]
    section = lax.axis_index("pipe")
    top = lax.axis_size("pipe") - 1
    block_b = mirrored(payload(stash_b, arriving_b, ids_b))
    block_a = payload(stash_a, arriving_a, ids_a)
    blocks_a = ring(block_a)
    other_gate, other_up, other_down = (swapped(weight) for weight in (w_gate, w_up, w_down))
    blocks_b = ring(passed(after(block_b, other_gate, other_up, other_down), int(3e9)))
    weights = [w_gate, other_gate, w_up, other_up, w_down, other_down]
    rows = [pltpu.VMEM((96, D), BF16)]

    terms_a, pre_a, ids_a, wide, downs = call(
        first_a_kernel,
        [((32, D), F32), ((32, 4 * HID), F32), ((64, IDCOLS), BF16)]
        + [((D, 4 * HID), BF16), ((2 * HID, D), BF16)],
        blocks_a + weights, rows, 2 * 96 * D * 128 * 8,
    )
    sends = [((16, D), F32)] + [((16, D), BF16)] * 3
    *terms, pre_b, ids_b = call(
        first_b_kernel, sends + [((32, 4 * HID), F32), ((64, IDCOLS), BF16)],
        blocks_b + [wide, downs, terms_a], rows, 2 * 96 * D * 128 * 8,
    )
    other_router = swapped(after(router, terms[0]))
    other_ids = swapped(jnp.concatenate([ids_a, ids_b], axis=0))
    grads = jnp.concatenate([arriving_a, block_b[1, :, :D]], axis=0)
    out = after(emitted(grads, returned(terms)), other_ids)
    moved = lax.ppermute(out, "pipe", [(i, i - 1) for i in range(1, top + 1)])
    expo, share, stats = call(
        forward_kernel, [((2 * OWN, 256), F32), ((2 * OWN, 256), F32), ((16, IDCOLS), BF16)],
        blocks_a + blocks_b + [ids_a, ids_b, other_ids, router, other_router],
        [pltpu.VMEM((128, D), BF16)], 2 * 256 * D * 64,
    )
    head = jnp.concatenate([head_a[0], head_b[0]], axis=0)
    grads = jnp.where(section == top, head, moved)
    gathered = ring(jnp.concatenate([grads, stats], axis=1))
    terms = call(
        second_tick_kernel, sends, gathered + [pre_a, pre_b, wide, downs], [pltpu.VMEM((64, D), BF16)],
        2 * 64 * D * 128 * 6,
    )
    own, other = call(
        router_kernel, [((OWN, D), F32)] * 2,
        blocks_a + blocks_b + [after(expo, *terms), share] + gathered,
        [pltpu.VMEM((192, D), BF16)], 2 * 192 * D * 64,
    )
    router_grad = own + swapped(other)
    parts = returned(terms)
    out_a = emitted(grads[:ROWS], [part[:ROWS] for part in parts])
    out_b = emitted(grads[ROWS:], [part[ROWS:] for part in parts])
    return out_a[None], after(mirrored(out_b), router_grad)[None], router_grad[None]


def solution(mesh):
    placed = (
        P("pipe", None, "expert", None),
        P("pipe", None, "expert", None),
        P("pipe", None, "expert", None),
        P("pipe", None, "expert", None),
        P("pipe", "expert", None),
        P("pipe", "expert", None),
        P(None, "expert", None),
        P(None, "expert", None),
        P("pipe", None, "expert"),
        P("pipe", None, "expert"),
        P("pipe", "expert", None),
        P("pipe", "expert", None),
    )
    return jax.shard_map(
        shards,
        mesh=mesh,
        in_specs=placed,
        out_specs=(P("pipe", "expert", None), P("pipe", "expert", None), P("pipe", "expert", None)),
        check_vma=False,
    )
```

```python
import functools

import jax
import jax.numpy as jnp
from jax import lax
from jax.experimental import pallas as pl
from jax.experimental.pallas import tpu as pltpu
from jax.sharding import PartitionSpec as P

D = 3584
HID = 128
EXPERTS = 256
OWN = 32
TOKENS = 64
TOPK = 8
ROWS = 8
CHIPS = 4
IDCOLS = 128
WIDE = D + IDCOLS
WIDTH = 512
VMEM_LIMIT = 48 * 1024 * 1024
z_weight = 0.01
balance_weight = 1.0
F32 = jnp.float32
BF16 = jnp.bfloat16


def dot(lhs, rhs, lhs_dim, rhs_dim):
    return lax.dot_general(
        lhs, rhs, (((lhs_dim,), (rhs_dim,)), ((), ())), preferred_element_type=F32
    )


def call(body, outs, args, scratch=(), flops=0):
    spec = pl.BlockSpec(memory_space=pltpu.VMEM)
    total = sum(a.size * a.dtype.itemsize for a in args)
    return pl.pallas_call(
        body,
        out_shape=[jax.ShapeDtypeStruct(shape, dtype) for shape, dtype in outs],
        in_specs=[spec] * len(args),
        out_specs=[spec] * len(outs),
        scratch_shapes=list(scratch),
        compiler_params=pltpu.CompilerParams(vmem_limit_bytes=VMEM_LIMIT),
        cost_estimate=pl.CostEstimate(flops=flops, bytes_accessed=total, transcendentals=0),
    )(*args)


def packed(parts):
    return jnp.concatenate([p.astype(F32) for p in parts], axis=0).astype(BF16)


def pack_kernel(stash, grads, ids, out, held_stash, held_grads, held_ids, sems):
    copies = [
        pltpu.make_async_copy(src, dst, sems.at[i])
        for i, (src, dst) in enumerate(
            ((ids, held_ids), (stash, held_stash), (grads, held_grads))
        )
    ]
    for copy in copies:
        copy.start()
    for copy in copies:
        copy.wait()
    empty = jnp.full((ROWS, IDCOLS - 2 * TOPK), -1.0, F32)
    used = [held_ids[0].astype(F32), held_ids[1].astype(F32), empty]
    for i, rows in enumerate((held_stash[0], held_grads[...], held_stash[1])):
        out[i, :, 0:D] = rows
        out[i, :, D:WIDE] = jnp.full((ROWS, IDCOLS), -1.0, F32).astype(BF16)
    out[0, :, D:WIDE] = jnp.concatenate(used, axis=1).astype(BF16)


def payload(stash, grads, ids):
    hbm = pl.BlockSpec(memory_space=pltpu.HBM)
    return pl.pallas_call(
        pack_kernel,
        out_shape=jax.ShapeDtypeStruct((3, ROWS, WIDE), BF16),
        in_specs=[hbm] * 3,
        out_specs=pl.BlockSpec(memory_space=pltpu.VMEM),
        scratch_shapes=[pltpu.VMEM(a.shape, a.dtype) for a in (stash, grads, ids)]
        + [pltpu.SemaphoreType.DMA((3,))],
    )(stash, grads, ids)


def differentials(hidden, gate, up):
    q = jax.nn.sigmoid(gate)
    d_gate = (hidden * up * q * (1.0 + gate * (1.0 - q))).astype(BF16)
    d_up = (hidden * gate * q).astype(BF16)
    return jnp.concatenate([d_gate, d_up], axis=1)


def stream_rows(blocks, held):
    for k, block in enumerate(blocks):
        held[16 * k : 16 * k + 16, :] = packed([block[0, :, 0:D], block[1, :, 0:D]])
    for k in range(0, CHIPS, 2):
        pair = [blocks[k][2, :, 0:D], blocks[k + 1][2, :, 0:D]]
        held[64 + 8 * k : 80 + 8 * k, :] = packed(pair)


def first_tick(blocks, wide, downs, pre, ids, held):
    stream_rows(blocks, held)
    for k, block in enumerate(blocks):
        ids[16 * k : 16 * k + 16, :] = packed([block[0, :, D:WIDE], block[1, :, D:WIDE]])
    rows = held[...]

    def pick(value, offset):
        return jnp.concatenate(
            [value[16 * k + offset : 16 * k + offset + 8] for k in range(CHIPS)], axis=0
        )

    values = dot(rows, wide[...], 1, 0)
    pre[...] = values[64:96]
    hidden = pick(dot(rows[0:64], downs[...], 1, 1), 8)
    values = pick(values, 0)
    return differentials(hidden, values[:, 0 : 2 * HID], values[:, 2 * HID :])


def first_a_kernel(*refs):
    blocks, weights, (terms, pre, ids, wide, downs, held) = refs[:4], refs[4:10], refs[10:16]
    for i, w in enumerate(weights[0:4]):
        wide[:, HID * i : HID * i + HID] = w[...]
    for i, w in enumerate(weights[4:6]):
        downs[HID * i : HID * i + HID, :] = w[...]
    operand = first_tick(blocks, wide, downs, pre, ids, held)
    for low in range(0, D, WIDTH):
        cols = pl.ds(low, WIDTH)
        terms[:, cols] = dot(operand, wide[cols, :], 1, 1)


def first_b_kernel(*refs):
    blocks, wide, downs, terms_a, outs = refs[:4], refs[4], refs[5], refs[6], refs[7:11]
    pre, ids, held = refs[11:14]
    operand = first_tick(blocks, wide, downs, pre, ids, held)
    for low in range(0, D, WIDTH):
        cols = pl.ds(low, WIDTH)
        terms_b = dot(operand, wide[cols, :], 1, 1)
        for k in range(CHIPS):
            both = [terms_a[8 * k : 8 * k + 8, cols], terms_b[8 * k : 8 * k + 8]]
            outs[k][:, cols] = jnp.concatenate(both, axis=0).astype(outs[k].dtype)


def second_tick_kernel(*refs):
    blocks, pre_a, pre_b, wide, downs = refs[:4], *refs[4:8]
    outs, held = refs[8:12], refs[12]
    for k in range(CHIPS):
        held[16 * k : 16 * k + 16, :] = blocks[k][:, 0:D]
    hidden = dot(held[...], downs[...], 1, 1)
    pre = jnp.concatenate(
        [p[8 * k : 8 * k + 8, :] for k in range(CHIPS) for p in (pre_a, pre_b)], axis=0
    )
    operand = differentials(hidden, pre[:, 0 : 2 * HID], pre[:, 2 * HID :])
    for low in range(0, D, WIDTH):
        cols = pl.ds(low, WIDTH)
        total = dot(operand, wide[cols, :], 1, 1)
        for k in range(CHIPS):
            outs[k][:, cols] = total[16 * k : 16 * k + 16].astype(outs[k].dtype)


def forward_kernel(*refs):
    streams, own_ids, other_ids, routers = (refs[0:4], refs[4:8]), refs[8:10], refs[10], refs[11:13]
    expo_ref, share_ref, stats_ref, held = refs[13:17]
    member = lax.axis_index("expert")
    logits = []
    for blocks in streams:
        stream_rows(blocks, held)
        held[96:128, :] = held[64:96, :]
        rows = held[...]
        logits.append(jnp.concatenate([dot(r[...], rows, 1, 1) for r in routers], axis=0))
    logits = jnp.concatenate(logits, axis=1)
    ids = [
        jnp.concatenate([own_ids[0][...], own_ids[1][...]], axis=0).astype(F32).T,
        other_ids[...].astype(F32).T,
    ]
    row = lax.broadcasted_iota(jnp.int32, (2 * OWN, 128), 0)
    column = lax.broadcasted_iota(jnp.int32, (2 * OWN, 128), 1)
    own = row + OWN * member
    other = row - OWN + OWN * (member + 1 - 2 * lax.rem(member, 2))
    experts = jnp.where(row < OWN, own, other).astype(F32)
    scale = EXPERTS / (TOKENS * TOPK)
    shares = []
    for tick in range(2):
        hits = jnp.zeros((2 * OWN, 128), F32)
        for core in range(2):
            for j in range(TOPK):
                slot = TOPK * tick + j
                hits += (experts == ids[core][slot : slot + 1, :]).astype(F32)
        count_a = jnp.sum(jnp.where(column < 64, hits, 0.0), axis=1, keepdims=True)
        count_b = jnp.sum(jnp.where(column < 64, 0.0, hits), axis=1, keepdims=True)
        shares.append((count_a * scale, count_b * scale))
    share = jnp.concatenate(
        [jnp.where(column < 64, shares[0][i], shares[1][i]) for i in range(2)], axis=1
    )
    peak = jnp.max(logits, axis=0, keepdims=True)
    expo = jnp.exp(logits - peak)
    total = jnp.sum(expo, axis=0, keepdims=True)
    weighted = jnp.sum(expo * share, axis=0, keepdims=True)
    expo_ref[...] = expo
    share_ref[...] = share
    figures = []
    for value, count in ((peak, 3), (total, 2), (weighted, 2)):
        for _ in range(count):
            figures.append(value.astype(BF16).astype(F32))
            value = value - figures[-1]
    rows = [f[:, low : low + 128] for low in (0, 128) for f in figures]
    stats_ref[...] = jnp.concatenate(rows + [jnp.zeros((2, 128), F32)], axis=0).astype(BF16)


def turned(value, k):
    if k == 0:
        return value
    early, late = value[:, 0:64], value[:, 64:96]
    early = pltpu.roll(jnp.concatenate([early, early], axis=1), 16 * k, 1)
    late = pltpu.roll(jnp.concatenate([late] * 4, axis=1), 8 * k, 1)
    return jnp.concatenate([early[:, 0:64], late[:, 0:64]], axis=1)


def router_kernel(*refs):
    streams, expo_ref, share_ref, parts = (refs[0:4], refs[4:8]), refs[8], refs[9], refs[10:14]
    own_out, other_out, held = refs[14:17]
    stats = []
    for k, part in enumerate(parts):
        value = turned(part[:, D:WIDE].astype(F32), k)
        wide = [jnp.concatenate([value[i : i + 1], value[i + 7 : i + 8]], axis=1) for i in range(7)]
        stats.append((wide[0] + wide[1] + wide[2], wide[3] + wide[4], wide[5] + wide[6]))
    mine = stats[0]
    peaks = [s[0] for s in stats]
    peak = functools.reduce(jnp.maximum, peaks)
    factors = [jnp.exp(p - peak) for p in peaks]
    total = sum(s[1] * f for s, f in zip(stats, factors))
    weighted = sum(s[2] * f for s, f in zip(stats, factors))
    log_total = peak + jnp.log(total)
    mean_share = weighted / total
    probs = expo_ref[...] * (jnp.exp(mine[0] - peak) / total)
    slopes = (
        2.0 * z_weight * log_total - balance_weight * mean_share + balance_weight * share_ref[...]
    ) * probs
    column = lax.broadcasted_iota(jnp.int32, (2 * OWN, 128), 1)
    kept = ((column % 16) < 8) & (column < 64) | (column >= 64) & (column < 96)
    for i, blocks in enumerate(streams):
        stream_rows(blocks, held.at[pl.ds(96 * i, 96), :])
    chosen = [
        jnp.where(kept, slopes[:, 128 * i : 128 * i + 128], 0.0).astype(BF16)[:, 0:96] for i in range(2)
    ]
    for low in range(0, D, WIDTH):
        cols = pl.ds(low, WIDTH)
        part = dot(chosen[0], held[0:96, cols], 1, 0) + dot(chosen[1], held[96:192, cols], 1, 0)
        own_out[:, cols] = part[0:OWN]
        other_out[:, cols] = part[OWN:]


def touch_kernel(value, out):
    pass


def passed(value, flops):
    spec = pl.BlockSpec(memory_space=pl.ANY)
    return pl.pallas_call(
        touch_kernel, out_shape=jax.ShapeDtypeStruct(value.shape, value.dtype),
        in_specs=[spec], out_specs=spec, input_output_aliases={0: 0},
        cost_estimate=pl.CostEstimate(flops=flops, bytes_accessed=0, transcendentals=0),
    )(value)


def swapped(value):
    return lax.ppermute(value, "expert", [(e, e ^ 1) for e in range(8)])


def mirrored(value):
    count = lax.axis_size("pipe")
    return lax.ppermute(value, "pipe", [(i, count - 1 - i) for i in range(count)])


def from_chip(value, k):
    return lax.ppermute(value, "expert", [((e + 2 * k) % 8, e) for e in range(8)])


def ring(value):
    return [value] + [from_chip(value, k) for k in range(1, CHIPS)]


def returned(parts):
    return [parts[0]] + [from_chip(parts[CHIPS - k], k) for k in range(1, CHIPS)]


def emitted(grads, parts):
    total = grads.astype(F32)
    for part in parts:
        total = total + part.astype(F32)
    return total.astype(BF16)


def after(value, *earlier):
    return lax.optimization_barrier((value, *earlier))[0]


def shards(
    stash_a, stash_b, ids_a, ids_b, arriving_a, arriving_b, head_a, head_b,
    w_gate, w_up, w_down, router,
):
    stash_a, stash_b, ids_a, ids_b = stash_a[0], stash_b[0], ids_a[0], ids_b[0]
    arriving_a, arriving_b = arriving_a[0], arriving_b[0]
    w_gate, w_up, w_down, router = w_gate[0], w_up[0], w_down[0], router[0]
    section = lax.axis_index("pipe")
    top = lax.axis_size("pipe") - 1
    block_b = mirrored(payload(stash_b, arriving_b, ids_b))
    block_a = payload(stash_a, arriving_a, ids_a)
    blocks_a = ring(block_a)
    other_gate, other_up, other_down = (swapped(weight) for weight in (w_gate, w_up, w_down))
    blocks_b = ring(passed(after(block_b, other_gate, other_up, other_down), int(3e9)))
    weights = [w_gate, other_gate, w_up, other_up, w_down, other_down]
    rows = [pltpu.VMEM((96, D), BF16)]

    terms_a, pre_a, ids_a, wide, downs = call(
        first_a_kernel,
        [((32, D), F32), ((32, 4 * HID), F32), ((64, IDCOLS), BF16)]
        + [((D, 4 * HID), BF16), ((2 * HID, D), BF16)],
        blocks_a + weights, rows, 2 * 96 * D * 128 * 8,
    )
    sends = [((16, D), F32)] + [((16, D), BF16)] * 3
    *terms, pre_b, ids_b = call(
        first_b_kernel, sends + [((32, 4 * HID), F32), ((64, IDCOLS), BF16)],
        blocks_b + [wide, downs, terms_a], rows, 2 * 96 * D * 128 * 8,
    )
    other_router = swapped(after(router, terms[0]))
    other_ids = swapped(jnp.concatenate([ids_a, ids_b], axis=0))
    grads = jnp.concatenate([arriving_a, block_b[1, :, :D]], axis=0)
    out = after(emitted(grads, returned(terms)), other_ids)
    moved = lax.ppermute(out, "pipe", [(i, i - 1) for i in range(1, top + 1)])
    expo, share, stats = call(
        forward_kernel, [((2 * OWN, 256), F32), ((2 * OWN, 256), F32), ((16, IDCOLS), BF16)],
        blocks_a + blocks_b + [ids_a, ids_b, other_ids, router, other_router],
        [pltpu.VMEM((128, D), BF16)], 2 * 256 * D * 64,
    )
    head = jnp.concatenate([head_a[0], head_b[0]], axis=0)
    grads = jnp.where(section == top, head, moved)
    gathered = ring(jnp.concatenate([grads, stats], axis=1))
    terms = call(
        second_tick_kernel, sends, gathered + [pre_a, pre_b, wide, downs], [pltpu.VMEM((64, D), BF16)],
        2 * 64 * D * 128 * 6,
    )
    own, other = call(
        router_kernel, [((OWN, D), F32)] * 2,
        blocks_a + blocks_b + [after(expo, *terms), share] + gathered,
        [pltpu.VMEM((192, D), BF16)], 2 * 192 * D * 64,
    )
    router_grad = own + swapped(other)
    parts = returned(terms)
    out_a = emitted(grads[:ROWS], [part[:ROWS] for part in parts])
    out_b = emitted(grads[ROWS:], [part[ROWS:] for part in parts])
    return out_a[None], after(mirrored(out_b), router_grad)[None], router_grad[None]


def solution(mesh):
    placed = (
        P("pipe", None, "expert", None),
        P("pipe", None, "expert", None),
        P("pipe", None, "expert", None),
        P("pipe", None, "expert", None),
        P("pipe", "expert", None),
        P("pipe", "expert", None),
        P(None, "expert", None),
        P(None, "expert", None),
        P("pipe", None, "expert"),
        P("pipe", None, "expert"),
        P("pipe", "expert", None),
        P("pipe", "expert", None),
    )
    return jax.shard_map(
        shards,
        mesh=mesh,
        in_specs=placed,
        out_specs=(P("pipe", "expert", None), P("pipe", "expert", None), P("pipe", "expert", None)),
        check_vma=False,
    )
```

```python
import functools

import jax
import jax.numpy as jnp
from jax import lax
from jax.experimental import pallas as pl
from jax.experimental.pallas import tpu as pltpu
from jax.sharding import PartitionSpec as P

D = 3584
HID = 128
EXPERTS = 256
OWN = 32
TOKENS = 64
TOPK = 8
ROWS = 8
CHIPS = 4
IDCOLS = 128
WIDE = D + IDCOLS
WIDTH = 512
VMEM_LIMIT = 48 * 1024 * 1024
z_weight = 0.01
balance_weight = 1.0
F32 = jnp.float32
BF16 = jnp.bfloat16


def dot(lhs, rhs, lhs_dim, rhs_dim):
    return lax.dot_general(
        lhs, rhs, (((lhs_dim,), (rhs_dim,)), ((), ())), preferred_element_type=F32
    )


def call(body, outs, args, scratch=(), flops=0):
    spec = pl.BlockSpec(memory_space=pltpu.VMEM)
    total = sum(a.size * a.dtype.itemsize for a in args)
    return pl.pallas_call(
        body,
        out_shape=[jax.ShapeDtypeStruct(shape, dtype) for shape, dtype in outs],
        in_specs=[spec] * len(args),
        out_specs=[spec] * len(outs),
        scratch_shapes=list(scratch),
        compiler_params=pltpu.CompilerParams(vmem_limit_bytes=VMEM_LIMIT),
        cost_estimate=pl.CostEstimate(flops=flops, bytes_accessed=total, transcendentals=0),
    )(*args)


def packed(parts):
    return jnp.concatenate([p.astype(F32) for p in parts], axis=0).astype(BF16)


def pack_kernel(stash, grads, ids, out, held_stash, held_grads, held_ids, sems):
    copies = [
        pltpu.make_async_copy(src, dst, sems.at[i])
        for i, (src, dst) in enumerate(
            ((ids, held_ids), (stash, held_stash), (grads, held_grads))
        )
    ]
    for copy in copies:
        copy.start()
    for copy in copies:
        copy.wait()
    empty = jnp.full((ROWS, IDCOLS - 2 * TOPK), -1.0, F32)
    used = [held_ids[0].astype(F32), held_ids[1].astype(F32), empty]
    for i, rows in enumerate((held_stash[0], held_grads[...], held_stash[1])):
        out[i, :, 0:D] = rows
        out[i, :, D:WIDE] = jnp.full((ROWS, IDCOLS), -1.0, F32).astype(BF16)
    out[0, :, D:WIDE] = jnp.concatenate(used, axis=1).astype(BF16)


def payload(stash, grads, ids):
    hbm = pl.BlockSpec(memory_space=pltpu.HBM)
    return pl.pallas_call(
        pack_kernel,
        out_shape=jax.ShapeDtypeStruct((3, ROWS, WIDE), BF16),
        in_specs=[hbm] * 3,
        out_specs=pl.BlockSpec(memory_space=pltpu.VMEM),
        scratch_shapes=[pltpu.VMEM(a.shape, a.dtype) for a in (stash, grads, ids)]
        + [pltpu.SemaphoreType.DMA((3,))],
    )(stash, grads, ids)


def differentials(hidden, gate, up):
    d_gate, d_up = [], []
    for h, g, u in zip(hidden, gate, up):
        q = jax.nn.sigmoid(g)
        d_gate.append((h * u * q * (1.0 + g * (1.0 - q))).astype(BF16))
        d_up.append((h * g * q).astype(BF16))
    return d_gate, d_up


def terms_of(d_gate, d_up, gates, ups, cols):
    total = dot(d_gate[0], gates[0][cols, :], 1, 1)
    total += dot(d_gate[1], gates[1][cols, :], 1, 1)
    total += dot(d_up[0], ups[0][cols, :], 1, 1)
    total += dot(d_up[1], ups[1][cols, :], 1, 1)
    return total


def stream_rows(blocks, held):
    for k, block in enumerate(blocks):
        held[16 * k : 16 * k + 16, :] = packed([block[0, :, 0:D], block[1, :, 0:D]])
    for k in range(0, CHIPS, 2):
        pair = [blocks[k][2, :, 0:D], blocks[k + 1][2, :, 0:D]]
        held[64 + 8 * k : 80 + 8 * k, :] = packed(pair)


def first_tick(blocks, weights, pre, ids, held):
    gates, ups, downs = weights[0:2], weights[2:4], weights[4:6]
    stream_rows(blocks, held)
    for k, block in enumerate(blocks):
        ids[16 * k : 16 * k + 16, :] = packed([block[0, :, D:WIDE], block[1, :, D:WIDE]])
    rows = held[...]

    def pick(value, offset):
        return jnp.concatenate(
            [value[16 * k + offset : 16 * k + offset + 8] for k in range(CHIPS)], axis=0
        )

    values = [dot(rows, w[...], 1, 0) for w in (*gates, *ups)]
    for i, value in enumerate(values):
        pre[:, HID * i : HID * i + HID] = value[64:96]
    hidden = [pick(dot(rows[0:64], w[...], 1, 1), 8) for w in downs]
    picked = [pick(value, 0) for value in values]
    return (*differentials(hidden, picked[0:2], picked[2:4]), gates, ups)


def first_a_kernel(*refs):
    blocks, weights, (terms, pre, ids, held) = refs[:4], refs[4:10], refs[10:14]
    operands = first_tick(blocks, weights, pre, ids, held)
    for low in range(0, D, WIDTH):
        cols = pl.ds(low, WIDTH)
        terms[:, cols] = terms_of(*operands, cols)


def first_b_kernel(*refs):
    blocks, weights, terms_a, outs, (pre, ids, held) = (
        refs[:4], refs[4:10], refs[10], refs[11:15], refs[15:18]
    )
    operands = first_tick(blocks, weights, pre, ids, held)
    for low in range(0, D, WIDTH):
        cols = pl.ds(low, WIDTH)
        terms_b = terms_of(*operands, cols)
        for k in range(CHIPS):
            both = [terms_a[8 * k : 8 * k + 8, cols], terms_b[8 * k : 8 * k + 8]]
            outs[k][:, cols] = jnp.concatenate(both, axis=0).astype(outs[k].dtype)


def second_tick_kernel(*refs):
    blocks, pre_a, pre_b, weights = refs[:4], refs[4], refs[5], refs[6:12]
    outs, held = refs[12:16], refs[16]
    gates, ups, downs = weights[0:2], weights[2:4], weights[4:6]
    for k in range(CHIPS):
        held[16 * k : 16 * k + 16, :] = blocks[k][:, 0:D]
    rows = held[...]
    hidden = [dot(rows, w[...], 1, 1) for w in downs]
    pre = jnp.concatenate(
        [p[8 * k : 8 * k + 8, :] for k in range(CHIPS) for p in (pre_a, pre_b)], axis=0
    )
    parts = [pre[:, HID * i : HID * i + HID] for i in range(4)]
    operands = (*differentials(hidden, parts[0:2], parts[2:4]), gates, ups)
    for low in range(0, D, WIDTH):
        cols = pl.ds(low, WIDTH)
        total = terms_of(*operands, cols)
        for k in range(CHIPS):
            outs[k][:, cols] = total[16 * k : 16 * k + 16].astype(outs[k].dtype)


def forward_kernel(*refs):
    streams, own_ids, other_ids, routers = (refs[0:4], refs[4:8]), refs[8:10], refs[10], refs[11:13]
    expo_ref, share_ref, stats_ref, held = refs[13:17]
    member = lax.axis_index("expert")
    logits = []
    for blocks in streams:
        stream_rows(blocks, held)
        held[96:128, :] = held[64:96, :]
        rows = held[...]
        logits.append(jnp.concatenate([dot(r[...], rows, 1, 1) for r in routers], axis=0))
    logits = jnp.concatenate(logits, axis=1)
    ids = [
        jnp.concatenate([own_ids[0][...], own_ids[1][...]], axis=0).astype(F32).T,
        other_ids[...].astype(F32).T,
    ]
    row = lax.broadcasted_iota(jnp.int32, (2 * OWN, 128), 0)
    column = lax.broadcasted_iota(jnp.int32, (2 * OWN, 128), 1)
    own = row + OWN * member
    other = row - OWN + OWN * (member + 1 - 2 * lax.rem(member, 2))
    experts = jnp.where(row < OWN, own, other).astype(F32)
    scale = EXPERTS / (TOKENS * TOPK)
    shares = []
    for tick in range(2):
        hits = jnp.zeros((2 * OWN, 128), F32)
        for core in range(2):
            for j in range(TOPK):
                slot = TOPK * tick + j
                hits += (experts == ids[core][slot : slot + 1, :]).astype(F32)
        count_a = jnp.sum(jnp.where(column < 64, hits, 0.0), axis=1, keepdims=True)
        count_b = jnp.sum(jnp.where(column < 64, 0.0, hits), axis=1, keepdims=True)
        shares.append((count_a * scale, count_b * scale))
    share = jnp.concatenate(
        [jnp.where(column < 64, shares[0][i], shares[1][i]) for i in range(2)], axis=1
    )
    peak = jnp.max(logits, axis=0, keepdims=True)
    expo = jnp.exp(logits - peak)
    total = jnp.sum(expo, axis=0, keepdims=True)
    weighted = jnp.sum(expo * share, axis=0, keepdims=True)
    expo_ref[...] = expo
    share_ref[...] = share
    figures = []
    for value, count in ((peak, 3), (total, 2), (weighted, 2)):
        for _ in range(count):
            figures.append(value.astype(BF16).astype(F32))
            value = value - figures[-1]
    rows = [f[:, low : low + 128] for low in (0, 128) for f in figures]
    stats_ref[...] = jnp.concatenate(rows + [jnp.zeros((2, 128), F32)], axis=0).astype(BF16)


def turned(value, k):
    if k == 0:
        return value
    early, late = value[:, 0:64], value[:, 64:96]
    early = pltpu.roll(jnp.concatenate([early, early], axis=1), 16 * k, 1)
    late = pltpu.roll(jnp.concatenate([late] * 4, axis=1), 8 * k, 1)
    return jnp.concatenate([early[:, 0:64], late[:, 0:64]], axis=1)


def router_kernel(*refs):
    streams, expo_ref, share_ref, parts = (refs[0:4], refs[4:8]), refs[8], refs[9], refs[10:14]
    own_out, other_out, held = refs[14:17]
    stats = []
    for k, part in enumerate(parts):
        value = turned(part[:, D:WIDE].astype(F32), k)
        wide = [jnp.concatenate([value[i : i + 1], value[i + 7 : i + 8]], axis=1) for i in range(7)]
        stats.append((wide[0] + wide[1] + wide[2], wide[3] + wide[4], wide[5] + wide[6]))
    mine = stats[0]
    peaks = [s[0] for s in stats]
    peak = functools.reduce(jnp.maximum, peaks)
    factors = [jnp.exp(p - peak) for p in peaks]
    total = sum(s[1] * f for s, f in zip(stats, factors))
    weighted = sum(s[2] * f for s, f in zip(stats, factors))
    log_total = peak + jnp.log(total)
    mean_share = weighted / total
    probs = expo_ref[...] * (jnp.exp(mine[0] - peak) / total)
    slopes = (
        2.0 * z_weight * log_total - balance_weight * mean_share + balance_weight * share_ref[...]
    ) * probs
    column = lax.broadcasted_iota(jnp.int32, (2 * OWN, 128), 1)
    kept = ((column % 16) < 8) & (column < 64) | (column >= 64) & (column < 96)
    for i, blocks in enumerate(streams):
        stream_rows(blocks, held.at[pl.ds(96 * i, 96), :])
    chosen = [
        jnp.where(kept, slopes[:, 128 * i : 128 * i + 128], 0.0).astype(BF16)[:, 0:96] for i in range(2)
    ]
    for low in range(0, D, WIDTH):
        cols = pl.ds(low, WIDTH)
        part = dot(chosen[0], held[0:96, cols], 1, 0) + dot(chosen[1], held[96:192, cols], 1, 0)
        own_out[:, cols] = part[0:OWN]
        other_out[:, cols] = part[OWN:]


def touch_kernel(value, out):
    pass


def passed(value, flops):
    spec = pl.BlockSpec(memory_space=pl.ANY)
    return pl.pallas_call(
        touch_kernel, out_shape=jax.ShapeDtypeStruct(value.shape, value.dtype),
        in_specs=[spec], out_specs=spec, input_output_aliases={0: 0},
        cost_estimate=pl.CostEstimate(flops=flops, bytes_accessed=0, transcendentals=0),
    )(value)


def swapped(value):
    return lax.ppermute(value, "expert", [(e, e ^ 1) for e in range(8)])


def mirrored(value):
    count = lax.axis_size("pipe")
    return lax.ppermute(value, "pipe", [(i, count - 1 - i) for i in range(count)])


def from_chip(value, k):
    return lax.ppermute(value, "expert", [((e + 2 * k) % 8, e) for e in range(8)])


def ring(value):
    return [value] + [from_chip(value, k) for k in range(1, CHIPS)]


def returned(parts):
    return [parts[0]] + [from_chip(parts[CHIPS - k], k) for k in range(CHIPS - 1, 0, -1)]


def emitted(grads, parts):
    total = grads.astype(F32)
    for part in parts:
        total = total + part.astype(F32)
    return total.astype(BF16)


def after(value, *earlier):
    return lax.optimization_barrier((value, *earlier))[0]


def shards(
    stash_a, stash_b, ids_a, ids_b, arriving_a, arriving_b, head_a, head_b,
    w_gate, w_up, w_down, router,
):
    stash_a, stash_b, ids_a, ids_b = stash_a[0], stash_b[0], ids_a[0], ids_b[0]
    arriving_a, arriving_b = arriving_a[0], arriving_b[0]
    w_gate, w_up, w_down, router = w_gate[0], w_up[0], w_down[0], router[0]
    section = lax.axis_index("pipe")
    top = lax.axis_size("pipe") - 1
    block_b = mirrored(payload(stash_b, arriving_b, ids_b))
    block_a = payload(stash_a, arriving_a, ids_a)
    blocks_a = ring(block_a)
    other_gate, other_up, other_down = (swapped(weight) for weight in (w_gate, w_up, w_down))
    blocks_b = ring(passed(after(block_b, other_gate, other_up, other_down), int(3e9)))
    weights = [w_gate, other_gate, w_up, other_up, w_down, other_down]
    rows = [pltpu.VMEM((96, D), BF16)]

    terms_a, pre_a, ids_a = call(
        first_a_kernel, [((32, D), F32), ((32, 4 * HID), F32), ((64, IDCOLS), BF16)],
        blocks_a + weights, rows, 2 * 96 * D * 128 * 8,
    )
    sends = [((16, D), F32)] + [((16, D), BF16)] * 3
    *terms, pre_b, ids_b = call(
        first_b_kernel, sends + [((32, 4 * HID), F32), ((64, IDCOLS), BF16)],
        blocks_b + weights + [terms_a], rows, 2 * 96 * D * 128 * 8,
    )
    other_router = swapped(after(router, terms[0]))
    other_ids = swapped(jnp.concatenate([ids_a, ids_b], axis=0))
    grads = jnp.concatenate([arriving_a, block_b[1, :, :D]], axis=0)
    out = after(emitted(grads, returned(terms)), other_ids)
    moved = lax.ppermute(out, "pipe", [(i, i - 1) for i in range(1, top + 1)])
    expo, share, stats = call(
        forward_kernel, [((2 * OWN, 256), F32), ((2 * OWN, 256), F32), ((16, IDCOLS), BF16)],
        blocks_a + blocks_b + [ids_a, ids_b, other_ids, router, other_router],
        [pltpu.VMEM((128, D), BF16)], 2 * 256 * D * 64,
    )
    head = jnp.concatenate([head_a[0], head_b[0]], axis=0)
    grads = jnp.where(section == top, head, moved)
    gathered = ring(jnp.concatenate([grads, stats], axis=1))
    terms = call(
        second_tick_kernel, sends, gathered + [pre_a, pre_b] + weights, [pltpu.VMEM((64, D), BF16)],
        2 * 64 * D * 128 * 6,
    )
    own, other = call(
        router_kernel, [((OWN, D), F32)] * 2,
        blocks_a + blocks_b + [after(expo, *terms), share] + gathered,
        [pltpu.VMEM((192, D), BF16)], 2 * 192 * D * 64,
    )
    router_grad = own + swapped(other)
    parts = returned(terms)
    out_a = emitted(grads[:ROWS], [part[:ROWS] for part in parts])
    out_b = emitted(grads[ROWS:], [part[ROWS:] for part in parts])
    return out_a[None], after(mirrored(out_b), router_grad)[None], router_grad[None]


def solution(mesh):
    placed = (
        P("pipe", None, "expert", None),
        P("pipe", None, "expert", None),
        P("pipe", None, "expert", None),
        P("pipe", None, "expert", None),
        P("pipe", "expert", None),
        P("pipe", "expert", None),
        P(None, "expert", None),
        P(None, "expert", None),
        P("pipe", None, "expert"),
        P("pipe", None, "expert"),
        P("pipe", "expert", None),
        P("pipe", "expert", None),
    )
    return jax.shard_map(
        shards,
        mesh=mesh,
        in_specs=placed,
        out_specs=(P("pipe", "expert", None), P("pipe", "expert", None), P("pipe", "expert", None)),
        check_vma=False,
    )
```

```python
import functools

import jax
import jax.numpy as jnp
from jax import lax
from jax.experimental import pallas as pl
from jax.experimental.pallas import tpu as pltpu
from jax.sharding import PartitionSpec as P

D = 3584
HID = 128
EXPERTS = 256
OWN = 32
TOKENS = 64
TOPK = 8
ROWS = 8
CHIPS = 4
IDCOLS = 128
WIDE = D + IDCOLS
WIDTH = 512
VMEM_LIMIT = 48 * 1024 * 1024
z_weight = 0.01
balance_weight = 1.0
F32 = jnp.float32
BF16 = jnp.bfloat16


def dot(lhs, rhs, lhs_dim, rhs_dim):
    return lax.dot_general(
        lhs, rhs, (((lhs_dim,), (rhs_dim,)), ((), ())), preferred_element_type=F32
    )


def call(body, outs, args, scratch=(), flops=0):
    spec = pl.BlockSpec(memory_space=pltpu.VMEM)
    total = sum(a.size * a.dtype.itemsize for a in args)
    return pl.pallas_call(
        body,
        out_shape=[jax.ShapeDtypeStruct(shape, dtype) for shape, dtype in outs],
        in_specs=[spec] * len(args),
        out_specs=[spec] * len(outs),
        scratch_shapes=list(scratch),
        compiler_params=pltpu.CompilerParams(vmem_limit_bytes=VMEM_LIMIT),
        cost_estimate=pl.CostEstimate(flops=flops, bytes_accessed=total, transcendentals=0),
    )(*args)


def packed(parts):
    return jnp.concatenate([p.astype(F32) for p in parts], axis=0).astype(BF16)


def pack_kernel(stash, grads, ids, out, held_stash, held_grads, held_ids, sems):
    copies = [
        pltpu.make_async_copy(src, dst, sems.at[i])
        for i, (src, dst) in enumerate(
            ((ids, held_ids), (stash, held_stash), (grads, held_grads))
        )
    ]
    for copy in copies:
        copy.start()
    for copy in copies:
        copy.wait()
    empty = jnp.full((ROWS, IDCOLS - 2 * TOPK), -1.0, F32)
    used = [held_ids[0].astype(F32), held_ids[1].astype(F32), empty]
    for i, rows in enumerate((held_stash[0], held_grads[...], held_stash[1])):
        out[i, :, 0:D] = rows
        out[i, :, D:WIDE] = jnp.full((ROWS, IDCOLS), -1.0, F32).astype(BF16)
    out[0, :, D:WIDE] = jnp.concatenate(used, axis=1).astype(BF16)


def payload(stash, grads, ids):
    hbm = pl.BlockSpec(memory_space=pltpu.HBM)
    return pl.pallas_call(
        pack_kernel,
        out_shape=jax.ShapeDtypeStruct((3, ROWS, WIDE), BF16),
        in_specs=[hbm] * 3,
        out_specs=pl.BlockSpec(memory_space=pltpu.VMEM),
        scratch_shapes=[pltpu.VMEM(a.shape, a.dtype) for a in (stash, grads, ids)]
        + [pltpu.SemaphoreType.DMA((3,))],
    )(stash, grads, ids)


def differentials(hidden, gate, up):
    d_gate, d_up = [], []
    for h, g, u in zip(hidden, gate, up):
        q = jax.nn.sigmoid(g)
        d_gate.append((h * u * q * (1.0 + g * (1.0 - q))).astype(BF16))
        d_up.append((h * g * q).astype(BF16))
    return d_gate, d_up


def terms_of(d_gate, d_up, gates, ups, cols):
    total = dot(d_gate[0], gates[0][cols, :], 1, 1)
    total += dot(d_gate[1], gates[1][cols, :], 1, 1)
    total += dot(d_up[0], ups[0][cols, :], 1, 1)
    total += dot(d_up[1], ups[1][cols, :], 1, 1)
    return total


def stream_rows(blocks, held):
    for k, block in enumerate(blocks):
        held[16 * k : 16 * k + 16, :] = packed([block[0, :, 0:D], block[1, :, 0:D]])
    for k in range(0, CHIPS, 2):
        pair = [blocks[k][2, :, 0:D], blocks[k + 1][2, :, 0:D]]
        held[64 + 8 * k : 80 + 8 * k, :] = packed(pair)


def first_tick(blocks, weights, pre, ids, held):
    gates, ups, downs = weights[0:2], weights[2:4], weights[4:6]
    stream_rows(blocks, held)
    for k, block in enumerate(blocks):
        ids[16 * k : 16 * k + 16, :] = packed([block[0, :, D:WIDE], block[1, :, D:WIDE]])
    rows = held[...]

    def pick(value, offset):
        return jnp.concatenate(
            [value[16 * k + offset : 16 * k + offset + 8] for k in range(CHIPS)], axis=0
        )

    values = [dot(rows, w[...], 1, 0) for w in (*gates, *ups)]
    for i, value in enumerate(values):
        pre[:, HID * i : HID * i + HID] = value[64:96]
    hidden = [pick(dot(rows[0:64], w[...], 1, 1), 8) for w in downs]
    picked = [pick(value, 0) for value in values]
    return (*differentials(hidden, picked[0:2], picked[2:4]), gates, ups)


def first_a_kernel(*refs):
    blocks, weights, (terms, pre, ids, held) = refs[:4], refs[4:10], refs[10:14]
    operands = first_tick(blocks, weights, pre, ids, held)
    for low in range(0, D, WIDTH):
        cols = pl.ds(low, WIDTH)
        terms[:, cols] = terms_of(*operands, cols)


def first_b_kernel(*refs):
    blocks, weights, terms_a, outs, (pre, ids, held) = (
        refs[:4], refs[4:10], refs[10], refs[11:15], refs[15:18]
    )
    operands = first_tick(blocks, weights, pre, ids, held)
    for low in range(0, D, WIDTH):
        cols = pl.ds(low, WIDTH)
        terms_b = terms_of(*operands, cols)
        for k in range(CHIPS):
            both = [terms_a[8 * k : 8 * k + 8, cols], terms_b[8 * k : 8 * k + 8]]
            outs[k][:, cols] = jnp.concatenate(both, axis=0).astype(outs[k].dtype)


def second_tick_kernel(*refs):
    blocks, pre_a, pre_b, weights = refs[:4], refs[4], refs[5], refs[6:12]
    outs, held = refs[12:16], refs[16]
    gates, ups, downs = weights[0:2], weights[2:4], weights[4:6]
    for k in range(CHIPS):
        held[16 * k : 16 * k + 16, :] = blocks[k][:, 0:D]
    rows = held[...]
    hidden = [dot(rows, w[...], 1, 1) for w in downs]
    pre = jnp.concatenate(
        [p[8 * k : 8 * k + 8, :] for k in range(CHIPS) for p in (pre_a, pre_b)], axis=0
    )
    parts = [pre[:, HID * i : HID * i + HID] for i in range(4)]
    operands = (*differentials(hidden, parts[0:2], parts[2:4]), gates, ups)
    for low in range(0, D, WIDTH):
        cols = pl.ds(low, WIDTH)
        total = terms_of(*operands, cols)
        for k in range(CHIPS):
            outs[k][:, cols] = total[16 * k : 16 * k + 16].astype(outs[k].dtype)


def forward_kernel(*refs):
    streams, own_ids, other_ids, routers = (refs[0:4], refs[4:8]), refs[8:10], refs[10], refs[11:13]
    expo_ref, share_ref, stats_ref, held = refs[13:17]
    member = lax.axis_index("expert")
    logits = []
    for blocks in streams:
        stream_rows(blocks, held)
        held[96:128, :] = held[64:96, :]
        rows = held[...]
        logits.append(jnp.concatenate([dot(r[...], rows, 1, 1) for r in routers], axis=0))
    logits = jnp.concatenate(logits, axis=1)
    ids = [
        jnp.concatenate([own_ids[0][...], own_ids[1][...]], axis=0).astype(F32).T,
        other_ids[...].astype(F32).T,
    ]
    row = lax.broadcasted_iota(jnp.int32, (2 * OWN, 128), 0)
    column = lax.broadcasted_iota(jnp.int32, (2 * OWN, 128), 1)
    own = row + OWN * member
    other = row - OWN + OWN * (member + 1 - 2 * lax.rem(member, 2))
    experts = jnp.where(row < OWN, own, other).astype(F32)
    scale = EXPERTS / (TOKENS * TOPK)
    shares = []
    for tick in range(2):
        hits = jnp.zeros((2 * OWN, 128), F32)
        for core in range(2):
            for j in range(TOPK):
                slot = TOPK * tick + j
                hits += (experts == ids[core][slot : slot + 1, :]).astype(F32)
        count_a = jnp.sum(jnp.where(column < 64, hits, 0.0), axis=1, keepdims=True)
        count_b = jnp.sum(jnp.where(column < 64, 0.0, hits), axis=1, keepdims=True)
        shares.append((count_a * scale, count_b * scale))
    share = jnp.concatenate(
        [jnp.where(column < 64, shares[0][i], shares[1][i]) for i in range(2)], axis=1
    )
    peak = jnp.max(logits, axis=0, keepdims=True)
    expo = jnp.exp(logits - peak)
    total = jnp.sum(expo, axis=0, keepdims=True)
    weighted = jnp.sum(expo * share, axis=0, keepdims=True)
    expo_ref[...] = expo
    share_ref[...] = share
    figures = []
    for value, count in ((peak, 3), (total, 2), (weighted, 2)):
        for _ in range(count):
            figures.append(value.astype(BF16).astype(F32))
            value = value - figures[-1]
    rows = [f[:, low : low + 128] for low in (0, 128) for f in figures]
    stats_ref[...] = jnp.concatenate(rows + [jnp.zeros((2, 128), F32)], axis=0).astype(BF16)


def turned(value, k):
    if k == 0:
        return value
    early, late = value[:, 0:64], value[:, 64:96]
    early = pltpu.roll(jnp.concatenate([early, early], axis=1), 16 * k, 1)
    late = pltpu.roll(jnp.concatenate([late] * 4, axis=1), 8 * k, 1)
    return jnp.concatenate([early[:, 0:64], late[:, 0:64]], axis=1)


def router_kernel(*refs):
    streams, expo_ref, share_ref, parts = (refs[0:4], refs[4:8]), refs[8], refs[9], refs[10:14]
    own_out, other_out, held = refs[14:17]
    stats = []
    for k, part in enumerate(parts):
        value = turned(part[:, D:WIDE].astype(F32), k)
        wide = [jnp.concatenate([value[i : i + 1], value[i + 7 : i + 8]], axis=1) for i in range(7)]
        stats.append((wide[0] + wide[1] + wide[2], wide[3] + wide[4], wide[5] + wide[6]))
    mine = stats[0]
    peaks = [s[0] for s in stats]
    peak = functools.reduce(jnp.maximum, peaks)
    factors = [jnp.exp(p - peak) for p in peaks]
    total = sum(s[1] * f for s, f in zip(stats, factors))
    weighted = sum(s[2] * f for s, f in zip(stats, factors))
    log_total = peak + jnp.log(total)
    mean_share = weighted / total
    probs = expo_ref[...] * (jnp.exp(mine[0] - peak) / total)
    slopes = (
        2.0 * z_weight * log_total - balance_weight * mean_share + balance_weight * share_ref[...]
    ) * probs
    column = lax.broadcasted_iota(jnp.int32, (2 * OWN, 128), 1)
    kept = ((column % 16) < 8) & (column < 64) | (column >= 64) & (column < 96)
    for i, blocks in enumerate(streams):
        stream_rows(blocks, held.at[pl.ds(96 * i, 96), :])
    chosen = [
        jnp.where(kept, slopes[:, 128 * i : 128 * i + 128], 0.0).astype(BF16)[:, 0:96] for i in range(2)
    ]
    for low in range(0, D, WIDTH):
        cols = pl.ds(low, WIDTH)
        part = dot(chosen[0], held[0:96, cols], 1, 0) + dot(chosen[1], held[96:192, cols], 1, 0)
        own_out[:, cols] = part[0:OWN]
        other_out[:, cols] = part[OWN:]


def touch_kernel(value, out):
    pass


def passed(value, flops):
    spec = pl.BlockSpec(memory_space=pl.ANY)
    return pl.pallas_call(
        touch_kernel, out_shape=jax.ShapeDtypeStruct(value.shape, value.dtype),
        in_specs=[spec], out_specs=spec, input_output_aliases={0: 0},
        cost_estimate=pl.CostEstimate(flops=flops, bytes_accessed=0, transcendentals=0),
    )(value)


def swapped(value):
    return lax.ppermute(value, "expert", [(e, e ^ 1) for e in range(8)])


def mirrored(value):
    count = lax.axis_size("pipe")
    return lax.ppermute(value, "pipe", [(i, count - 1 - i) for i in range(count)])


def from_chip(value, k):
    return lax.ppermute(value, "expert", [((e + 2 * k) % 8, e) for e in range(8)])


def ring(value):
    return [value] + [from_chip(value, k) for k in range(1, CHIPS)]


def returned(parts):
    return [parts[0]] + [from_chip(parts[CHIPS - k], k) for k in range(1, CHIPS)]


def emitted(grads, parts):
    total = grads.astype(F32)
    for part in parts:
        total = total + part.astype(F32)
    return total.astype(BF16)


def after(value, *earlier):
    return lax.optimization_barrier((value, *earlier))[0]


def shards(
    stash_a, stash_b, ids_a, ids_b, arriving_a, arriving_b, head_a, head_b,
    w_gate, w_up, w_down, router,
):
    stash_a, stash_b, ids_a, ids_b = stash_a[0], stash_b[0], ids_a[0], ids_b[0]
    arriving_a, arriving_b = arriving_a[0], arriving_b[0]
    w_gate, w_up, w_down, router = w_gate[0], w_up[0], w_down[0], router[0]
    section = lax.axis_index("pipe")
    top = lax.axis_size("pipe") - 1
    block_b = mirrored(payload(stash_b, arriving_b, ids_b))
    block_a = payload(stash_a, arriving_a, ids_a)
    blocks_a = ring(block_a)
    other_gate, other_up, other_down = (swapped(weight) for weight in (w_gate, w_up, w_down))
    blocks_b = ring(passed(after(block_b, other_gate, other_up, other_down), int(3e9)))
    weights = [w_gate, other_gate, w_up, other_up, w_down, other_down]
    rows = [pltpu.VMEM((96, D), BF16)]

    terms_a, pre_a, ids_a = call(
        first_a_kernel, [((32, D), F32), ((32, 4 * HID), F32), ((64, IDCOLS), BF16)],
        blocks_a + weights, rows, 2 * 96 * D * 128 * 8,
    )
    sends = [((16, D), F32)] + [((16, D), BF16)] * 3
    *terms, pre_b, ids_b = call(
        first_b_kernel, sends + [((32, 4 * HID), F32), ((64, IDCOLS), BF16)],
        blocks_b + weights + [terms_a], rows, 2 * 96 * D * 128 * 8,
    )
    other_router = swapped(after(router, terms[0]))
    other_ids = swapped(jnp.concatenate([ids_a, ids_b], axis=0))
    grads = jnp.concatenate([arriving_a, block_b[1, :, :D]], axis=0)
    out = emitted(grads, returned(terms))
    moved = lax.ppermute(out, "pipe", [(i, i - 1) for i in range(1, top + 1)])
    expo, share, stats = call(
        forward_kernel, [((2 * OWN, 256), F32), ((2 * OWN, 256), F32), ((16, IDCOLS), BF16)],
        blocks_a + blocks_b + [ids_a, ids_b, other_ids, router, other_router],
        [pltpu.VMEM((128, D), BF16)], 2 * 256 * D * 64,
    )
    head = jnp.concatenate([head_a[0], head_b[0]], axis=0)
    grads = jnp.where(section == top, head, moved)
    gathered = ring(jnp.concatenate([grads, stats], axis=1))
    terms = call(
        second_tick_kernel, sends, gathered + [pre_a, pre_b] + weights, [pltpu.VMEM((64, D), BF16)],
        2 * 64 * D * 128 * 6,
    )
    own, other = call(
        router_kernel, [((OWN, D), F32)] * 2,
        blocks_a + blocks_b + [after(expo, *terms), share] + gathered,
        [pltpu.VMEM((192, D), BF16)], 2 * 192 * D * 64,
    )
    router_grad = own + swapped(other)
    parts = returned(terms)
    out_a = emitted(grads[:ROWS], [part[:ROWS] for part in parts])
    out_b = emitted(grads[ROWS:], [part[ROWS:] for part in parts])
    return out_a[None], after(mirrored(out_b), router_grad)[None], router_grad[None]


def solution(mesh):
    placed = (
        P("pipe", None, "expert", None),
        P("pipe", None, "expert", None),
        P("pipe", None, "expert", None),
        P("pipe", None, "expert", None),
        P("pipe", "expert", None),
        P("pipe", "expert", None),
        P(None, "expert", None),
        P(None, "expert", None),
        P("pipe", None, "expert"),
        P("pipe", None, "expert"),
        P("pipe", "expert", None),
        P("pipe", "expert", None),
    )
    return jax.shard_map(
        shards,
        mesh=mesh,
        in_specs=placed,
        out_specs=(P("pipe", "expert", None), P("pipe", "expert", None), P("pipe", "expert", None)),
        check_vma=False,
    )
```
